32 devices in a mesh: ctx: 8 (over z, x), head: 4 (over y, core).
Axes of the slice: x: 2, y: 2, z: 4, core: 2. Of those that a mesh axis runs over, the one named last changes fastest.
Arguments:
- query: bfloat16 [2048, 6144], P('ctx', 'head'), may hold values from -6 to 6
- key_in: bfloat16 [2048, 6144], P('ctx', 'head'), may hold values from -6 to 6
- value: bfloat16 [2048, 6144], P('ctx', 'head'), may hold values from -6 to 6
- out_weight: bfloat16 [6144, 6144], P('head'), may hold values from -0.078125 to 0.078125
- grad_layer: bfloat16 [2048, 6144], P(('ctx', 'head')), may hold values from -6 to 6
- decay_exp: int32 [48], P('head'), may hold values from 5 to 22
Outputs:
- grad_query: bfloat16 [2048, 6144], P('ctx', 'head')
- grad_key: bfloat16 [2048, 6144], P('ctx', 'head')
- grad_value: bfloat16 [2048, 6144], P('ctx', 'head')
The draws below stay inside these ranges and needn't reach their ends.
All inputs are finite; a program needn't handle non-finite values.
Results may differ from the reference program's by a relative error of at most 0.013.
Values may be sent and summed in bfloat16 or wider, within the bound.
No kernel may reach another device: no remote copies, remote signals or barrier semaphores. Data moves between devices by JAX's collectives and lax.ppermute only.
A program may use at most 64 MiB of HBM per device.

```python
import jax
import jax.numpy as jnp
from jax import lax

HEADS = 48
DH = 128
MODEL = 6144
BLOCK = 256
TOKENS = 2048


def touch_ends(result, own_key, least, largest):
    dims = result.shape
    spot = [jax.random.randint(jax.random.fold_in(own_key, axis), (), 0, dims[axis]) for axis in range(len(dims))]
    result = result.at[tuple(spot)].set(least)
    longest = dims.index(max(dims))
    spot[longest] = (spot[longest] + 1) % dims[longest]
    return result.at[tuple(spot)].set(largest)


def block_levels(rng, extent, shards, smallest, top_value):
    def one(position, shards_of):
        draws = jax.random.uniform(jax.random.fold_in(jax.random.fold_in(rng, 6), position), (shards_of,), jnp.float32, smallest / len(shards), top_value / len(shards))
        return jnp.repeat(jnp.exp(draws), extent[position] // shards_of).reshape((-1,) + (1,) * (len(extent) - position - 1))

    level = one(*shards[0])
    for cut in shards[1:]:
        level = level * one(*cut)
    return level


def scatter_about(key, dims, deviation, most, cuts=(), dtype=jnp.bfloat16):
    result = deviation * jax.random.normal(key, dims, jnp.float32)
    if cuts:
        result = result * block_levels(key, dims, cuts, -0.22, 0.18)
    return jnp.clip(result, -most, most).astype(dtype)


def setup_inputs(seed: int = 0) -> dict:
    arg_keys = jax.random.split(jax.random.key(seed), 7)
    return {
        "query": scatter_about(arg_keys[0], (TOKENS, HEADS * DH), 1.0, 6.0, ((0, 8), (1, 4))),
        "key_in": scatter_about(arg_keys[1], (TOKENS, HEADS * DH), 1.0, 6.0, ((0, 8), (1, 4))),
        "value": scatter_about(arg_keys[2], (TOKENS, HEADS * DH), 1.0, 6.0, ((0, 8), (1, 4))),
        "out_weight": scatter_about(arg_keys[3], (HEADS * DH, MODEL), (HEADS * DH) ** -0.5, 0.078125, ((0, 4),)),
        "grad_layer": scatter_about(arg_keys[4], (TOKENS, MODEL), 1.0, 6.0, ((0, 32),)),
        "decay_exp": touch_ends(jax.random.randint(arg_keys[5], (HEADS,), 5, 23), jax.random.fold_in(arg_keys[5], 1), 5, 22).astype(jnp.int32),
    }


EPSILON = 1e-06

def head_grads(packed):
    queries, keys_in, values_in, cotangent, log_rate = packed
    token_count = queries.shape[0]
    block_count = token_count // BLOCK
    highest = lax.Precision.HIGHEST
    offsets = jnp.arange(BLOCK).astype(jnp.float32)
    spread = offsets[:, None] - offsets[None, :]
    decay_mask = jnp.where(spread >= 0, jnp.exp(jnp.maximum(spread, 0.0) * log_rate), 0.0)
    query_decay = jnp.exp((offsets + 1.0) * log_rate)
    key_decay = jnp.exp((BLOCK - 1.0 - offsets) * log_rate)
    block_decay = jnp.exp(BLOCK * log_rate)

    def blocked(field):
        return field.reshape(block_count, BLOCK, DH)

    def forward_step(state, pieces):
        query_block, key_block, value_block = pieces
        scores = jnp.dot(query_block, key_block.T, preferred_element_type=jnp.float32)
        weights = (scores * decay_mask).astype(jnp.bfloat16)
        output = jnp.dot(weights, value_block, preferred_element_type=jnp.float32)
        output = output + jnp.dot(query_block.astype(jnp.float32) * query_decay[:, None], state, precision=highest)
        update = jnp.dot((key_block.astype(jnp.float32) * key_decay[:, None]).T, value_block.astype(jnp.float32), precision=highest)
        return (block_decay * state + update, (output, state))
    start = jnp.zeros((DH, DH), jnp.float32)
    _, (attended, states) = lax.scan(forward_step, start, (blocked(queries), blocked(keys_in), blocked(values_in)))
    square_mean = lax.optimization_barrier(jnp.mean(attended * attended, axis=-1, keepdims=True)) + EPSILON
    inverse = lax.rsqrt(square_mean)
    normed = attended * inverse
    cot_float = blocked(cotangent).astype(jnp.float32)
    dout = ((cot_float - normed * lax.optimization_barrier(jnp.mean(cot_float * normed, axis=-1, keepdims=True))) * inverse).astype(jnp.bfloat16)

    def backward_step(back, pieces):
        query_block, key_block, value_block, dout_block, state = pieces
        dout_float = dout_block.astype(jnp.float32)
        scores = jnp.dot(query_block, key_block.T, preferred_element_type=jnp.float32)
        weights = (scores * decay_mask).astype(jnp.bfloat16)
        dscores = jnp.dot(dout_block, value_block.T, preferred_element_type=jnp.float32)
        dweights = (dscores * decay_mask).astype(jnp.bfloat16)
        grad_q = jnp.dot(dweights, key_block, preferred_element_type=jnp.float32)
        grad_q = grad_q + jnp.dot(dout_float * query_decay[:, None], state.T, precision=highest)
        grad_k = jnp.dot(dweights.T, query_block, preferred_element_type=jnp.float32)
        grad_k = grad_k + jnp.dot(value_block.astype(jnp.float32) * key_decay[:, None], back.T, precision=highest)
        grad_v = jnp.dot(weights.T, dout_block, preferred_element_type=jnp.float32)
        grad_v = grad_v + jnp.dot(key_block.astype(jnp.float32) * key_decay[:, None], back, precision=highest)
        update = jnp.dot((query_block.astype(jnp.float32) * query_decay[:, None]).T, dout_float, precision=highest)
        return (block_decay * back + update, (grad_q.astype(jnp.bfloat16), grad_k.astype(jnp.bfloat16), grad_v.astype(jnp.bfloat16)))
    _, (grad_q, grad_k, grad_v) = lax.scan(backward_step, start, (blocked(queries), blocked(keys_in), blocked(values_in), dout, states), reverse=True)
    return (grad_q.reshape(token_count, DH), grad_k.reshape(token_count, DH), grad_v.reshape(token_count, DH))

def reference(query, key_in, value, out_weight, grad_layer, decay_exp):
    token_count = query.shape[0]
    log_rate = jnp.log1p(-jnp.exp2(-decay_exp.astype(jnp.float32)))
    dnormed = jnp.dot(grad_layer, out_weight.T, preferred_element_type=jnp.float32).astype(jnp.bfloat16)

    def heads_first(field):
        return jnp.transpose(field.reshape(token_count, HEADS, DH), (1, 0, 2))

    def rows_first(field):
        return jnp.transpose(field, (1, 0, 2)).reshape(token_count, HEADS * DH)
    grads = lax.map(head_grads, (heads_first(query), heads_first(key_in), heads_first(value), heads_first(dnormed), log_rate))
    return (rows_first(grads[0]), rows_first(grads[1]), rows_first(grads[2]))
```

```python
import functools

import jax
import jax.numpy as jnp
from jax import lax
from jax.experimental import pallas as pl
from jax.experimental.pallas import tpu as pltpu
from jax.sharding import PartitionSpec as P

EPSILON = 1e-06
GROUP = 4
BF16 = jnp.bfloat16
F32 = jnp.float32
VMEM = pltpu.VMEM
SMEM = pltpu.SMEM


def call(kernel, outs, grid=(), in_specs=None, out_specs=None, scratch=(), flops=0, moved=0, limit=32, prefetch=0):
    return pl.pallas_call(
        kernel,
        out_shape=outs,
        grid_spec=pltpu.PrefetchScalarGridSpec(
            num_scalar_prefetch=prefetch,
            grid=grid,
            in_specs=in_specs,
            out_specs=out_specs,
            scratch_shapes=list(scratch),
        ),
        compiler_params=pltpu.CompilerParams(vmem_limit_bytes=limit * 2**20),
        cost_estimate=pl.CostEstimate(flops=flops, bytes_accessed=moved, transcendentals=0),
    )


def dot(a, b, dims):
    return lax.dot_general(a, b, (dims, ((), ())), preferred_element_type=F32)


NN = ((1,), (0,))
NT = ((1,), (1,))
TN = ((0,), (0,))


def row_decay(rate, rows, width, from_end):
    place = lax.broadcasted_iota(jnp.int32, (rows, width), 0)
    count = (rows - 1 - place) if from_end else (place + 1)
    return jnp.exp(count.astype(F32) * rate)


def block_decay_mask(rate, rows):
    gap = lax.broadcasted_iota(jnp.int32, (rows, rows), 0) - lax.broadcasted_iota(jnp.int32, (rows, rows), 1)
    return jnp.where(gap >= 0, jnp.exp(jnp.maximum(gap, 0).astype(F32) * rate), 0.0)


def local_state_kernel(heads, quarter, member_ref, rate_ref, k_ref, v_ref, *rest):
    outs, held = rest[:GROUP], rest[GROUP]
    rows, width = k_ref.shape[0], k_ref.shape[1] // heads
    for h in range(heads):
        cols = slice(h * width, (h + 1) * width)
        decay = row_decay(rate_ref[h], rows, width, True)
        k = (k_ref[:, cols].astype(F32) * decay).astype(BF16)
        held[h * width : (h + 1) * width, :] = dot(k, v_ref[:, cols], TN).astype(BF16)
    deal(member_ref[0], quarter, held, outs)


def deal(member, quarter, held, outs):
    for slot in range(GROUP):
        start = pl.multiple_of((member ^ slot) * quarter, 16)
        outs[slot][...] = held[pl.ds(start, quarter), :]


def collect(member, quarter, pieces, held):
    for slot in range(GROUP):
        start = pl.multiple_of((member ^ slot) * quarter, 16)
        held[pl.ds(start, quarter), :] = pieces[slot][...]


def within_kernel(per_step, rate_ref, q_ref, k_ref, v_ref, out_ref):
    rows, width = q_ref.shape[0], q_ref.shape[1] // per_step
    for g in range(per_step):
        cols = slice(g * width, (g + 1) * width)
        mask = block_decay_mask(rate_ref[pl.program_id(0) * per_step + g], rows)
        weights = (dot(q_ref[:, cols], k_ref[:, cols], NT) * mask).astype(BF16)
        out_ref[:, cols] = dot(weights, v_ref[:, cols], NN)


def project_kernel(slots, first, last, place_ref, *refs):
    pieces, refs = refs[:slots], refs[slots:]
    weight_ref = refs[0]
    whole = jnp.concatenate([r[...] for r in pieces], axis=0)
    total = dot(whole, weight_ref[...], NT)
    if not first:
        total = total + refs[1][...]
    out_ref = refs[-1]
    if not last:
        out_ref[...] = total
        return
    rows = pieces[0].shape[0]
    for slot in range(slots):
        start = pl.multiple_of(place_ref[slot] * rows, rows)
        out_ref[pl.ds(start, rows), :] = total[slot * rows : (slot + 1) * rows, :].astype(BF16)


def turn_kernel(heads, quarter, member_ref, rate_ref, q_ref, within_ref, cot_ref, *rest):
    pieces, dout_ref, state_ref = rest[:GROUP], rest[GROUP], rest[GROUP + 1]
    outs, held = rest[GROUP + 2 : 2 * GROUP + 2], rest[2 * GROUP + 2]
    rows, width = q_ref.shape[0], q_ref.shape[1] // heads
    collect(member_ref[0], quarter, pieces, state_ref)
    for h in range(heads):
        cols = slice(h * width, (h + 1) * width)
        band = slice(h * width, (h + 1) * width)
        q = (q_ref[:, cols].astype(F32) * row_decay(rate_ref[h], rows, width, False)).astype(BF16)
        attended = within_ref[:, cols] + dot(q, state_ref[band, :], NN)
        inverse = lax.rsqrt(jnp.mean(attended * attended, axis=-1, keepdims=True) + EPSILON)
        normed = attended * inverse
        cot = cot_ref[:, cols].astype(F32)
        dout = ((cot - normed * jnp.mean(cot * normed, axis=-1, keepdims=True)) * inverse).astype(BF16)
        dout_ref[:, cols] = dout
        held[band, :] = dot(q, dout, TN).astype(BF16)
    deal(member_ref[0], quarter, held, outs)


def grads_kernel(per_step, rate_ref, q_ref, k_ref, v_ref, dout_ref, state_ref, gq_ref, gk_ref, gv_ref):
    rows, width = q_ref.shape[0], q_ref.shape[1] // per_step
    for g in range(per_step):
        cols = slice(g * width, (g + 1) * width)
        rate = rate_ref[pl.program_id(0) * per_step + g]
        mask = block_decay_mask(rate, rows)
        q, k, v, dout = q_ref[:, cols], k_ref[:, cols], v_ref[:, cols], dout_ref[:, cols]
        weights = (dot(q, k, NT) * mask).astype(BF16)
        dweights = (dot(dout, v, NT) * mask).astype(BF16)
        late = (dout.astype(F32) * row_decay(rate, rows, width, False)).astype(BF16)
        gq = dot(dweights, k, NN) + dot(late, state_ref[cols, :], NT)
        gq_ref[:, cols] = gq.astype(BF16)
        gk_ref[:, cols] = dot(dweights, q, TN)
        gv_ref[:, cols] = dot(weights, dout, TN)


def finish_kernel(heads, quarter, member_ref, rate_ref, k_ref, v_ref, gk_in, gv_in, *rest):
    pieces, gk_ref, gv_ref, held = rest[:GROUP], rest[GROUP], rest[GROUP + 1], rest[GROUP + 2]
    rows, width = k_ref.shape[0], k_ref.shape[1] // heads
    collect(member_ref[0], quarter, pieces, held)
    for h in range(heads):
        cols = slice(h * width, (h + 1) * width)
        decay = row_decay(rate_ref[h], rows, width, True)
        back = held[cols, :]
        k = (k_ref[:, cols].astype(F32) * decay).astype(BF16)
        v = (v_ref[:, cols].astype(F32) * decay).astype(BF16)
        gk_ref[:, cols] = (gk_in[:, cols] + dot(v, back, NT)).astype(BF16)
        gv_ref[:, cols] = (gv_in[:, cols] + dot(k, back, NN)).astype(BF16)


def scan(pieces, decay, axis, count, reverse):
    index = lax.axis_index(axis)
    member = index % GROUP

    def swap(x, bits):
        return lax.ppermute(x, axis, [(i, i ^ bits) for i in range(count)])

    got = jnp.stack([pieces[0]] + [swap(pieces[s], s) for s in range(1, GROUP)])
    order = list(range(GROUP))
    if reverse:
        order.reverse()
    before = {}
    total = None
    for m in order:
        state = lax.dynamic_index_in_dim(got, member ^ m, 0, False).astype(F32)
        before[m] = total
        total = state if total is None else total * decay + state
    group_decay = decay ** GROUP
    groups = count // GROUP
    group = index // GROUP
    if groups > 1:
        span = 1
        carry = None
        summed = total
        spread = group_decay
        sent = summed.astype(BF16)
        def shift(x, by):
            step = -by if reverse else by
            pairs = [(i, (i + step * GROUP) % count) for i in range(count)]
            moved = lax.ppermute(x, axis, pairs)
            if reverse:
                here = group + by < groups
            else:
                here = group >= by
            return jnp.where(here, moved.astype(F32), 0.0)

        carry = shift(sent, 1)
        while span < groups - 1:
            carry = carry + spread * shift(carry.astype(BF16), span)
            spread = spread * spread
            span *= 2
    else:
        carry = jnp.zeros_like(total)
    done = []
    reach = carry
    for m in order:
        done.append(reach if before[m] is None else before[m] + reach)
        reach = reach * decay
    done = jnp.stack([done[order.index(m)].astype(BF16) for m in range(GROUP)])
    back = [lax.dynamic_index_in_dim(done, member ^ s, 0, False) for s in range(GROUP)]
    return [back[0]] + [swap(back[s], s) for s in range(1, GROUP)]


def gather_slots(grad_layer, axis, count, parts):
    index = lax.axis_index(axis)
    core, line = index % 2, index // 2
    lines = count // 2
    rows, width = grad_layer.shape
    places = []
    for s in range(lines):
        for c in range(2):
            places.append(((line + s) % lines) * 2 + (core ^ c))
    flip = [(i, i ^ 1) for i in range(count)]
    cuts = [sum(parts[:n]) for n in range(len(parts))]
    own = lax.ppermute(grad_layer, axis, flip)
    columns = []
    for start, size in zip(cuts, parts):
        piece = grad_layer[:, start : start + size]
        slots = []
        for s in range(1, lines):
            pairs = [(i, (i - 2 * s) % count) for i in range(count)]
            moved = lax.ppermute(piece, axis, pairs)
            slots += [moved, lax.ppermute(moved, axis, flip)]
        columns.append(slots)
    return grad_layer, own, columns, cuts, jnp.stack(places).astype(jnp.int32)


def project(grad_layer, out_weight, axis, count, parts):
    own, other, columns, cuts, places = gather_slots(grad_layer, axis, count, parts)
    rows = grad_layer.shape[0]
    wide = out_weight.shape[0]
    tile = 256 if wide % 256 == 0 else 128
    total = None
    for n, (start, size) in enumerate(zip(cuts, parts)):
        first, last = n == 0, n == len(parts) - 1
        at = start // size
        fixed = pl.BlockSpec((rows, size), lambda i, p, at=at: (0, at))
        moved = pl.BlockSpec((rows, size), lambda i, p: (0, 0))
        specs = [fixed, fixed] + [moved] * (count - 2)
        specs += [pl.BlockSpec((tile, size), lambda i, p, at=at: (i, at))]
        block = pl.BlockSpec((rows * count, tile), lambda i, p: (0, i))
        operands = [own, other] + columns[n] + [out_weight]
        if not first:
            specs.append(block)
            operands.append(total)
        total = call(
            functools.partial(project_kernel, count, first, last),
            jax.ShapeDtypeStruct((rows * count, wide), BF16 if last else F32),
            grid=(wide // tile,),
            in_specs=specs,
            out_specs=block,
            flops=2 * rows * count * size * wide,
            moved=2 * size * wide,
            limit=40,
            prefetch=1,
        )(places, *operands)
    return total


def body(ctx_count, head_count, query, key_in, value, out_weight, grad_layer, decay_exp):
    rows, flat = query.shape
    heads = decay_exp.shape[0]
    width = flat // heads
    quarter = flat // GROUP
    per_step = 3 if heads % 3 == 0 else 1
    rate = jnp.log1p(-jnp.exp2(-decay_exp.astype(F32)))
    index = lax.axis_index("ctx")
    member = (index % GROUP).reshape(1).astype(jnp.int32)
    row_rate = jnp.broadcast_to(jnp.repeat(rate, width)[:, None], (flat, width))
    owned_rate = lax.dynamic_slice_in_dim(row_rate, member[0] * quarter, quarter, 0)
    owned_decay = jnp.exp(rows * owned_rate)

    scalar = pl.BlockSpec(memory_space=SMEM)
    plain = pl.BlockSpec(memory_space=VMEM)
    piece = jax.ShapeDtypeStruct((quarter, width), BF16)
    held = pltpu.VMEM((flat, width), BF16)
    unit = 2 * rows * width * width * heads
    size = rows * flat * 2

    pieces = call(
        functools.partial(local_state_kernel, heads, quarter),
        [piece] * GROUP,
        in_specs=[scalar, scalar, plain, plain],
        out_specs=[plain] * GROUP,
        scratch=[held],
        flops=unit,
        moved=3 * size,
    )(member, rate, key_in, value)

    parts = [4096, 2048] if grad_layer.shape[1] == 6144 else [grad_layer.shape[1]]
    cotangent = project(grad_layer, out_weight, "head", head_count, parts)

    state = scan(pieces, owned_decay, "ctx", ctx_count, False)

    steps = heads // per_step
    block = pl.BlockSpec((rows, per_step * width), lambda i: (0, i))
    within = call(
        functools.partial(within_kernel, per_step),
        jax.ShapeDtypeStruct((rows, flat), F32),
        grid=(steps,),
        in_specs=[scalar, block, block, block],
        out_specs=block,
        flops=4 * unit,
        moved=5 * size,
    )(rate, query, key_in, value)

    turned = call(
        functools.partial(turn_kernel, heads, quarter),
        [jax.ShapeDtypeStruct((rows, flat), BF16), jax.ShapeDtypeStruct((flat, width), BF16)] + [piece] * GROUP,
        in_specs=[scalar, scalar, plain, plain, plain] + [plain] * GROUP,
        out_specs=[plain] * (2 + GROUP),
        scratch=[held],
        flops=2 * unit,
        moved=6 * size,
    )(member, rate, query, within, cotangent, *state)
    dout, whole_state, pieces = turned[0], turned[1], turned[2:]

    back = scan(pieces, owned_decay, "ctx", ctx_count, True)

    state_block = pl.BlockSpec((per_step * width, width), lambda i: (i, 0))
    grad_query, key_part, value_part = call(
        functools.partial(grads_kernel, per_step),
        [
            jax.ShapeDtypeStruct((rows, flat), BF16),
            jax.ShapeDtypeStruct((rows, flat), F32),
            jax.ShapeDtypeStruct((rows, flat), F32),
        ],
        grid=(steps,),
        in_specs=[scalar, block, block, block, block, state_block],
        out_specs=[block, block, block],
        flops=11 * unit,
        moved=10 * size,
    )(rate, query, key_in, value, dout, whole_state)

    grad_key, grad_value = call(
        functools.partial(finish_kernel, heads, quarter),
        [jax.ShapeDtypeStruct((rows, flat), BF16)] * 2,
        in_specs=[scalar, scalar, plain, plain, plain, plain] + [plain] * GROUP,
        out_specs=[plain, plain],
        scratch=[held],
        flops=2 * unit,
        moved=8 * size,
    )(member, rate, key_in, value, key_part, value_part, *back)
    return grad_query, grad_key, grad_value


def solution(mesh):
    return jax.shard_map(
        functools.partial(body, mesh.shape["ctx"], mesh.shape["head"]),
        mesh=mesh,
        in_specs=(
            P("ctx", "head"),
            P("ctx", "head"),
            P("ctx", "head"),
            P("head", None),
            P(("ctx", "head"), None),
            P("head"),
        ),
        out_specs=(P("ctx", "head"), P("ctx", "head"), P("ctx", "head")),
        check_vma=False,
    )
```

```python
import functools

import jax
import jax.numpy as jnp
from jax import lax
from jax.experimental import pallas as pl
from jax.experimental.pallas import tpu as pltpu
from jax.sharding import PartitionSpec as P

EPSILON = 1e-06
GROUP = 4
LOADS = 3
BF16 = jnp.bfloat16
F32 = jnp.float32

PLAIN = pl.BlockSpec(memory_space=pltpu.VMEM)
STREAM = pl.BlockSpec(memory_space=pltpu.HBM)


def call(kernel, outs, in_specs, scratch=(), limit=8):
    made = pl.pallas_call(
        kernel,
        out_shape=outs,
        in_specs=in_specs,
        out_specs=[PLAIN] * len(outs),
        scratch_shapes=list(scratch),
        compiler_params=pltpu.CompilerParams(vmem_limit_bytes=limit * 2**20),
        cost_estimate=pl.CostEstimate(flops=1, bytes_accessed=1, transcendentals=0),
    )

    def run(*operands):
        held = [
            pltpu.with_memory_space_constraint(x, pltpu.HBM) if spec is STREAM else x
            for x, spec in zip(operands, in_specs)
        ]
        return made(*held)

    return run


def dot(a, b, dims):
    return lax.dot_general(a, b, (dims, ((), ())), preferred_element_type=F32)


NN = ((1,), (0,))
NT = ((1,), (1,))
TN = ((0,), (0,))


def steps_from(rows, width, axis, start, turn):
    place = lax.broadcasted_iota(jnp.int32, (rows, width), axis)
    return (start + turn * place).astype(F32)


def query_decay(rate, rows, width):
    return jnp.exp(steps_from(rows, width, 0, 1, 1) * rate)


def key_decay(rate, rows, width):
    return jnp.exp(steps_from(rows, width, 0, rows - 1, -1) * rate)


def since_decay(rate, rows):
    return jnp.exp(steps_from(8, rows, 1, -1, -1) * rate)[0:1]


def head_rate(rates_ref, head):
    return rates_ref[8 * head : 8 * head + 1, 0:1]


def group_member():
    return lax.axis_index("ctx") % GROUP


def decayed_pairs(left, right, upto, since, half):
    keep = steps_from(half, half, 0, 0, 1) >= steps_from(half, half, 1, 0, 1)

    def tile(rows, columns):
        pair = dot(left[rows], right[columns], NT)
        return pair * upto[rows, :half] * since[:, columns]

    low, high = slice(0, half), slice(half, 2 * half)
    top = jnp.where(keep, tile(low, low), 0.0).astype(BF16)
    side = tile(high, low).astype(BF16)
    end = jnp.where(keep, tile(high, high), 0.0).astype(BF16)
    return top, jnp.concatenate([side, end], axis=1)


def mix(pairs, values, half):
    top, bottom = pairs
    return jnp.concatenate([dot(top, values[:half], NN), dot(bottom, values, NN)], axis=0)


def mix_back(pairs, values, half):
    top, bottom = pairs
    low = dot(top, values[:half], TN)
    both = dot(bottom, values[half:], TN)
    return jnp.concatenate([low + both[:half], both[half:]], axis=0)


def deal(quarter, held, outs):
    for slot in range(GROUP):
        start = pl.multiple_of((group_member() ^ slot) * quarter, 16)
        outs[slot][...] = held[pl.ds(start, quarter), :]


def collect(quarter, pieces, held):
    for slot in range(GROUP):
        start = pl.multiple_of((group_member() ^ slot) * quarter, 16)
        held[pl.ds(start, quarter), :] = pieces[slot][...]


def local_state_kernel(heads, quarter, cuts, exponent_hbm, q_hbm, k_hbm, v_hbm, grad_hbm, *rest):
    outs, rest = rest[:GROUP], rest[GROUP:]
    parts, rest = rest[: len(cuts)], rest[len(cuts) :]
    rates_ref, q_ref, k_ref, v_ref, late_ref, held, exponent_ref, sems, later = rest
    rows = k_ref.shape[0]
    width = k_ref.shape[1] // heads
    exponents = pltpu.make_async_copy(exponent_hbm, exponent_ref, later.at[len(cuts) + 1])
    exponents.start()
    loads = []
    chunks = sems.shape[1]
    for chunk in range(chunks):
        cols = slice(chunk * heads // chunks * width, (chunk + 1) * heads // chunks * width)
        loads.append(
            [
                pltpu.make_async_copy(source.at[:, cols], target.at[:, cols], sems.at[n, chunk])
                for n, (source, target) in enumerate(((k_hbm, k_ref), (v_hbm, v_ref)))
            ]
        )
        for load in loads[-1]:
            load.start()
    moves = [pltpu.make_async_copy(q_hbm, q_ref, later.at[len(cuts)])]
    for n, (start, size) in enumerate(cuts):
        moves.append(pltpu.make_async_copy(grad_hbm.at[:, start : start + size], parts[n], later.at[n]))
    for move in moves:
        move.start()
    exponents.wait()
    for h in range(heads):
        spread = jnp.full((8, 128), exponent_ref[h].astype(F32))
        rates_ref[8 * h : 8 * h + 8, :] = jnp.log1p(-jnp.exp2(-spread))
    for h in range(heads):
        if h % (heads // chunks) == 0:
            for load in loads[h * chunks // heads]:
                load.wait()
        cols = slice(h * width, (h + 1) * width)
        k = (k_ref[:, cols].astype(F32) * key_decay(head_rate(rates_ref, h), rows, width)).astype(BF16)
        late_ref[:, cols] = k
        held[cols, :] = dot(k, v_ref[:, cols], TN).astype(BF16)
    deal(quarter, held, outs)
    for move in moves:
        move.wait()


def owned_parts(quarter, member, width):
    start = member * quarter
    while start < (member + 1) * quarter:
        head = start // width
        end = min((head + 1) * width, (member + 1) * quarter)
        yield slice(start - member * quarter, end - member * quarter), head
        start = end


def total_kernel(order, rows, rates_ref, *rest):
    pieces, out_ref = rest[:GROUP], rest[GROUP]
    quarter, width = out_ref.shape
    for me in range(GROUP):

        @pl.when(group_member() == me)
        def _():
            for part, head in owned_parts(quarter, me, width):
                decay = jnp.exp(rows * head_rate(rates_ref, head))
                total = None
                for m in order:
                    state = pieces[m ^ me][part, :].astype(F32)
                    total = state if total is None else total * decay + state
                out_ref[part, :] = total.astype(BF16)


def spread_kernel(order, rows, groups, reverse, rates_ref, carry_ref, *rest):
    pieces, outs = rest[:GROUP], rest[GROUP:]
    quarter, width = outs[0].shape
    group = lax.axis_index("ctx") // GROUP
    first = group == (groups - 1 if reverse else 0)
    for me in range(GROUP):

        @pl.when(group_member() == me)
        def _():
            for part, head in owned_parts(quarter, me, width):
                decay = jnp.exp(rows * head_rate(rates_ref, head))
                state = jnp.where(first, 0.0, carry_ref[part, :].astype(F32))
                for n, m in enumerate(order):
                    outs[m ^ me][part, :] = state.astype(BF16)
                    if n + 1 < GROUP:
                        state = state * decay + pieces[m ^ me][part, :].astype(F32)


def weight_loads(start, weight_hbm, weight_ref, sems):
    size = weight_ref.shape[1]
    rows = weight_ref.shape[0] // LOADS
    bands = [slice(n * rows, (n + 1) * rows) for n in range(LOADS)]
    return [
        pltpu.make_async_copy(weight_hbm.at[band, start : start + size], weight_ref.at[band, :], sems.at[n])
        for n, band in enumerate(bands)
    ]


def load_kernel(start, weight_hbm, weight_ref, sems):
    loads = weight_loads(start, weight_hbm, weight_ref, sems)
    for load in loads:
        load.start()
    for load in loads:
        load.wait()


def within_kernel(heads, start, rates_ref, q_ref, k_ref, v_ref, weight_hbm, out_ref, early_ref, weight_ref, sems):
    loads = weight_loads(start, weight_hbm, weight_ref, sems)
    for load in loads:
        load.start()
    rows, width = q_ref.shape[0], q_ref.shape[1] // heads
    half = rows // 2
    for h in range(heads):
        cols = slice(h * width, (h + 1) * width)
        rate = head_rate(rates_ref, h)
        upto = query_decay(rate, rows, half)
        q = q_ref[:, cols]
        early_ref[:, cols] = (q.astype(F32) * upto).astype(BF16)
        weights = decayed_pairs(q, k_ref[:, cols], upto, since_decay(rate, rows), half)
        out_ref[:, cols] = mix(weights, v_ref[:, cols], half)
    for load in loads:
        load.wait()


def project_kernel(slots, start, tile, first, last, *refs):
    pieces, refs = refs[:slots], refs[slots:]
    weight_ref, out_ref = refs[0], refs[-1]
    rows, size = pieces[0].shape[0], weight_ref.shape[1]
    spans = [slice(start, start + size) if p.shape[1] > size else slice(0, size) for p in pieces]
    index = lax.axis_index("head")
    core, line = index % 2, index // 2
    lines = slots // 2

    @pl.loop(0, weight_ref.shape[0] // tile)
    def one(step):
        cols = pl.ds(pl.multiple_of(step * tile, tile), tile)
        whole = jnp.concatenate([p[:, s] for p, s in zip(pieces, spans)], axis=0)
        total = dot(whole, weight_ref[cols, :], NT)
        if not first:
            total = total + refs[1][:, cols]
        if not last:
            out_ref[:, cols] = total
            return
        for slot in range(slots):
            place = ((line + slot // 2) % lines) * 2 + (core ^ (slot % 2))
            at = pl.ds(pl.multiple_of(place * rows, rows), rows)
            out_ref[at, cols] = total[slot * rows : (slot + 1) * rows, :].astype(BF16)


def turn_kernel(heads, quarter, q_ref, within_ref, cot_ref, *rest):
    pieces, dout_ref, state_ref = rest[:GROUP], rest[GROUP], rest[GROUP + 1]
    outs, held = rest[GROUP + 2 : 2 * GROUP + 2], rest[2 * GROUP + 2]
    width = q_ref.shape[1] // heads
    collect(quarter, pieces, state_ref)
    for h in range(heads):
        cols = slice(h * width, (h + 1) * width)
        q = q_ref[:, cols]
        attended = within_ref[:, cols] + dot(q, state_ref[cols, :], NN)
        inverse = lax.rsqrt(jnp.mean(attended * attended, axis=-1, keepdims=True) + EPSILON)
        normed = attended * inverse
        cot = cot_ref[:, cols].astype(F32)
        dout = ((cot - normed * jnp.mean(cot * normed, axis=-1, keepdims=True)) * inverse).astype(BF16)
        dout_ref[:, cols] = dout
        held[cols, :] = dot(q, dout, TN).astype(BF16)
    deal(quarter, held, outs)


def query_grads_kernel(heads, rates_ref, q_ref, k_ref, v_ref, dout_ref, state_ref, gq_ref, gk_ref):
    rows, width = q_ref.shape[0], q_ref.shape[1] // heads
    half = rows // 2
    for h in range(heads):
        cols = slice(h * width, (h + 1) * width)
        rate = head_rate(rates_ref, h)
        upto = query_decay(rate, rows, width)
        dout = dout_ref[:, cols]
        dweights = decayed_pairs(dout, v_ref[:, cols], upto, since_decay(rate, rows), half)
        late = (dout.astype(F32) * upto).astype(BF16)
        gq = mix(dweights, k_ref[:, cols], half) + dot(late, state_ref[cols, :], NT)
        gq_ref[:, cols] = gq.astype(BF16)
        gk_ref[:, cols] = mix_back(dweights, q_ref[:, cols], half)


def value_grads_kernel(heads, rates_ref, q_ref, k_ref, v_ref, dout_ref, gv_ref, late_ref):
    rows, width = q_ref.shape[0], q_ref.shape[1] // heads
    half = rows // 2
    for h in range(heads):
        cols = slice(h * width, (h + 1) * width)
        rate = head_rate(rates_ref, h)
        upto = query_decay(rate, rows, width)
        weights = decayed_pairs(q_ref[:, cols], k_ref[:, cols], upto, since_decay(rate, rows), half)
        gv_ref[:, cols] = mix_back(weights, dout_ref[:, cols], half)
        late_ref[:, cols] = (v_ref[:, cols].astype(F32) * key_decay(rate, rows, width)).astype(BF16)


def finish_kernel(heads, quarter, k_ref, v_ref, gk_in, gv_in, *rest):
    pieces, gk_ref, gv_ref, held = rest[:GROUP], rest[GROUP], rest[GROUP + 1], rest[GROUP + 2]
    width = k_ref.shape[1] // heads
    collect(quarter, pieces, held)
    for h in range(heads):
        cols = slice(h * width, (h + 1) * width)
        back = held[cols, :]
        gk_ref[:, cols] = (gk_in[:, cols] + dot(v_ref[:, cols], back, NT)).astype(BF16)
        gv_ref[:, cols] = (gv_in[:, cols] + dot(k_ref[:, cols], back, NN)).astype(BF16)


def scan(pieces, rates, rows, axis, count, reverse, beside):
    piece = jax.ShapeDtypeStruct(pieces[0].shape, BF16)
    order = list(range(GROUP))
    if reverse:
        order.reverse()

    def swap(x, bits):
        return lax.ppermute(x, axis, [(i, i ^ bits) for i in range(count)])

    got = [pieces[0]] + [swap(pieces[s], s) for s in range(1, GROUP)]
    got, first = lax.optimization_barrier((got, beside[0]()))
    (total,) = call(
        functools.partial(total_kernel, order, rows), [piece], [PLAIN] * (1 + GROUP), limit=4
    )(rates, *got)
    groups = count // GROUP

    def shift(x, by):
        step = -by if reverse else by
        return lax.ppermute(x, axis, [(i, (i + step * GROUP) % count) for i in range(count)])

    carry = total
    if groups > 1:
        carry = shift(total, 1)
        span = 1
        while span < groups - 1:
            carry = widen(carry, shift(carry, span), rates, rows, axis, groups, span, reverse)
            span *= 2
    carry, second = lax.optimization_barrier((carry, beside[1](total)))
    back = call(
        functools.partial(spread_kernel, order, rows, groups, reverse),
        [piece] * GROUP,
        [PLAIN] * (2 + GROUP),
        limit=4,
    )(rates, carry, *got)
    return back, [back[0]] + [swap(back[s], s) for s in range(1, GROUP)], carry, first, second


def widen_kernel(rows, groups, span, reverse, rates_ref, near_ref, far_ref, out_ref):
    quarter, width = out_ref.shape
    group = lax.axis_index("ctx") // GROUP
    reached = group + span + 1 <= groups - 1 if reverse else group >= span + 1
    for me in range(GROUP):

        @pl.when(group_member() == me)
        def _():
            for part, head in owned_parts(quarter, me, width):
                decay = jnp.exp(GROUP * rows * span * head_rate(rates_ref, head))
                far = jnp.where(reached, far_ref[part, :].astype(F32), 0.0)
                out_ref[part, :] = (near_ref[part, :].astype(F32) + decay * far).astype(BF16)


def widen(near, far, rates, rows, axis, groups, span, reverse):
    kernel = functools.partial(widen_kernel, rows, groups, span, reverse)
    return call(kernel, [jax.ShapeDtypeStruct(near.shape, BF16)], [PLAIN] * 3, limit=4)(rates, near, far)[0]


def gather_lines(parts, axis, count):
    lines = count // 2
    shifts = [[(i, (i - 2 * s) % count) for i in range(count)] for s in range(1, lines)]
    return [[lax.ppermute(part, axis, pairs) for pairs in shifts] for part in parts]


def flipped(x, axis, count):
    return lax.ppermute(x, axis, [(i, i ^ 1) for i in range(count)])


def project(near, moved, flips, weight, before, start, last, count):
    slots = near + [x for pair in zip(moved, flips) for x in pair]
    wide = weight.shape[0]
    operands = slots + [weight] + ([] if before is None else [before])
    (total,) = call(
        functools.partial(project_kernel, count, start, 512 if wide % 512 == 0 else wide, before is None, last),
        [jax.ShapeDtypeStruct((near[0].shape[0] * count, wide), BF16 if last else F32)],
        [PLAIN] * len(operands),
    )(*operands)
    return total


def body(ctx_count, head_count, query, key_in, value, out_weight, grad_layer, decay_exp):
    rows, flat = query.shape
    heads = decay_exp.shape[0]
    width = flat // heads
    quarter = flat // GROUP
    near, model = grad_layer.shape
    third = model // 3
    cuts = [(0, 2 * third), (2 * third, third)]

    piece = jax.ShapeDtypeStruct((quarter, width), BF16)
    whole_rows = jax.ShapeDtypeStruct((rows, flat), BF16)
    whole_sums = jax.ShapeDtypeStruct((rows, flat), F32)
    whole_state = jax.ShapeDtypeStruct((flat, width), BF16)
    held = pltpu.VMEM((flat, width), BF16)

    made = call(
        functools.partial(local_state_kernel, heads, quarter, cuts),
        [piece] * GROUP
        + [jax.ShapeDtypeStruct((near, part), BF16) for _, part in cuts]
        + [jax.ShapeDtypeStruct((8 * heads, 128), F32)]
        + [whole_rows] * 4,
        [STREAM] * 5,
        [
            held,
            pltpu.SMEM((heads,), jnp.int32),
            pltpu.SemaphoreType.DMA((2, max(n for n in (1, 2, 3, 4) if heads % n == 0))),
            pltpu.SemaphoreType.DMA((len(cuts) + 2,)),
        ],
    )(decay_exp, query, key_in, value, grad_layer)
    pieces, parts = made[:GROUP], made[GROUP:-5]
    rates, query, key_in, value, late_keys = made[-5:]

    wide = out_weight.shape[0]
    load_sems = pltpu.SemaphoreType.DMA((LOADS,))
    moved = gather_lines(parts, "head", head_count)

    def within():
        return call(
            functools.partial(within_kernel, heads, cuts[1][0]),
            [whole_sums, whole_rows, jax.ShapeDtypeStruct((wide, cuts[1][1]), BF16)],
            [PLAIN] * 4 + [STREAM],
            [load_sems],
        )(rates, query, key_in, value, out_weight)

    def load(total):
        weight, own, first, _ = lax.optimization_barrier((out_weight, grad_layer, moved[0], total))
        (held_weight,) = call(
            functools.partial(load_kernel, cuts[0][0]),
            [jax.ShapeDtypeStruct((wide, cuts[0][1]), BF16)],
            [STREAM],
            [load_sems],
            limit=2,
        )(weight)
        flips.append([flipped(x, "head", head_count) for x in first])
        near.extend([grad_layer, flipped(own, "head", head_count)])
        return held_weight

    flips, near = [], []
    spread, state, carry, (attended, early_queries, late_weight), early_weight = scan(
        pieces, rates, rows, "ctx", ctx_count, False, [within, load]
    )
    last_moved, _ = lax.optimization_barrier((moved[1], carry))
    flips.append([flipped(x, "head", head_count) for x in last_moved])
    early_weight, _ = lax.optimization_barrier((early_weight, spread))
    partial = project(near, moved[0], flips[0], early_weight, None, cuts[0][0], False, head_count)
    cotangent = project(near, moved[1], flips[1], late_weight, partial, cuts[1][0], True, head_count)

    turned = call(
        functools.partial(turn_kernel, heads, quarter),
        [whole_rows, whole_state] + [piece] * GROUP,
        [PLAIN] * (3 + GROUP),
        [held],
    )(early_queries, attended, cotangent, *state)
    dout, forward_state, pieces = turned[0], turned[1], turned[2:]

    def query_grads():
        return call(functools.partial(query_grads_kernel, heads), [whole_rows, whole_sums], [PLAIN] * 6)(
            rates, query, key_in, value, dout, forward_state
        )

    def value_grads(_):
        return call(functools.partial(value_grads_kernel, heads), [whole_sums, whole_rows], [PLAIN] * 5)(
            rates, query, key_in, value, dout
        )

    _, back, _, (grad_query, key_part), (value_part, late_values) = scan(
        pieces, rates, rows, "ctx", ctx_count, True, [query_grads, value_grads]
    )

    grad_key, grad_value = call(
        functools.partial(finish_kernel, heads, quarter), [whole_rows] * 2, [PLAIN] * (4 + GROUP), [held]
    )(late_keys, late_values, key_part, value_part, *back)
    return grad_query, grad_key, grad_value


def solution(mesh):
    return jax.shard_map(
        functools.partial(body, mesh.shape["ctx"], mesh.shape["head"]),
        mesh=mesh,
        in_specs=(
            P("ctx", "head"),
            P("ctx", "head"),
            P("ctx", "head"),
            P("head", None),
            P(("ctx", "head"), None),
            P("head"),
        ),
        out_specs=(P("ctx", "head"), P("ctx", "head"), P("ctx", "head")),
        check_vma=False,
    )
```

```python
import functools

import jax
import jax.numpy as jnp
from jax import lax
from jax.experimental import pallas as pl
from jax.experimental.pallas import tpu as pltpu
from jax.sharding import PartitionSpec as P

EPSILON = 1e-06
GROUP = 4
BF16 = jnp.bfloat16
F32 = jnp.float32

PLAIN = pl.BlockSpec(memory_space=pltpu.VMEM)
STREAM = pl.BlockSpec(memory_space=pltpu.HBM)


def call(kernel, outs, in_specs, scratch=(), limit=8, work=1):
    made = pl.pallas_call(
        kernel,
        out_shape=outs,
        in_specs=in_specs,
        out_specs=[PLAIN] * len(outs),
        scratch_shapes=list(scratch),
        compiler_params=pltpu.CompilerParams(vmem_limit_bytes=limit * 2**20),
        cost_estimate=pl.CostEstimate(flops=work, bytes_accessed=1, transcendentals=0),
    )

    def run(*operands):
        held = [
            pltpu.with_memory_space_constraint(x, pltpu.HBM) if spec is STREAM else x
            for x, spec in zip(operands, in_specs)
        ]
        return made(*held)

    return run


def dot(a, b, dims):
    return lax.dot_general(a, b, (dims, ((), ())), preferred_element_type=F32)


NN = ((1,), (0,))
NT = ((1,), (1,))
TN = ((0,), (0,))


def steps_from(rows, width, axis, start, turn):
    place = lax.broadcasted_iota(jnp.int32, (rows, width), axis)
    return (start + turn * place).astype(F32)


def query_decay(rate, rows, width):
    return jnp.exp(steps_from(rows, width, 0, 1, 1) * rate)


def key_decay(rate, rows, width):
    return jnp.exp(steps_from(rows, width, 0, rows - 1, -1) * rate)


def since_decay(rate, rows):
    return jnp.exp(steps_from(8, rows, 1, -1, -1) * rate)[0:1]


def head_rate(rates_ref, head):
    return rates_ref[8 * head : 8 * head + 1, 0:1]


def group_member():
    return lax.axis_index("ctx") % GROUP


def decayed_pairs(left, right, upto, since, half):
    keep = steps_from(half, half, 0, 0, 1) >= steps_from(half, half, 1, 0, 1)

    def tile(rows, columns):
        pair = dot(left[rows], right[columns], NT)
        return pair * upto[rows, :half] * since[:, columns]

    low, high = slice(0, half), slice(half, 2 * half)
    top = jnp.where(keep, tile(low, low), 0.0).astype(BF16)
    side = tile(high, low).astype(BF16)
    end = jnp.where(keep, tile(high, high), 0.0).astype(BF16)
    return top, jnp.concatenate([side, end], axis=1)


def mix(pairs, values, half):
    top, bottom = pairs
    return jnp.concatenate([dot(top, values[:half], NN), dot(bottom, values, NN)], axis=0)


def mix_back(pairs, values, half):
    top, bottom = pairs
    low = dot(top, values[:half], TN)
    both = dot(bottom, values[half:], TN)
    return jnp.concatenate([low + both[:half], both[half:]], axis=0)


def deal(quarter, held, outs):
    for slot in range(GROUP):
        start = pl.multiple_of((group_member() ^ slot) * quarter, 16)
        outs[slot][...] = held[pl.ds(start, quarter), :]


def collect(quarter, pieces, held):
    for slot in range(GROUP):
        start = pl.multiple_of((group_member() ^ slot) * quarter, 16)
        held[pl.ds(start, quarter), :] = pieces[slot][...]


def local_state_kernel(heads, quarter, exponent_hbm, q_hbm, k_hbm, v_hbm, grad_hbm, *rest):
    outs, rest = rest[:GROUP], rest[GROUP:]
    rates_ref, q_ref, k_ref, v_ref, late_ref, grad_ref, held, exponent_ref, sems, later = rest
    rows = k_ref.shape[0]
    width = k_ref.shape[1] // heads
    exponents = pltpu.make_async_copy(exponent_hbm, exponent_ref, later.at[2])
    exponents.start()
    loads = []
    chunks = sems.shape[1]
    for chunk in range(chunks):
        cols = slice(chunk * heads // chunks * width, (chunk + 1) * heads // chunks * width)
        loads.append(
            [
                pltpu.make_async_copy(source.at[:, cols], target.at[:, cols], sems.at[n, chunk])
                for n, (source, target) in enumerate(((k_hbm, k_ref), (v_hbm, v_ref)))
            ]
        )
        for load in loads[-1]:
            load.start()
    moves = [
        pltpu.make_async_copy(q_hbm, q_ref, later.at[0]),
        pltpu.make_async_copy(grad_hbm, grad_ref, later.at[1]),
    ]
    for move in moves:
        move.start()
    exponents.wait()
    for h in range(heads):
        spread = jnp.full((8, 128), exponent_ref[h].astype(F32))
        rates_ref[8 * h : 8 * h + 8, :] = jnp.log1p(-jnp.exp2(-spread))
    for h in range(heads):
        if h % (heads // chunks) == 0:
            for load in loads[h * chunks // heads]:
                load.wait()
        cols = slice(h * width, (h + 1) * width)
        k = (k_ref[:, cols].astype(F32) * key_decay(head_rate(rates_ref, h), rows, width)).astype(BF16)
        late_ref[:, cols] = k
        held[cols, :] = dot(k, v_ref[:, cols], TN).astype(BF16)
    deal(quarter, held, outs)
    for move in moves:
        move.wait()


def owned_parts(quarter, member, width):
    start = member * quarter
    while start < (member + 1) * quarter:
        head = start // width
        end = min((head + 1) * width, (member + 1) * quarter)
        yield slice(start - member * quarter, end - member * quarter), head
        start = end


def total_kernel(order, rows, rates_ref, *rest):
    pieces, out_ref = rest[:GROUP], rest[GROUP]
    quarter, width = out_ref.shape
    for me in range(GROUP):

        @pl.when(group_member() == me)
        def _():
            for part, head in owned_parts(quarter, me, width):
                decay = jnp.exp(rows * head_rate(rates_ref, head))
                total = None
                for m in order:
                    state = pieces[m ^ me][part, :].astype(F32)
                    total = state if total is None else total * decay + state
                out_ref[part, :] = total.astype(BF16)


def spread_kernel(order, rows, groups, reverse, rates_ref, carry_ref, *rest):
    pieces, outs = rest[:GROUP], rest[GROUP:]
    quarter, width = outs[0].shape
    group = lax.axis_index("ctx") // GROUP
    first = group == (groups - 1 if reverse else 0)
    for me in range(GROUP):

        @pl.when(group_member() == me)
        def _():
            for part, head in owned_parts(quarter, me, width):
                decay = jnp.exp(rows * head_rate(rates_ref, head))
                state = jnp.where(first, 0.0, carry_ref[part, :].astype(F32))
                for n, m in enumerate(order):
                    outs[m ^ me][part, :] = state.astype(BF16)
                    if n + 1 < GROUP:
                        state = state * decay + pieces[m ^ me][part, :].astype(F32)


def within_kernel(heads, rates_ref, q_ref, k_ref, v_ref, out_ref, early_ref):
    rows, width = q_ref.shape[0], q_ref.shape[1] // heads
    half = rows // 2
    for h in range(heads):
        cols = slice(h * width, (h + 1) * width)
        rate = head_rate(rates_ref, h)
        upto = query_decay(rate, rows, half)
        q = q_ref[:, cols]
        early_ref[:, cols] = (q.astype(F32) * upto).astype(BF16)
        weights = decayed_pairs(q, k_ref[:, cols], upto, since_decay(rate, rows), half)
        out_ref[:, cols] = mix(weights, v_ref[:, cols], half)


def project_kernel(slots, tile, *refs):
    pieces, weight_ref, out_ref = refs[:slots], refs[slots], refs[slots + 1]
    rows = pieces[0].shape[0]
    index = lax.axis_index("head")
    core, line = index % 2, index // 2
    lines = slots // 2

    @pl.loop(0, weight_ref.shape[0] // tile)
    def one(step):
        cols = pl.ds(pl.multiple_of(step * tile, tile), tile)
        whole = jnp.concatenate([p[...] for p in pieces], axis=0)
        total = dot(whole, weight_ref[cols, :], NT)
        for slot in range(slots):
            place = ((line + slot // 2) % lines) * 2 + (core ^ (slot % 2))
            at = pl.ds(pl.multiple_of(place * rows, rows), rows)
            out_ref[at, cols] = total[slot * rows : (slot + 1) * rows, :].astype(BF16)


def turn_kernel(heads, quarter, q_ref, within_ref, cot_ref, *rest):
    pieces, dout_ref, state_ref = rest[:GROUP], rest[GROUP], rest[GROUP + 1]
    outs, held = rest[GROUP + 2 : 2 * GROUP + 2], rest[2 * GROUP + 2]
    width = q_ref.shape[1] // heads
    collect(quarter, pieces, state_ref)
    for h in range(heads):
        cols = slice(h * width, (h + 1) * width)
        q = q_ref[:, cols]
        attended = within_ref[:, cols] + dot(q, state_ref[cols, :], NN)
        inverse = lax.rsqrt(jnp.mean(attended * attended, axis=-1, keepdims=True) + EPSILON)
        normed = attended * inverse
        cot = cot_ref[:, cols].astype(F32)
        dout = ((cot - normed * jnp.mean(cot * normed, axis=-1, keepdims=True)) * inverse).astype(BF16)
        dout_ref[:, cols] = dout
        held[cols, :] = dot(q, dout, TN).astype(BF16)
    deal(quarter, held, outs)


def query_grads_kernel(heads, rates_ref, q_ref, k_ref, v_ref, dout_ref, state_ref, gq_ref, gk_ref):
    rows, width = q_ref.shape[0], q_ref.shape[1] // heads
    half = rows // 2
    for h in range(heads):
        cols = slice(h * width, (h + 1) * width)
        rate = head_rate(rates_ref, h)
        upto = query_decay(rate, rows, width)
        dout = dout_ref[:, cols]
        dweights = decayed_pairs(dout, v_ref[:, cols], upto, since_decay(rate, rows), half)
        late = (dout.astype(F32) * upto).astype(BF16)
        gq = mix(dweights, k_ref[:, cols], half) + dot(late, state_ref[cols, :], NT)
        gq_ref[:, cols] = gq.astype(BF16)
        gk_ref[:, cols] = mix_back(dweights, q_ref[:, cols], half)


def value_grads_kernel(heads, rates_ref, q_ref, k_ref, v_ref, dout_ref, gv_ref, late_ref):
    rows, width = q_ref.shape[0], q_ref.shape[1] // heads
    half = rows // 2
    for h in range(heads):
        cols = slice(h * width, (h + 1) * width)
        rate = head_rate(rates_ref, h)
        upto = query_decay(rate, rows, width)
        weights = decayed_pairs(q_ref[:, cols], k_ref[:, cols], upto, since_decay(rate, rows), half)
        gv_ref[:, cols] = mix_back(weights, dout_ref[:, cols], half)
        late_ref[:, cols] = (v_ref[:, cols].astype(F32) * key_decay(rate, rows, width)).astype(BF16)


def finish_kernel(heads, quarter, k_ref, v_ref, gk_in, gv_in, *rest):
    pieces, gk_ref, gv_ref, held = rest[:GROUP], rest[GROUP], rest[GROUP + 1], rest[GROUP + 2]
    width = k_ref.shape[1] // heads
    collect(quarter, pieces, held)
    for h in range(heads):
        cols = slice(h * width, (h + 1) * width)
        back = held[cols, :]
        gk_ref[:, cols] = (gk_in[:, cols] + dot(v_ref[:, cols], back, NT)).astype(BF16)
        gv_ref[:, cols] = (gv_in[:, cols] + dot(k_ref[:, cols], back, NN)).astype(BF16)


def scan(pieces, rates, rows, axis, count, reverse, beside):
    piece = jax.ShapeDtypeStruct(pieces[0].shape, BF16)
    order = list(range(GROUP))
    if reverse:
        order.reverse()

    def swap(x, bits):
        return lax.ppermute(x, axis, [(i, i ^ bits) for i in range(count)])

    got = [pieces[0]] + [swap(pieces[s], s) for s in range(1, GROUP)]
    got, first = lax.optimization_barrier((got, beside[0]()))
    (total,) = call(
        functools.partial(total_kernel, order, rows), [piece], [PLAIN] * (1 + GROUP), limit=4
    )(rates, *got)
    groups = count // GROUP

    def shift(x, by):
        step = -by if reverse else by
        return lax.ppermute(x, axis, [(i, (i + step * GROUP) % count) for i in range(count)])

    carry = total
    if groups > 1:
        carry = shift(total, 1)
        span = 1
        while span < groups - 1:
            carry = widen(carry, shift(carry, span), rates, rows, axis, groups, span, reverse)
            span *= 2
    carry, second = lax.optimization_barrier((carry, beside[1](total)))
    back = call(
        functools.partial(spread_kernel, order, rows, groups, reverse),
        [piece] * GROUP,
        [PLAIN] * (2 + GROUP),
        limit=4,
    )(rates, carry, *got)
    return [back[0]] + [swap(back[s], s) for s in range(1, GROUP)], carry, first, second


def widen_kernel(rows, groups, span, reverse, rates_ref, near_ref, far_ref, out_ref):
    quarter, width = out_ref.shape
    group = lax.axis_index("ctx") // GROUP
    reached = group + span + 1 <= groups - 1 if reverse else group >= span + 1
    for me in range(GROUP):

        @pl.when(group_member() == me)
        def _():
            for part, head in owned_parts(quarter, me, width):
                decay = jnp.exp(GROUP * rows * span * head_rate(rates_ref, head))
                far = jnp.where(reached, far_ref[part, :].astype(F32), 0.0)
                out_ref[part, :] = (near_ref[part, :].astype(F32) + decay * far).astype(BF16)


def widen(near, far, rates, rows, axis, groups, span, reverse):
    kernel = functools.partial(widen_kernel, rows, groups, span, reverse)
    return call(kernel, [jax.ShapeDtypeStruct(near.shape, BF16)], [PLAIN] * 3, limit=4)(rates, near, far)[0]


def gather_lines(x, axis, count):
    lines = count // 2
    return [lax.ppermute(x, axis, [(i, (i - 2 * s) % count) for i in range(count)]) for s in range(1, lines)]


def flipped(x, axis, count):
    return lax.ppermute(x, axis, [(i, i ^ 1) for i in range(count)])


def project(slots, weight):
    wide = weight.shape[0]
    return call(
        functools.partial(project_kernel, len(slots), 512 if wide % 512 == 0 else wide),
        [jax.ShapeDtypeStruct((slots[0].shape[0] * len(slots), wide), BF16)],
        [PLAIN] * (len(slots) + 1),
    )(*slots, weight)[0]


def body(ctx_count, head_count, query, key_in, value, out_weight, grad_layer, decay_exp):
    rows, flat = query.shape
    heads = decay_exp.shape[0]
    width = flat // heads
    quarter = flat // GROUP

    piece = jax.ShapeDtypeStruct((quarter, width), BF16)
    whole_rows = jax.ShapeDtypeStruct((rows, flat), BF16)
    whole_sums = jax.ShapeDtypeStruct((rows, flat), F32)
    whole_state = jax.ShapeDtypeStruct((flat, width), BF16)
    held = pltpu.VMEM((flat, width), BF16)

    moved = gather_lines(grad_layer, "head", head_count)
    made = call(
        functools.partial(local_state_kernel, heads, quarter),
        [piece] * GROUP
        + [jax.ShapeDtypeStruct((8 * heads, 128), F32)]
        + [whole_rows] * 4
        + [jax.ShapeDtypeStruct(grad_layer.shape, BF16)],
        [STREAM] * 5,
        [
            held,
            pltpu.SMEM((heads,), jnp.int32),
            pltpu.SemaphoreType.DMA((2, max(n for n in (1, 2, 3, 4) if heads % n == 0))),
            pltpu.SemaphoreType.DMA((3,)),
        ],
        work=3 * 10**9,
    )(decay_exp, query, key_in, value, grad_layer)
    pieces = made[:GROUP]
    rates, query, key_in, value, late_keys, own = made[GROUP:]

    def within():
        return call(
            functools.partial(within_kernel, heads), [whole_sums, whole_rows], [PLAIN] * 4, work=3 * 10**9
        )(rates, query, key_in, value)

    def other(total):
        held_own, _ = lax.optimization_barrier((own, total))
        others.append(flipped(held_own, "head", head_count))
        return ()

    others = []
    state, carry, (attended, early_queries), _ = scan(
        pieces, rates, rows, "ctx", ctx_count, False, [within, other]
    )
    moved, _ = lax.optimization_barrier((moved, carry))
    slots = [own] + others
    for x in moved:
        slots += [x, flipped(x, "head", head_count)]
    cotangent = project(slots, out_weight)

    turned = call(
        functools.partial(turn_kernel, heads, quarter),
        [whole_rows, whole_state] + [piece] * GROUP,
        [PLAIN] * (3 + GROUP),
        [held],
    )(early_queries, attended, cotangent, *state)
    dout, forward_state, pieces = turned[0], turned[1], turned[2:]

    def query_grads():
        return call(functools.partial(query_grads_kernel, heads), [whole_rows, whole_sums], [PLAIN] * 6)(
            rates, query, key_in, value, dout, forward_state
        )

    def value_grads(_):
        return call(functools.partial(value_grads_kernel, heads), [whole_sums, whole_rows], [PLAIN] * 5)(
            rates, query, key_in, value, dout
        )

    back, _, (grad_query, key_part), (value_part, late_values) = scan(
        pieces, rates, rows, "ctx", ctx_count, True, [query_grads, value_grads]
    )

    grad_key, grad_value = call(
        functools.partial(finish_kernel, heads, quarter), [whole_rows] * 2, [PLAIN] * (4 + GROUP), [held]
    )(late_keys, late_values, key_part, value_part, *back)
    return grad_query, grad_key, grad_value


def solution(mesh):
    return jax.shard_map(
        functools.partial(body, mesh.shape["ctx"], mesh.shape["head"]),
        mesh=mesh,
        in_specs=(
            P("ctx", "head"),
            P("ctx", "head"),
            P("ctx", "head"),
            P("head", None),
            P(("ctx", "head"), None),
            P("head"),
        ),
        out_specs=(P("ctx", "head"), P("ctx", "head"), P("ctx", "head")),
        check_vma=False,
    )
```

```python
import functools

import jax
import jax.numpy as jnp
from jax import lax
from jax.experimental import pallas as pl
from jax.experimental.pallas import tpu as pltpu
from jax.sharding import PartitionSpec as P

EPSILON = 1e-06
GROUP = 4
SENT = (0, 1, 3, 2)
BF16 = jnp.bfloat16
F32 = jnp.float32

PLAIN = pl.BlockSpec(memory_space=pltpu.VMEM)
STREAM = pl.BlockSpec(memory_space=pltpu.HBM)


def call(kernel, outs, in_specs, scratch=(), limit=8, work=1, out_specs=None, aliases=None):
    made = pl.pallas_call(
        kernel,
        out_shape=outs,
        in_specs=in_specs,
        out_specs=out_specs or [PLAIN] * len(outs),
        scratch_shapes=list(scratch),
        input_output_aliases=aliases or {},
        compiler_params=pltpu.CompilerParams(vmem_limit_bytes=limit * 2**20),
        cost_estimate=pl.CostEstimate(flops=work, bytes_accessed=1, transcendentals=0),
    )

    def run(*operands):
        held = [
            pltpu.with_memory_space_constraint(x, pltpu.HBM) if spec is STREAM else x
            for x, spec in zip(operands, in_specs)
        ]
        return made(*held)

    return run


def dot(a, b, dims):
    return lax.dot_general(a, b, (dims, ((), ())), preferred_element_type=F32)


NN = ((1,), (0,))
NT = ((1,), (1,))
TN = ((0,), (0,))


def steps_from(rows, width, axis, start, turn):
    place = lax.broadcasted_iota(jnp.int32, (rows, width), axis)
    return (start + turn * place).astype(F32)


def query_decay(rate, rows, width):
    return jnp.exp(steps_from(rows, width, 0, 1, 1) * rate)


def key_decay(rate, rows, width):
    return jnp.exp(steps_from(rows, width, 0, rows - 1, -1) * rate)


def since_decay(rate, rows):
    return jnp.exp(steps_from(8, rows, 1, -1, -1) * rate)[0:1]


def head_rate(rates_ref, head):
    return rates_ref[band(head, 8), :][0:1, 0:1]


def band(place, size):
    return pl.ds(pl.multiple_of(place * size, size), size)


def slot_heads(slots, heads):
    per = -(-heads // GROUP)

    def visit(one):
        for n, slot in enumerate(slots):
            for j in range(per):
                head = (group_member() ^ slot) * per + j
                if heads % GROUP == 0:
                    one(n * per + j, head)
                else:
                    pl.when(head < heads)(functools.partial(one, n * per + j, head))

    return visit


def group_member():
    return lax.axis_index("ctx") % GROUP


def decayed_pairs(left, right, upto, since, half):
    keep = steps_from(half, half, 0, 0, 1) >= steps_from(half, half, 1, 0, 1)

    def tile(rows, columns):
        pair = dot(left[rows], right[columns], NT)
        return pair * upto[rows, :half] * since[:, columns]

    low, high = slice(0, half), slice(half, 2 * half)
    top = jnp.where(keep, tile(low, low), 0.0).astype(BF16)
    side = tile(high, low).astype(BF16)
    end = jnp.where(keep, tile(high, high), 0.0).astype(BF16)
    return top, jnp.concatenate([side, end], axis=1)


def mix(pairs, values, half):
    top, bottom = pairs
    return jnp.concatenate([dot(top, values[:half], NN), dot(bottom, values, NN)], axis=0)


def mix_back(pairs, values, half):
    top, bottom = pairs
    low = dot(top, values[:half], TN)
    both = dot(bottom, values[half:], TN)
    return jnp.concatenate([low + both[:half], both[half:]], axis=0)


def deal(quarter, held, outs):
    for slot in range(GROUP):
        outs[slot][...] = held[band(group_member() ^ slot, quarter), :]


def local_state_kernel(heads, quarter, exponent_hbm, q_hbm, k_hbm, v_hbm, grad_hbm, *rest):
    outs, rest = rest[:GROUP], rest[GROUP:]
    rates_ref, q_ref, k_ref, v_ref, late_ref, grad_ref, held, exponent_ref, sems, later = rest
    rows = k_ref.shape[0]
    width = k_ref.shape[1] // heads
    exponents = pltpu.make_async_copy(exponent_hbm, exponent_ref, later.at[2])
    exponents.start()
    loads = []
    chunks = sems.shape[1]
    for chunk in range(chunks):
        cols = slice(chunk * heads // chunks * width, (chunk + 1) * heads // chunks * width)
        loads.append(
            [
                pltpu.make_async_copy(source.at[:, cols], target.at[:, cols], sems.at[n, chunk])
                for n, (source, target) in enumerate(((k_hbm, k_ref), (v_hbm, v_ref)))
            ]
        )
        for load in loads[-1]:
            load.start()
    moves = [
        pltpu.make_async_copy(q_hbm, q_ref, later.at[0]),
        pltpu.make_async_copy(grad_hbm, grad_ref, later.at[1]),
    ]
    for move in moves:
        move.start()
    exponents.wait()
    for h in range(heads):
        spread = jnp.full((8, 128), exponent_ref[h].astype(F32))
        rates_ref[8 * h : 8 * h + 8, :] = jnp.log1p(-jnp.exp2(-spread))
    for h in range(heads):
        if h % (heads // chunks) == 0:
            for load in loads[h * chunks // heads]:
                load.wait()
        cols = slice(h * width, (h + 1) * width)
        k = (k_ref[:, cols].astype(F32) * key_decay(head_rate(rates_ref, h), rows, width)).astype(BF16)
        late_ref[:, cols] = k
        held[cols, :] = dot(k, v_ref[:, cols], TN).astype(BF16)
    deal(quarter, held, outs)
    for move in moves:
        move.wait()


def owned_parts(member, heads, width):
    per = -(-heads // GROUP)
    for j in range(per):
        if member * per + j < heads:
            yield slice(j * width, (j + 1) * width), member * per + j


def total_kernel(order, rows, heads, rates_ref, *rest):
    pieces, out_ref = [rest[SENT.index(s)] for s in range(GROUP)], rest[GROUP]
    width = out_ref.shape[1]
    for me in range(GROUP):

        @pl.when(group_member() == me)
        def _():
            for part, head in owned_parts(me, heads, width):
                decay = jnp.exp(rows * head_rate(rates_ref, head))
                total = None
                for m in order:
                    state = pieces[m ^ me][part, :].astype(F32)
                    total = state if total is None else total * decay + state
                out_ref[part, :] = total.astype(BF16)


def spread_kernel(order, rows, heads, groups, reverse, rates_ref, carry_ref, *rest):
    pieces, outs = [rest[SENT.index(s)] for s in range(GROUP)], rest[GROUP:]
    width = outs[0].shape[1]
    group = lax.axis_index("ctx") // GROUP
    first = group == (groups - 1 if reverse else 0)
    for me in range(GROUP):

        @pl.when(group_member() == me)
        def _():
            for part, head in owned_parts(me, heads, width):
                decay = jnp.exp(rows * head_rate(rates_ref, head))
                state = jnp.where(first, 0.0, carry_ref[part, :].astype(F32))
                for n, m in enumerate(order):
                    outs[m ^ me][part, :] = state.astype(BF16)
                    if n + 1 < GROUP:
                        state = state * decay + pieces[m ^ me][part, :].astype(F32)


def within_kernel(heads, rates_ref, q_ref, k_ref, v_ref, out_ref, early_ref, late_ref, top_ref, bottom_ref):
    rows, width = q_ref.shape[0], q_ref.shape[1] // heads
    half = rows // 2
    for h in range(heads):
        cols = slice(h * width, (h + 1) * width)
        held = slice(h * half, (h + 1) * half)
        rate = head_rate(rates_ref, h)
        upto = query_decay(rate, rows, half)
        q, v = q_ref[:, cols], v_ref[:, cols]
        early_ref[:, cols] = (q.astype(F32) * upto).astype(BF16)
        late_ref[:, cols] = (v.astype(F32) * key_decay(rate, rows, width)).astype(BF16)
        weights = decayed_pairs(q, k_ref[:, cols], upto, since_decay(rate, rows), half)
        top_ref[held, :], bottom_ref[held, :] = weights
        out_ref[:, cols] = mix(weights, v, half)


def project_rows(slots, heads, width, pieces, weight_ref, cot_ref):
    count = len(pieces)
    rows = pieces[0].shape[0]
    per = -(-heads // GROUP)
    taken = per if heads % GROUP == 0 else 1
    tile = taken * width
    index = lax.axis_index("head")
    core, line = index % 2, index // 2

    @pl.loop(0, len(slots) * per // taken)
    def one(step):
        head = (group_member() ^ (slots[0] + step * taken // per)) * per + step * taken % per

        @pl.when(head < heads)
        def _():
            whole = jnp.concatenate([p[...] for p in pieces], axis=0)
            total = dot(whole, weight_ref[band(head // taken, tile), :], NT)
            for n in range(count):
                place = ((line + n // 2) % (count // 2)) * 2 + (core ^ (n % 2))
                cot_ref[band(place, rows), band(step, tile)] = total[n * rows : (n + 1) * rows, :].astype(BF16)


def turn_heads(slots, heads, early_ref, attended_ref, cot_ref, states, outs, dout_ref):
    width = early_ref.shape[1] // heads
    per = -(-heads // GROUP)

    @slot_heads(slots, heads)
    def two(n, head):
        cols = slice(n * width, (n + 1) * width)
        part = slice(n % per * width, (n % per + 1) * width)
        q = early_ref[:, band(head, width)]
        attended = attended_ref[:, band(head, width)] + dot(q, states[n // per][part, :], NN)
        inverse = lax.rsqrt(jnp.mean(attended * attended, axis=-1, keepdims=True) + EPSILON)
        normed = attended * inverse
        cot = cot_ref[:, cols].astype(F32)
        dout = ((cot - normed * jnp.mean(cot * normed, axis=-1, keepdims=True)) * inverse).astype(BF16)
        dout_ref[:, cols] = dout
        outs[n // per][part, :] = dot(q, dout, TN).astype(BF16)


def project_kernel(slots, heads, width, *refs):
    project_rows(slots, heads, width, refs[:-2], refs[-2], refs[-1])


def turn_kernel(slots, heads, early_ref, attended_ref, cot_ref, *refs):
    states, outs, dout_ref = refs[: len(slots)], refs[len(slots) : -1], refs[-1]
    turn_heads(slots, heads, early_ref, attended_ref, cot_ref, states, outs, dout_ref)


def turn_own_kernel(heads, width, early_ref, attended_ref, state_ref, *refs):
    pieces, (weight_ref, out_ref, dout_ref, cot_ref) = refs[:-4], refs[-4:]
    project_rows([0], heads, width, pieces, weight_ref, cot_ref)
    turn_heads([0], heads, early_ref, attended_ref, cot_ref, [state_ref], [out_ref], dout_ref)


def slot_columns(own_ref, rest_ref, n, width):
    at = n * width
    wide = own_ref.shape[1]
    return own_ref[:, at : at + width] if at < wide else rest_ref[:, at - wide : at - wide + width]


def value_grads_kernel(heads, top_ref, bottom_ref, own_ref, rest_ref, gv_ref):
    half = top_ref.shape[1]
    width = own_ref.shape[1] // -(-heads // GROUP)

    @slot_heads(range(GROUP), heads)
    def one(n, head):
        weights = top_ref[band(head, half), :], bottom_ref[band(head, half), :]
        gv_ref[:, n * width : (n + 1) * width] = mix_back(weights, slot_columns(own_ref, rest_ref, n, width), half)


def key_grads_kernel(heads, rates_ref, q_ref, v_ref, own_ref, rest_ref, gk_ref, top_ref, bottom_ref):
    rows, width = q_ref.shape[0], q_ref.shape[1] // heads
    half = rows // 2

    @slot_heads(range(GROUP), heads)
    def one(n, head):
        held = slice(n * half, (n + 1) * half)
        rate = head_rate(rates_ref, head)
        upto = query_decay(rate, rows, half)
        dout = slot_columns(own_ref, rest_ref, n, width)
        dweights = decayed_pairs(dout, v_ref[:, band(head, width)], upto, since_decay(rate, rows), half)
        top_ref[held, :], bottom_ref[held, :] = dweights
        gk_ref[:, n * width : (n + 1) * width] = mix_back(dweights, q_ref[:, band(head, width)], half)


def query_grads_kernel(heads, rates_ref, k_ref, top_ref, bottom_ref, own_ref, rest_ref, *rest):
    states, gq_ref = rest[:GROUP], rest[GROUP]
    rows, width = k_ref.shape[0], k_ref.shape[1] // heads
    half = rows // 2
    per = -(-heads // GROUP)

    @slot_heads(range(GROUP), heads)
    def one(n, head):
        held = slice(n * half, (n + 1) * half)
        dout = slot_columns(own_ref, rest_ref, n, width)
        late = (dout.astype(F32) * query_decay(head_rate(rates_ref, head), rows, width)).astype(BF16)
        state = states[n // per][n % per * width : (n % per + 1) * width, :]
        gq = mix((top_ref[held, :], bottom_ref[held, :]), k_ref[:, band(head, width)], half) + dot(late, state, NT)
        gq_ref[:, band(head, width)] = gq.astype(BF16)


def finish_kernel(slots, heads, taken_over, late_keys, late_values, gk_in, gv_in, *rest):
    backs, rest = rest[: len(slots)], rest[len(slots) + taken_over :]
    gk_hbm, gv_hbm, gk_ref, gv_ref, sems = rest
    per = -(-heads // GROUP)
    width = late_keys.shape[1] // heads

    def stores(n, head):
        cols = slice(n * width, (n + 1) * width)
        for side, (source, target) in enumerate(((gk_ref, gk_hbm), (gv_ref, gv_hbm))):
            yield pltpu.make_async_copy(source.at[:, cols], target.at[:, band(head, width)], sems.at[side, n])

    @slot_heads(slots, heads)
    def one(n, head):
        cols = slice(n * width, (n + 1) * width)
        at = (slots[n // per] * per + n % per) * width
        back = backs[n // per][n % per * width : (n % per + 1) * width, :]
        gk = gk_in[:, at : at + width] + dot(late_values[:, band(head, width)], back, NT)
        gv = gv_in[:, at : at + width] + dot(late_keys[:, band(head, width)], back, NN)
        gk_ref[:, cols] = gk.astype(BF16)
        gv_ref[:, cols] = gv.astype(BF16)
        for store in stores(n, head):
            store.start()

    @slot_heads(slots, heads)
    def two(n, head):
        for store in stores(n, head):
            store.wait()


def swaps(pieces, axis, count):
    return {s: lax.ppermute(pieces[s], axis, [(i, i ^ s) for i in range(count)]) for s in range(1, GROUP)}


def add_up(got, rates, rows, heads, reverse):
    order = list(reversed(range(GROUP))) if reverse else list(range(GROUP))
    kernel = functools.partial(total_kernel, order, rows, heads)
    return call(kernel, [jax.ShapeDtypeStruct(got[0].shape, BF16)], [PLAIN] * (1 + GROUP), limit=4)(
        rates, *[got[s] for s in SENT]
    )[0]


def from_groups(total, rates, rows, heads, axis, count, reverse):
    groups = count // GROUP

    def shift(x, by):
        step = -by if reverse else by
        return lax.ppermute(x, axis, [(i, (i + step * GROUP) % count) for i in range(count)])

    carry = total
    if groups > 1:
        carry = shift(total, 1)
        span = 1
        while span < groups - 1:
            carry = widen(carry, shift(carry, span), rates, rows, heads, groups, span, reverse)
            span *= 2
    return carry


def spread_out(carry, got, rates, rows, heads, count, reverse):
    order = list(reversed(range(GROUP))) if reverse else list(range(GROUP))
    kernel = functools.partial(spread_kernel, order, rows, heads, count // GROUP, reverse)
    piece = jax.ShapeDtypeStruct(carry.shape, BF16)
    return call(kernel, [piece] * GROUP, [PLAIN] * (2 + GROUP), limit=4)(rates, carry, *[got[s] for s in SENT])


def widen_kernel(rows, heads, groups, span, reverse, rates_ref, near_ref, far_ref, out_ref):
    width = out_ref.shape[1]
    group = lax.axis_index("ctx") // GROUP
    reached = group + span + 1 <= groups - 1 if reverse else group >= span + 1
    for me in range(GROUP):

        @pl.when(group_member() == me)
        def _():
            for part, head in owned_parts(me, heads, width):
                decay = jnp.exp(GROUP * rows * span * head_rate(rates_ref, head))
                far = jnp.where(reached, far_ref[part, :].astype(F32), 0.0)
                out_ref[part, :] = (near_ref[part, :].astype(F32) + decay * far).astype(BF16)


def widen(near, far, rates, rows, heads, groups, span, reverse):
    kernel = functools.partial(widen_kernel, rows, heads, groups, span, reverse)
    return call(kernel, [jax.ShapeDtypeStruct(near.shape, BF16)], [PLAIN] * 3, limit=4)(rates, near, far)[0]


def gather_lines(x, axis, count):
    lines = count // 2
    return [lax.ppermute(x, axis, [(i, (i - 2 * s) % count) for i in range(count)]) for s in range(1, lines)]


def flipped(x, axis, count):
    return lax.ppermute(x, axis, [(i, i ^ 1) for i in range(count)])


def after(x, *others):
    return lax.optimization_barrier((x, others))[0]


def body(ctx_count, head_count, query, key_in, value, out_weight, grad_layer, decay_exp):
    rows, flat = query.shape
    heads = decay_exp.shape[0]
    width = flat // heads
    per = -(-heads // GROUP)
    quarter = per * width
    half = rows // 2
    rest = list(range(1, GROUP))

    def shaped(*shape, dtype=BF16):
        return jax.ShapeDtypeStruct(shape, dtype)

    piece = shaped(quarter, width)
    whole_rows = shaped(rows, flat)
    slot_sums = shaped(rows, GROUP * quarter, dtype=F32)

    moved = gather_lines(grad_layer, "head", head_count)
    made = call(
        functools.partial(local_state_kernel, heads, quarter),
        [piece] * GROUP
        + [shaped(8 * heads, 128, dtype=F32)]
        + [whole_rows] * 4
        + [shaped(*grad_layer.shape)],
        [STREAM] * 5,
        [
            pltpu.VMEM((GROUP * quarter, width), BF16),
            pltpu.SMEM((heads,), jnp.int32),
            pltpu.SemaphoreType.DMA((2, max(n for n in (1, 2, 3, 4) if heads % n == 0))),
            pltpu.SemaphoreType.DMA((3,)),
        ],
        work=3 * 10**9,
    )(decay_exp, query, key_in, value, grad_layer)
    pieces = made[:GROUP]
    rates, query, key_in, value, late_keys, own = made[GROUP:]

    got = {0: pieces[0], **swaps(pieces, "ctx", ctx_count)}
    inner = call(
        functools.partial(within_kernel, heads),
        [shaped(rows, flat, dtype=F32), whole_rows, whole_rows, shaped(heads * half, half), shaped(heads * half, rows)],
        [PLAIN] * 4,
        work=3 * 10**9,
    )(rates, query, key_in, value)
    got = dict(zip(SENT, after([got[s] for s in SENT], *inner)))
    attended, early_queries, late_values, top, bottom = inner
    total = add_up(got, rates, rows, heads, False)
    carry = from_groups(total, rates, rows, heads, "ctx", ctx_count, False)
    slots = [own, flipped(after(own, total), "head", head_count)]
    for x in moved:
        x = after(x, carry)
        slots += [x, flipped(x, "head", head_count)]
    ready = spread_out(carry, got, rates, rows, heads, ctx_count, False)
    states = {0: ready[0], **swaps(ready, "ctx", ctx_count)}

    def projected(which, slots):
        kernel = functools.partial(project_kernel, which, heads, width)
        return call(kernel, [shaped(rows, len(which) * quarter)], [PLAIN] * (head_count + 1))(*slots, out_weight)[0]

    slots[-1] = after(slots[-1], ready)
    cot = projected(rest, slots)
    made = call(functools.partial(turn_kernel, rest, heads), [piece] * 3 + [shaped(rows, 3 * quarter)], [PLAIN] * 6)(
        early_queries, attended, cot, *[states[s] for s in rest]
    )
    pieces, dout_rest = dict(zip(rest, made)), made[-1]
    got = swaps(pieces, "ctx", ctx_count)
    mine, dout_own = call(
        functools.partial(turn_own_kernel, heads, width),
        [piece, shaped(rows, quarter)],
        [PLAIN] * (head_count + 4),
        [pltpu.VMEM((rows, quarter), BF16)],
    )(after(early_queries, dout_rest), attended, states[0], *slots, out_weight)
    (value_part,) = call(functools.partial(value_grads_kernel, heads), [slot_sums], [PLAIN] * 4)(
        top, bottom, dout_own, dout_rest
    )
    got = dict(zip(SENT, after([{0: mine, **got}[s] for s in SENT], value_part)))
    total = add_up(got, rates, rows, heads, True)
    carry = from_groups(total, rates, rows, heads, "ctx", ctx_count, True)
    key_part, top, bottom = call(
        functools.partial(key_grads_kernel, heads),
        [slot_sums, shaped(GROUP * per * half, half), shaped(GROUP * per * half, rows)],
        [PLAIN] * 5,
    )(rates, query, after(value, total), dout_own, dout_rest)
    ready = spread_out(after(carry, key_part), got, rates, rows, heads, ctx_count, True)
    back = {0: ready[0], **swaps(ready, "ctx", ctx_count)}
    (grad_query,) = call(functools.partial(query_grads_kernel, heads), [whole_rows], [PLAIN] * (6 + GROUP))(
        rates, after(key_in, ready[0]), top, bottom, dout_own, dout_rest, *[states[s] for s in range(GROUP)]
    )
    early_slots, late_slots = [0, 1], [3, 2]
    sums = [late_keys, late_values, key_part, value_part]
    grads = []
    for which, pieces in ((early_slots, [back[0], after(back[1], grad_query)]), (late_slots, None)):
        if pieces is None:
            pieces = after([back[s] for s in which], *grads)
        held = pltpu.VMEM((rows, 2 * quarter), BF16)
        grads = call(
            functools.partial(finish_kernel, which, heads, len(grads)),
            [whole_rows] * 2,
            [PLAIN] * 6 + [STREAM] * len(grads),
            [held, held, pltpu.SemaphoreType.DMA((2, 2 * per))],
            out_specs=[STREAM] * 2,
            aliases={6 + n: n for n in range(len(grads))},
        )(*sums, *pieces, *grads)
    grad_key, grad_value = grads
    return grad_query, grad_key, grad_value


def solution(mesh):
    return jax.shard_map(
        functools.partial(body, mesh.shape["ctx"], mesh.shape["head"]),
        mesh=mesh,
        in_specs=(
            P("ctx", "head"),
            P("ctx", "head"),
            P("ctx", "head"),
            P("head", None),
            P(("ctx", "head"), None),
            P("head"),
        ),
        out_specs=(P("ctx", "head"), P("ctx", "head"), P("ctx", "head")),
        check_vma=False,
    )
```

```python
import functools

import jax
import jax.numpy as jnp
from jax import lax
from jax.experimental import pallas as pl
from jax.experimental.pallas import tpu as pltpu
from jax.sharding import PartitionSpec as P

EPSILON = 1e-06
GROUP = 4
SENT = (0, 1, 3, 2)
BF16 = jnp.bfloat16
F32 = jnp.float32

PLAIN = pl.BlockSpec(memory_space=pltpu.VMEM)
STREAM = pl.BlockSpec(memory_space=pltpu.HBM)


def call(kernel, outs, in_specs, scratch=(), limit=8, work=1, out_specs=None, aliases=None):
    made = pl.pallas_call(
        kernel,
        out_shape=outs,
        in_specs=in_specs,
        out_specs=out_specs or [PLAIN] * len(outs),
        scratch_shapes=list(scratch),
        input_output_aliases=aliases or {},
        compiler_params=pltpu.CompilerParams(vmem_limit_bytes=limit * 2**20),
        cost_estimate=pl.CostEstimate(flops=work, bytes_accessed=1, transcendentals=0),
    )

    def run(*operands):
        held = [
            pltpu.with_memory_space_constraint(x, pltpu.HBM) if spec is STREAM else x
            for x, spec in zip(operands, in_specs)
        ]
        return made(*held)

    return run


def dot(a, b, dims):
    return lax.dot_general(a, b, (dims, ((), ())), preferred_element_type=F32)


NN = ((1,), (0,))
NT = ((1,), (1,))
TN = ((0,), (0,))


def steps_from(rows, width, axis, start, turn):
    place = lax.broadcasted_iota(jnp.int32, (rows, width), axis)
    return (start + turn * place).astype(F32)


def query_decay(rate, rows, width):
    return jnp.exp(steps_from(rows, width, 0, 1, 1) * rate)


def key_decay(rate, rows, width):
    return jnp.exp(steps_from(rows, width, 0, rows - 1, -1) * rate)


def since_decay(rate, rows):
    return jnp.exp(steps_from(8, rows, 1, -1, -1) * rate)[0:1]


def head_rate(rates_ref, head):
    return rates_ref[band(head, 8), :][0:1, 0:1]


def band(place, size):
    return pl.ds(pl.multiple_of(place * size, size), size)


def slot_heads(slots, heads):
    per = -(-heads // GROUP)

    def visit(one):
        for n, slot in enumerate(slots):
            for j in range(per):
                head = (group_member() ^ slot) * per + j
                if heads % GROUP == 0:
                    one(n * per + j, head)
                else:
                    pl.when(head < heads)(functools.partial(one, n * per + j, head))

    return visit


def group_member():
    return lax.axis_index("ctx") % GROUP


def decayed_pairs(left, right, upto, since, half):
    keep = steps_from(half, half, 0, 0, 1) >= steps_from(half, half, 1, 0, 1)

    def tile(rows, columns):
        pair = dot(left[rows], right[columns], NT)
        return pair * upto[rows, :half] * since[:, columns]

    low, high = slice(0, half), slice(half, 2 * half)
    top = jnp.where(keep, tile(low, low), 0.0).astype(BF16)
    side = tile(high, low).astype(BF16)
    end = jnp.where(keep, tile(high, high), 0.0).astype(BF16)
    return top, jnp.concatenate([side, end], axis=1)


def mix(pairs, values, half):
    top, bottom = pairs
    return jnp.concatenate([dot(top, values[:half], NN), dot(bottom, values, NN)], axis=0)


def mix_back(pairs, values, half):
    top, bottom = pairs
    low = dot(top, values[:half], TN)
    both = dot(bottom, values[half:], TN)
    return jnp.concatenate([low + both[:half], both[half:]], axis=0)


def deal(quarter, held, outs):
    for slot in range(GROUP):
        outs[slot][...] = held[band(group_member() ^ slot, quarter), :]


def local_state_kernel(heads, quarter, exponent_hbm, q_hbm, k_hbm, v_hbm, grad_hbm, *rest):
    outs, rest = rest[:GROUP], rest[GROUP:]
    rates_ref, q_ref, k_ref, v_ref, late_ref, grad_ref, held, exponent_ref, sems, later = rest
    rows = k_ref.shape[0]
    width = k_ref.shape[1] // heads
    exponents = pltpu.make_async_copy(exponent_hbm, exponent_ref, later.at[2])
    exponents.start()
    loads = []
    chunks = sems.shape[1]
    for chunk in range(chunks):
        cols = slice(chunk * heads // chunks * width, (chunk + 1) * heads // chunks * width)
        loads.append(
            [
                pltpu.make_async_copy(source.at[:, cols], target.at[:, cols], sems.at[n, chunk])
                for n, (source, target) in enumerate(((k_hbm, k_ref), (v_hbm, v_ref)))
            ]
        )
        for load in loads[-1]:
            load.start()
    moves = [
        pltpu.make_async_copy(q_hbm, q_ref, later.at[0]),
        pltpu.make_async_copy(grad_hbm, grad_ref, later.at[1]),
    ]
    for move in moves:
        move.start()
    exponents.wait()
    for h in range(heads):
        spread = jnp.full((8, 128), exponent_ref[h].astype(F32))
        rates_ref[8 * h : 8 * h + 8, :] = jnp.log1p(-jnp.exp2(-spread))
    for h in range(heads):
        if h % (heads // chunks) == 0:
            for load in loads[h * chunks // heads]:
                load.wait()
        cols = slice(h * width, (h + 1) * width)
        k = (k_ref[:, cols].astype(F32) * key_decay(head_rate(rates_ref, h), rows, width)).astype(BF16)
        late_ref[:, cols] = k
        held[cols, :] = dot(k, v_ref[:, cols], TN).astype(BF16)
    deal(quarter, held, outs)
    for move in moves:
        move.wait()


def owned_parts(member, heads, width):
    per = -(-heads // GROUP)
    for j in range(per):
        if member * per + j < heads:
            yield slice(j * width, (j + 1) * width), member * per + j


def total_kernel(order, rows, heads, rates_ref, *rest):
    pieces, out_ref = [rest[SENT.index(s)] for s in range(GROUP)], rest[GROUP]
    width = out_ref.shape[1]
    for me in range(GROUP):

        @pl.when(group_member() == me)
        def _():
            for part, head in owned_parts(me, heads, width):
                decay = jnp.exp(rows * head_rate(rates_ref, head))
                total = None
                for m in order:
                    state = pieces[m ^ me][part, :].astype(F32)
                    total = state if total is None else total * decay + state
                out_ref[part, :] = total.astype(BF16)


def spread_kernel(order, rows, heads, groups, reverse, rates_ref, carry_ref, *rest):
    pieces, outs = [rest[SENT.index(s)] for s in range(GROUP)], rest[GROUP:]
    width = outs[0].shape[1]
    group = lax.axis_index("ctx") // GROUP
    first = group == (groups - 1 if reverse else 0)
    for me in range(GROUP):

        @pl.when(group_member() == me)
        def _():
            for part, head in owned_parts(me, heads, width):
                decay = jnp.exp(rows * head_rate(rates_ref, head))
                state = jnp.where(first, 0.0, carry_ref[part, :].astype(F32))
                for n, m in enumerate(order):
                    outs[m ^ me][part, :] = state.astype(BF16)
                    if n + 1 < GROUP:
                        state = state * decay + pieces[m ^ me][part, :].astype(F32)


def within_kernel(heads, rates_ref, q_ref, k_ref, v_ref, out_ref, early_ref, late_ref, top_ref, bottom_ref):
    rows, width = q_ref.shape[0], q_ref.shape[1] // heads
    half = rows // 2
    for h in range(heads):
        cols = slice(h * width, (h + 1) * width)
        held = slice(h * half, (h + 1) * half)
        rate = head_rate(rates_ref, h)
        upto = query_decay(rate, rows, half)
        q, v = q_ref[:, cols], v_ref[:, cols]
        early_ref[:, cols] = (q.astype(F32) * upto).astype(BF16)
        late_ref[:, cols] = (v.astype(F32) * key_decay(rate, rows, width)).astype(BF16)
        weights = decayed_pairs(q, k_ref[:, cols], upto, since_decay(rate, rows), half)
        top_ref[held, :], bottom_ref[held, :] = weights
        out_ref[:, cols] = mix(weights, v, half)


def project_rows(slots, heads, width, pieces, weight_ref, cot_ref):
    count = len(pieces)
    rows = pieces[0].shape[0]
    per = -(-heads // GROUP)
    taken = per if heads % GROUP == 0 else 1
    tile = taken * width
    index = lax.axis_index("head")
    core, line = index % 2, index // 2

    def one(step, head):
        whole = jnp.concatenate([p[...] for p in pieces], axis=0)
        total = dot(weight_ref[band(head // taken, tile), :], whole, NT).astype(BF16).T
        for n in range(count):
            place = ((line + n // 2) % (count // 2)) * 2 + (core ^ (n % 2))
            cot_ref[band(place, rows), slice(step * tile, (step + 1) * tile)] = total[n * rows : (n + 1) * rows, :]

    for step in range(len(slots) * per // taken):
        head = (group_member() ^ slots[step * taken // per]) * per + step * taken % per
        if heads % GROUP == 0:
            one(step, head)
        else:
            pl.when(head < heads)(functools.partial(one, step, head))


def turn_heads(slots, heads, early_ref, attended_ref, cot_ref, states, outs, dout_ref):
    width = early_ref.shape[1] // heads
    per = -(-heads // GROUP)

    @slot_heads(slots, heads)
    def two(n, head):
        cols = slice(n * width, (n + 1) * width)
        part = slice(n % per * width, (n % per + 1) * width)
        q = early_ref[:, band(head, width)]
        attended = attended_ref[:, band(head, width)] + dot(q, states[n // per][part, :], NN)
        inverse = lax.rsqrt(jnp.mean(attended * attended, axis=-1, keepdims=True) + EPSILON)
        normed = attended * inverse
        cot = cot_ref[:, cols].astype(F32)
        dout = ((cot - normed * jnp.mean(cot * normed, axis=-1, keepdims=True)) * inverse).astype(BF16)
        dout_ref[:, cols] = dout
        outs[n // per][part, :] = dot(q, dout, TN).astype(BF16)


def project_kernel(slots, heads, width, *refs):
    project_rows(slots, heads, width, refs[:-2], refs[-2], refs[-1])


def turn_kernel(slots, heads, early_ref, attended_ref, cot_ref, *refs):
    states, outs, dout_ref = refs[: len(slots)], refs[len(slots) : -1], refs[-1]
    turn_heads(slots, heads, early_ref, attended_ref, cot_ref, states, outs, dout_ref)


def turn_own_kernel(heads, width, early_ref, attended_ref, state_ref, *refs):
    pieces, (weight_ref, out_ref, dout_ref, cot_ref) = refs[:-4], refs[-4:]
    project_rows([0], heads, width, pieces, weight_ref, cot_ref)
    turn_heads([0], heads, early_ref, attended_ref, cot_ref, [state_ref], [out_ref], dout_ref)


def slot_columns(own_ref, rest_ref, n, width):
    at = n * width
    wide = own_ref.shape[1]
    return own_ref[:, at : at + width] if at < wide else rest_ref[:, at - wide : at - wide + width]


def value_grads_kernel(heads, top_ref, bottom_ref, own_ref, rest_ref, gv_ref):
    half = top_ref.shape[1]
    width = own_ref.shape[1] // -(-heads // GROUP)

    @slot_heads(SENT, heads)
    def one(n, head):
        weights = top_ref[band(head, half), :], bottom_ref[band(head, half), :]
        gv_ref[:, n * width : (n + 1) * width] = mix_back(weights, slot_columns(own_ref, rest_ref, n, width), half)


def key_grads_kernel(heads, rates_ref, q_ref, v_ref, own_ref, rest_ref, gk_ref, top_ref, bottom_ref):
    rows, width = q_ref.shape[0], q_ref.shape[1] // heads
    half = rows // 2

    @slot_heads(SENT, heads)
    def one(n, head):
        held = slice(n * half, (n + 1) * half)
        rate = head_rate(rates_ref, head)
        upto = query_decay(rate, rows, half)
        dout = slot_columns(own_ref, rest_ref, n, width)
        dweights = decayed_pairs(dout, v_ref[:, band(head, width)], upto, since_decay(rate, rows), half)
        top_ref[held, :], bottom_ref[held, :] = dweights
        gk_ref[:, n * width : (n + 1) * width] = mix_back(dweights, q_ref[:, band(head, width)], half)


def query_grads_kernel(heads, rates_ref, k_ref, top_ref, bottom_ref, own_ref, rest_ref, *rest):
    states, gq_ref = rest[:GROUP], rest[GROUP]
    rows, width = k_ref.shape[0], k_ref.shape[1] // heads
    half = rows // 2
    per = -(-heads // GROUP)

    @slot_heads(SENT, heads)
    def one(n, head):
        held = slice(n * half, (n + 1) * half)
        dout = slot_columns(own_ref, rest_ref, n, width)
        late = (dout.astype(F32) * query_decay(head_rate(rates_ref, head), rows, width)).astype(BF16)
        state = states[n // per][n % per * width : (n % per + 1) * width, :]
        gq = mix((top_ref[held, :], bottom_ref[held, :]), k_ref[:, band(head, width)], half) + dot(late, state, NT)
        gq_ref[:, band(head, width)] = gq.astype(BF16)


def finish_kernel(slots, heads, taken_over, late_keys, late_values, gk_in, gv_in, *rest):
    backs, rest = rest[: len(slots)], rest[len(slots) + taken_over :]
    gk_hbm, gv_hbm, gk_ref, gv_ref, sems = rest
    per = -(-heads // GROUP)
    width = late_keys.shape[1] // heads

    def stores(n, head):
        cols = slice(n * width, (n + 1) * width)
        for side, (source, target) in enumerate(((gk_ref, gk_hbm), (gv_ref, gv_hbm))):
            yield pltpu.make_async_copy(source.at[:, cols], target.at[:, band(head, width)], sems.at[side, n])

    @slot_heads(slots, heads)
    def one(n, head):
        cols = slice(n * width, (n + 1) * width)
        at = (SENT.index(slots[n // per]) * per + n % per) * width
        back = backs[n // per][n % per * width : (n % per + 1) * width, :]
        gk = gk_in[:, at : at + width] + dot(late_values[:, band(head, width)], back, NT)
        gv = gv_in[:, at : at + width] + dot(late_keys[:, band(head, width)], back, NN)
        gk_ref[:, cols] = gk.astype(BF16)
        gv_ref[:, cols] = gv.astype(BF16)
        for store in stores(n, head):
            store.start()

    @slot_heads(slots, heads)
    def two(n, head):
        for store in stores(n, head):
            store.wait()


def swaps(pieces, axis, count):
    return {s: lax.ppermute(pieces[s], axis, [(i, i ^ s) for i in range(count)]) for s in range(1, GROUP)}


def add_up(got, rates, rows, heads, reverse):
    order = list(reversed(range(GROUP))) if reverse else list(range(GROUP))
    kernel = functools.partial(total_kernel, order, rows, heads)
    return call(kernel, [jax.ShapeDtypeStruct(got[0].shape, BF16)], [PLAIN] * (1 + GROUP), limit=4)(
        rates, *[got[s] for s in SENT]
    )[0]


def from_groups(total, rates, rows, heads, axis, count, reverse):
    groups = count // GROUP

    def shift(x, by):
        step = -by if reverse else by
        return lax.ppermute(x, axis, [(i, (i + step * GROUP) % count) for i in range(count)])

    carry = total
    if groups > 1:
        carry = shift(total, 1)
        span = 1
        while span < groups - 1:
            carry = widen(carry, shift(carry, span), rates, rows, heads, groups, span, reverse)
            span *= 2
    return carry


def spread_out(carry, got, rates, rows, heads, count, reverse):
    order = list(reversed(range(GROUP))) if reverse else list(range(GROUP))
    kernel = functools.partial(spread_kernel, order, rows, heads, count // GROUP, reverse)
    piece = jax.ShapeDtypeStruct(carry.shape, BF16)
    return call(kernel, [piece] * GROUP, [PLAIN] * (2 + GROUP), limit=4)(rates, carry, *[got[s] for s in SENT])


def widen_kernel(rows, heads, groups, span, reverse, rates_ref, near_ref, far_ref, out_ref):
    width = out_ref.shape[1]
    group = lax.axis_index("ctx") // GROUP
    reached = group + span + 1 <= groups - 1 if reverse else group >= span + 1
    for me in range(GROUP):

        @pl.when(group_member() == me)
        def _():
            for part, head in owned_parts(me, heads, width):
                decay = jnp.exp(GROUP * rows * span * head_rate(rates_ref, head))
                far = jnp.where(reached, far_ref[part, :].astype(F32), 0.0)
                out_ref[part, :] = (near_ref[part, :].astype(F32) + decay * far).astype(BF16)


def widen(near, far, rates, rows, heads, groups, span, reverse):
    kernel = functools.partial(widen_kernel, rows, heads, groups, span, reverse)
    return call(kernel, [jax.ShapeDtypeStruct(near.shape, BF16)], [PLAIN] * 3, limit=4)(rates, near, far)[0]


def gather_lines(x, axis, count):
    lines = count // 2
    return [lax.ppermute(x, axis, [(i, (i - 2 * s) % count) for i in range(count)]) for s in range(1, lines)]


def flipped(x, axis, count):
    return lax.ppermute(x, axis, [(i, i ^ 1) for i in range(count)])


def after(x, *others):
    return lax.optimization_barrier((x, others))[0]


def body(ctx_count, head_count, query, key_in, value, out_weight, grad_layer, decay_exp):
    rows, flat = query.shape
    heads = decay_exp.shape[0]
    width = flat // heads
    per = -(-heads // GROUP)
    quarter = per * width
    half = rows // 2
    rest = list(SENT[1:])

    def shaped(*shape, dtype=BF16):
        return jax.ShapeDtypeStruct(shape, dtype)

    piece = shaped(quarter, width)
    whole_rows = shaped(rows, flat)
    slot_sums = shaped(rows, GROUP * quarter, dtype=F32)

    moved = gather_lines(grad_layer, "head", head_count)
    made = call(
        functools.partial(local_state_kernel, heads, quarter),
        [piece] * GROUP
        + [shaped(8 * heads, 128, dtype=F32)]
        + [whole_rows] * 4
        + [shaped(*grad_layer.shape)],
        [STREAM] * 5,
        [
            pltpu.VMEM((GROUP * quarter, width), BF16),
            pltpu.SMEM((heads,), jnp.int32),
            pltpu.SemaphoreType.DMA((2, max(n for n in (1, 2, 3, 4) if heads % n == 0))),
            pltpu.SemaphoreType.DMA((3,)),
        ],
        work=3 * 10**9,
    )(decay_exp, query, key_in, value, grad_layer)
    pieces = made[:GROUP]
    rates, query, key_in, value, late_keys, own = made[GROUP:]

    got = {0: pieces[0], **swaps(pieces, "ctx", ctx_count)}
    inner = call(
        functools.partial(within_kernel, heads),
        [shaped(rows, flat, dtype=F32), whole_rows, whole_rows, shaped(heads * half, half), shaped(heads * half, rows)],
        [PLAIN] * 4,
        work=3 * 10**9,
    )(rates, query, key_in, value)
    got = dict(zip(SENT, after([got[s] for s in SENT], *inner)))
    attended, early_queries, late_values, top, bottom = inner
    total = add_up(got, rates, rows, heads, False)
    carry = from_groups(total, rates, rows, heads, "ctx", ctx_count, False)
    slots = [own, flipped(after(own, total), "head", head_count)]
    for x in moved:
        x = after(x, carry)
        slots += [x, flipped(x, "head", head_count)]
    ready = spread_out(carry, got, rates, rows, heads, ctx_count, False)
    states = {0: ready[0], **swaps(ready, "ctx", ctx_count)}

    def projected(which, slots):
        kernel = functools.partial(project_kernel, which, heads, width)
        return call(kernel, [shaped(rows, len(which) * quarter)], [PLAIN] * (head_count + 1))(*slots, out_weight)[0]

    slots[-1] = after(slots[-1], ready)
    cot = projected(rest, slots)
    made = call(functools.partial(turn_kernel, rest, heads), [piece] * 3 + [shaped(rows, 3 * quarter)], [PLAIN] * 6)(
        early_queries, attended, cot, *[states[s] for s in rest]
    )
    pieces, dout_rest = dict(zip(rest, made)), made[-1]
    got = swaps(pieces, "ctx", ctx_count)
    mine, dout_own = call(
        functools.partial(turn_own_kernel, heads, width),
        [piece, shaped(rows, quarter)],
        [PLAIN] * (head_count + 4),
        [pltpu.VMEM((rows, quarter), BF16)],
    )(after(early_queries, dout_rest), attended, states[0], *slots, out_weight)
    (value_part,) = call(functools.partial(value_grads_kernel, heads), [slot_sums], [PLAIN] * 4)(
        top, bottom, dout_own, dout_rest
    )
    got = dict(zip(SENT, after([{0: mine, **got}[s] for s in SENT], value_part)))
    total = add_up(got, rates, rows, heads, True)
    carry = from_groups(total, rates, rows, heads, "ctx", ctx_count, True)
    key_part, top, bottom = call(
        functools.partial(key_grads_kernel, heads),
        [slot_sums, shaped(GROUP * per * half, half), shaped(GROUP * per * half, rows)],
        [PLAIN] * 5,
    )(rates, query, after(value, total), dout_own, dout_rest)
    ready = spread_out(after(carry, key_part), got, rates, rows, heads, ctx_count, True)
    back = {0: ready[0], **swaps(ready, "ctx", ctx_count)}
    (grad_query,) = call(functools.partial(query_grads_kernel, heads), [whole_rows], [PLAIN] * (6 + GROUP))(
        rates, after(key_in, ready[0]), top, bottom, dout_own, dout_rest, *[states[s] for s in SENT]
    )
    early_slots, late_slots = [0, 1], [3, 2]
    sums = [late_keys, late_values, key_part, value_part]
    grads = []
    for which, pieces in ((early_slots, [back[0], after(back[1], grad_query)]), (late_slots, None)):
        if pieces is None:
            pieces = after([back[s] for s in which], *grads)
        held = pltpu.VMEM((rows, 2 * quarter), BF16)
        grads = call(
            functools.partial(finish_kernel, which, heads, len(grads)),
            [whole_rows] * 2,
            [PLAIN] * 6 + [STREAM] * len(grads),
            [held, held, pltpu.SemaphoreType.DMA((2, 2 * per))],
            out_specs=[STREAM] * 2,
            aliases={6 + n: n for n in range(len(grads))},
        )(*sums, *pieces, *grads)
    grad_key, grad_value = grads
    return grad_query, grad_key, grad_value


def solution(mesh):
    return jax.shard_map(
        functools.partial(body, mesh.shape["ctx"], mesh.shape["head"]),
        mesh=mesh,
        in_specs=(
            P("ctx", "head"),
            P("ctx", "head"),
            P("ctx", "head"),
            P("head", None),
            P(("ctx", "head"), None),
            P("head"),
        ),
        out_specs=(P("ctx", "head"), P("ctx", "head"), P("ctx", "head")),
        check_vma=False,
    )
```

```python
import functools

import jax
import jax.numpy as jnp
from jax import lax
from jax.experimental import pallas as pl
from jax.experimental.pallas import tpu as pltpu
from jax.sharding import PartitionSpec as P

EPSILON = 1e-06
GROUP = 4
SENT = (0, 3, 1, 2)
BF16 = jnp.bfloat16
F32 = jnp.float32

PLAIN = pl.BlockSpec(memory_space=pltpu.VMEM)
STREAM = pl.BlockSpec(memory_space=pltpu.HBM)


def call(kernel, outs, in_specs, scratch=(), limit=8, work=1, out_specs=None, aliases=None):
    made = pl.pallas_call(
        kernel,
        out_shape=outs,
        in_specs=in_specs,
        out_specs=out_specs or [PLAIN] * len(outs),
        scratch_shapes=list(scratch),
        input_output_aliases=aliases or {},
        compiler_params=pltpu.CompilerParams(vmem_limit_bytes=limit * 2**20),
        cost_estimate=pl.CostEstimate(flops=work, bytes_accessed=1, transcendentals=0),
    )

    def run(*operands):
        held = [
            pltpu.with_memory_space_constraint(x, pltpu.HBM) if spec is STREAM else x
            for x, spec in zip(operands, in_specs)
        ]
        return made(*held)

    return run


def dot(a, b, dims):
    return lax.dot_general(a, b, (dims, ((), ())), preferred_element_type=F32)


NN = ((1,), (0,))
NT = ((1,), (1,))
TN = ((0,), (0,))


def steps_from(rows, width, axis, start, turn):
    place = lax.broadcasted_iota(jnp.int32, (rows, width), axis)
    return (start + turn * place).astype(F32)


def query_decay(rate, rows, width):
    return jnp.exp(steps_from(rows, width, 0, 1, 1) * rate)


def key_decay(rate, rows, width):
    return jnp.exp(steps_from(rows, width, 0, rows - 1, -1) * rate)


def since_decay(rate, rows):
    return jnp.exp(steps_from(8, rows, 1, -1, -1) * rate)[0:1]


def head_rate(rates_ref, head):
    return rates_ref[band(head, 8), :][0:1, 0:1]


def band(place, size):
    return pl.ds(pl.multiple_of(place * size, size), size)


def slot_heads(slots, heads):
    per = -(-heads // GROUP)

    def visit(one):
        for n, slot in enumerate(slots):
            for j in range(per):
                head = (group_member() ^ slot) * per + j
                if heads % GROUP == 0:
                    one(n * per + j, head)
                else:
                    pl.when(head < heads)(functools.partial(one, n * per + j, head))

    return visit


def group_member():
    return lax.axis_index("ctx") % GROUP


def decayed_pairs(left, right, upto, since, half):
    keep = steps_from(half, half, 0, 0, 1) >= steps_from(half, half, 1, 0, 1)

    def tile(rows, columns):
        pair = dot(left[rows], right[columns], NT)
        return pair * upto[rows, :half] * since[:, columns]

    low, high = slice(0, half), slice(half, 2 * half)
    top = jnp.where(keep, tile(low, low), 0.0).astype(BF16)
    side = tile(high, low).astype(BF16)
    end = jnp.where(keep, tile(high, high), 0.0).astype(BF16)
    return top, jnp.concatenate([side, end], axis=1)


def mix(pairs, values, half):
    top, bottom = pairs
    return jnp.concatenate([dot(top, values[:half], NN), dot(bottom, values, NN)], axis=0)


def mix_back(pairs, values, half):
    top, bottom = pairs
    low = dot(top, values[:half], TN)
    both = dot(bottom, values[half:], TN)
    return jnp.concatenate([low + both[:half], both[half:]], axis=0)


def deal(quarter, held, outs):
    for slot in range(GROUP):
        outs[slot][...] = held[band(group_member() ^ slot, quarter), :]


def local_state_kernel(heads, quarter, exponent_hbm, q_hbm, k_hbm, v_hbm, grad_hbm, *rest):
    outs, rest = rest[:GROUP], rest[GROUP:]
    rates_ref, q_ref, k_ref, v_ref, late_ref, grad_ref, held, decay_ref, exponent_ref, sems, later = rest
    rows = k_ref.shape[0]
    width = k_ref.shape[1] // heads
    exponents = pltpu.make_async_copy(exponent_hbm, exponent_ref, later.at[2])
    exponents.start()
    loads = []
    chunks = sems.shape[1]
    for chunk in range(chunks):
        cols = slice(chunk * heads // chunks * width, (chunk + 1) * heads // chunks * width)
        loads.append(
            [
                pltpu.make_async_copy(source.at[:, cols], target.at[:, cols], sems.at[n, chunk])
                for n, (source, target) in enumerate(((k_hbm, k_ref), (v_hbm, v_ref)))
            ]
        )
        for load in loads[-1]:
            load.start()
    moves = [
        pltpu.make_async_copy(q_hbm, q_ref, later.at[0]),
        pltpu.make_async_copy(grad_hbm, grad_ref, later.at[1]),
    ]
    for move in moves:
        move.start()
    exponents.wait()
    for h in range(heads):
        spread = jnp.full((8, 128), exponent_ref[h].astype(F32))
        rates_ref[8 * h : 8 * h + 8, :] = jnp.log1p(-jnp.exp2(-spread))
        decay_ref[:, h * width : (h + 1) * width] = key_decay(head_rate(rates_ref, h), rows, width)
    for h in range(heads):
        if h % (heads // chunks) == 0:
            for load in loads[h * chunks // heads]:
                load.wait()
        cols = slice(h * width, (h + 1) * width)
        k = (k_ref[:, cols].astype(F32) * decay_ref[:, cols]).astype(BF16)
        late_ref[:, cols] = k
        held[cols, :] = dot(k, v_ref[:, cols], TN).astype(BF16)
    deal(quarter, held, outs)
    for move in moves:
        move.wait()


def owned_parts(member, heads, width):
    per = -(-heads // GROUP)
    for j in range(per):
        if member * per + j < heads:
            yield slice(j * width, (j + 1) * width), member * per + j


def total_kernel(order, rows, heads, rates_ref, *rest):
    pieces, out_ref = [rest[SENT.index(s)] for s in range(GROUP)], rest[GROUP]
    width = out_ref.shape[1]
    for me in range(GROUP):

        @pl.when(group_member() == me)
        def _():
            for part, head in owned_parts(me, heads, width):
                decay = jnp.exp(rows * head_rate(rates_ref, head))
                total = None
                for m in order:
                    state = pieces[m ^ me][part, :].astype(F32)
                    total = state if total is None else total * decay + state
                out_ref[part, :] = total.astype(BF16)


def spread_kernel(order, rows, heads, groups, reverse, rates_ref, carry_ref, *rest):
    pieces, outs = [rest[SENT.index(s)] for s in range(GROUP)], rest[GROUP:]
    width = outs[0].shape[1]
    group = lax.axis_index("ctx") // GROUP
    first = group == (groups - 1 if reverse else 0)
    for me in range(GROUP):

        @pl.when(group_member() == me)
        def _():
            for part, head in owned_parts(me, heads, width):
                decay = jnp.exp(rows * head_rate(rates_ref, head))
                state = jnp.where(first, 0.0, carry_ref[part, :].astype(F32))
                for n, m in enumerate(order):
                    outs[m ^ me][part, :] = state.astype(BF16)
                    if n + 1 < GROUP:
                        state = state * decay + pieces[m ^ me][part, :].astype(F32)


def within_kernel(heads, rates_ref, q_ref, k_ref, v_ref, out_ref, early_ref, late_ref, top_ref, bottom_ref):
    rows, width = q_ref.shape[0], q_ref.shape[1] // heads
    half = rows // 2
    for h in range(heads):
        cols = slice(h * width, (h + 1) * width)
        held = slice(h * half, (h + 1) * half)
        rate = head_rate(rates_ref, h)
        upto = query_decay(rate, rows, half)
        q, v = q_ref[:, cols], v_ref[:, cols]
        early_ref[:, cols] = (q.astype(F32) * upto).astype(BF16)
        late_ref[:, cols] = (v.astype(F32) * key_decay(rate, rows, width)).astype(BF16)
        weights = decayed_pairs(q, k_ref[:, cols], upto, since_decay(rate, rows), half)
        top_ref[held, :], bottom_ref[held, :] = weights
        out_ref[:, cols] = mix(weights, v, half)


def project_rows(slots, heads, width, pieces, weight_ref, cot_ref):
    count = len(pieces)
    rows = pieces[0].shape[0]
    per = -(-heads // GROUP)
    taken = per if heads % GROUP == 0 else 1
    tile = taken * width
    index = lax.axis_index("head")
    core, line = index % 2, index // 2

    def one(step, head):
        whole = jnp.concatenate([p[...] for p in pieces], axis=0)
        total = dot(weight_ref[band(head // taken, tile), :], whole, NT).astype(BF16).T
        for n in range(count):
            place = ((line + n // 2) % (count // 2)) * 2 + (core ^ (n % 2))
            cot_ref[band(place, rows), slice(step * tile, (step + 1) * tile)] = total[n * rows : (n + 1) * rows, :]

    for step in range(len(slots) * per // taken):
        head = (group_member() ^ slots[step * taken // per]) * per + step * taken % per
        if heads % GROUP == 0:
            one(step, head)
        else:
            pl.when(head < heads)(functools.partial(one, step, head))


def turn_heads(slots, heads, early_ref, attended_ref, cot_ref, states, outs, dout_ref):
    width = early_ref.shape[1] // heads
    per = -(-heads // GROUP)

    @slot_heads(slots, heads)
    def two(n, head):
        cols = slice(n * width, (n + 1) * width)
        part = slice(n % per * width, (n % per + 1) * width)
        q = early_ref[:, band(head, width)]
        attended = attended_ref[:, band(head, width)] + dot(q, states[n // per][part, :], NN)
        cot = cot_ref[:, cols].astype(F32)
        squares = jnp.mean(attended * attended, axis=-1, keepdims=True)
        shared = jnp.mean(cot * attended, axis=-1, keepdims=True)
        inverse = lax.rsqrt(squares + EPSILON)
        dout = ((cot - attended * (shared * inverse * inverse)) * inverse).astype(BF16)
        dout_ref[:, cols] = dout
        outs[n // per][part, :] = dot(q, dout, TN).astype(BF16)


def project_kernel(slots, heads, width, *refs):
    project_rows(slots, heads, width, refs[:-2], refs[-2], refs[-1])


def turn_kernel(slots, heads, early_ref, attended_ref, cot_ref, *refs):
    states, outs, dout_ref = refs[: len(slots)], refs[len(slots) : -1], refs[-1]
    turn_heads(slots, heads, early_ref, attended_ref, cot_ref, states, outs, dout_ref)


def turn_own_kernel(heads, width, early_ref, attended_ref, state_ref, *refs):
    pieces, (weight_ref, out_ref, dout_ref, cot_ref) = refs[:-4], refs[-4:]
    project_rows([0], heads, width, pieces, weight_ref, cot_ref)
    turn_heads([0], heads, early_ref, attended_ref, cot_ref, [state_ref], [out_ref], dout_ref)


def slot_columns(own_ref, rest_ref, n, width):
    at = n * width
    wide = own_ref.shape[1]
    return own_ref[:, at : at + width] if at < wide else rest_ref[:, at - wide : at - wide + width]


def value_grads_kernel(heads, top_ref, bottom_ref, own_ref, rest_ref, gv_ref):
    half = top_ref.shape[1]
    width = own_ref.shape[1] // -(-heads // GROUP)

    @slot_heads(SENT, heads)
    def one(n, head):
        weights = top_ref[band(head, half), :], bottom_ref[band(head, half), :]
        gv_ref[:, n * width : (n + 1) * width] = mix_back(weights, slot_columns(own_ref, rest_ref, n, width), half)


def key_grads_kernel(heads, rates_ref, q_ref, v_ref, own_ref, rest_ref, gk_ref, top_ref, bottom_ref):
    rows, width = q_ref.shape[0], q_ref.shape[1] // heads
    half = rows // 2

    @slot_heads(SENT, heads)
    def one(n, head):
        held = slice(n * half, (n + 1) * half)
        rate = head_rate(rates_ref, head)
        upto = query_decay(rate, rows, half)
        dout = slot_columns(own_ref, rest_ref, n, width)
        dweights = decayed_pairs(dout, v_ref[:, band(head, width)], upto, since_decay(rate, rows), half)
        top_ref[held, :], bottom_ref[held, :] = dweights
        gk_ref[:, n * width : (n + 1) * width] = mix_back(dweights, q_ref[:, band(head, width)], half)


def query_grads_kernel(heads, rates_ref, k_ref, top_ref, bottom_ref, own_ref, rest_ref, *rest):
    states, gq_ref = rest[:GROUP], rest[GROUP]
    rows, width = k_ref.shape[0], k_ref.shape[1] // heads
    half = rows // 2
    per = -(-heads // GROUP)

    @slot_heads(SENT, heads)
    def one(n, head):
        held = slice(n * half, (n + 1) * half)
        dout = slot_columns(own_ref, rest_ref, n, width)
        late = (dout.astype(F32) * query_decay(head_rate(rates_ref, head), rows, width)).astype(BF16)
        state = states[n // per][n % per * width : (n % per + 1) * width, :]
        gq = mix((top_ref[held, :], bottom_ref[held, :]), k_ref[:, band(head, width)], half) + dot(late, state, NT)
        gq_ref[:, band(head, width)] = gq.astype(BF16)


def finish_kernel(slots, heads, taken_over, late_keys, late_values, gk_in, gv_in, *rest):
    backs, rest = rest[: len(slots)], rest[len(slots) + taken_over :]
    gk_hbm, gv_hbm, gk_ref, gv_ref, sems = rest
    per = -(-heads // GROUP)
    width = late_keys.shape[1] // heads

    def stores(n, head):
        cols = slice(n * width, (n + 1) * width)
        for side, (source, target) in enumerate(((gk_ref, gk_hbm), (gv_ref, gv_hbm))):
            yield pltpu.make_async_copy(source.at[:, cols], target.at[:, band(head, width)], sems.at[side, n])

    @slot_heads(slots, heads)
    def one(n, head):
        cols = slice(n * width, (n + 1) * width)
        at = (SENT.index(slots[n // per]) * per + n % per) * width
        back = backs[n // per][n % per * width : (n % per + 1) * width, :]
        gk = gk_in[:, at : at + width] + dot(late_values[:, band(head, width)], back, NT)
        gv = gv_in[:, at : at + width] + dot(late_keys[:, band(head, width)], back, NN)
        gk_ref[:, cols] = gk.astype(BF16)
        gv_ref[:, cols] = gv.astype(BF16)
        for store in stores(n, head):
            store.start()

    @slot_heads(slots, heads)
    def two(n, head):
        for store in stores(n, head):
            store.wait()


def swaps(pieces, axis, count):
    return {s: lax.ppermute(pieces[s], axis, [(i, i ^ s) for i in range(count)]) for s in range(1, GROUP)}


def add_up(got, rates, rows, heads, reverse):
    order = list(reversed(range(GROUP))) if reverse else list(range(GROUP))
    kernel = functools.partial(total_kernel, order, rows, heads)
    return call(kernel, [jax.ShapeDtypeStruct(got[0].shape, BF16)], [PLAIN] * (1 + GROUP), limit=4)(
        rates, *[got[s] for s in SENT]
    )[0]


def from_groups(total, rates, rows, heads, axis, count, reverse):
    groups = count // GROUP

    def shift(x, by):
        step = -by if reverse else by
        return lax.ppermute(x, axis, [(i, (i + step * GROUP) % count) for i in range(count)])

    carry = total
    if groups > 1:
        carry = shift(total, 1)
        span = 1
        while span < groups - 1:
            carry = widen(carry, shift(carry, span), rates, rows, heads, groups, span, reverse)
            span *= 2
    return carry


def spread_out(carry, got, rates, rows, heads, count, reverse):
    order = list(reversed(range(GROUP))) if reverse else list(range(GROUP))
    kernel = functools.partial(spread_kernel, order, rows, heads, count // GROUP, reverse)
    piece = jax.ShapeDtypeStruct(carry.shape, BF16)
    return call(kernel, [piece] * GROUP, [PLAIN] * (2 + GROUP), limit=4)(rates, carry, *[got[s] for s in SENT])


def widen_kernel(rows, heads, groups, span, reverse, rates_ref, near_ref, far_ref, out_ref):
    width = out_ref.shape[1]
    group = lax.axis_index("ctx") // GROUP
    reached = group + span + 1 <= groups - 1 if reverse else group >= span + 1
    for me in range(GROUP):

        @pl.when(group_member() == me)
        def _():
            for part, head in owned_parts(me, heads, width):
                decay = jnp.exp(GROUP * rows * span * head_rate(rates_ref, head))
                far = jnp.where(reached, far_ref[part, :].astype(F32), 0.0)
                out_ref[part, :] = (near_ref[part, :].astype(F32) + decay * far).astype(BF16)


def widen(near, far, rates, rows, heads, groups, span, reverse):
    kernel = functools.partial(widen_kernel, rows, heads, groups, span, reverse)
    return call(kernel, [jax.ShapeDtypeStruct(near.shape, BF16)], [PLAIN] * 3, limit=4)(rates, near, far)[0]


def gather_lines(x, axis, count):
    lines = count // 2
    return [lax.ppermute(x, axis, [(i, (i - 2 * s) % count) for i in range(count)]) for s in range(1, lines)]


def flipped(x, axis, count):
    return lax.ppermute(x, axis, [(i, i ^ 1) for i in range(count)])


def after(x, *others):
    return lax.optimization_barrier((x, others))[0]


def body(ctx_count, head_count, query, key_in, value, out_weight, grad_layer, decay_exp):
    rows, flat = query.shape
    heads = decay_exp.shape[0]
    width = flat // heads
    per = -(-heads // GROUP)
    quarter = per * width
    half = rows // 2
    rest = list(SENT[1:])

    def shaped(*shape, dtype=BF16):
        return jax.ShapeDtypeStruct(shape, dtype)

    piece = shaped(quarter, width)
    whole_rows = shaped(rows, flat)
    slot_sums = shaped(rows, GROUP * quarter, dtype=F32)

    moved = gather_lines(grad_layer, "head", head_count)
    made = call(
        functools.partial(local_state_kernel, heads, quarter),
        [piece] * GROUP
        + [shaped(8 * heads, 128, dtype=F32)]
        + [whole_rows] * 4
        + [shaped(*grad_layer.shape)],
        [STREAM] * 5,
        [
            pltpu.VMEM((GROUP * quarter, width), BF16),
            pltpu.VMEM((rows, flat), F32),
            pltpu.SMEM((heads,), jnp.int32),
            pltpu.SemaphoreType.DMA((2, max(n for n in (1, 2, 3, 4) if heads % n == 0))),
            pltpu.SemaphoreType.DMA((3,)),
        ],
        work=3 * 10**9,
    )(decay_exp, query, key_in, value, grad_layer)
    pieces = made[:GROUP]
    rates, query, key_in, value, late_keys, own = made[GROUP:]

    got = {0: pieces[0], **swaps(pieces, "ctx", ctx_count)}
    inner = call(
        functools.partial(within_kernel, heads),
        [shaped(rows, flat, dtype=F32), whole_rows, whole_rows, shaped(heads * half, half), shaped(heads * half, rows)],
        [PLAIN] * 4,
        work=3 * 10**9,
    )(rates, query, key_in, value)
    got = dict(zip(SENT, after([got[s] for s in SENT], *inner)))
    attended, early_queries, late_values, top, bottom = inner
    total = add_up(got, rates, rows, heads, False)
    carry = from_groups(total, rates, rows, heads, "ctx", ctx_count, False)
    slots = [own, flipped(after(own, total), "head", head_count)]
    for x in moved:
        x = after(x, carry)
        slots += [x, flipped(x, "head", head_count)]
    ready = spread_out(carry, got, rates, rows, heads, ctx_count, False)
    states = {0: ready[0], **swaps(ready, "ctx", ctx_count)}

    def projected(which, slots):
        kernel = functools.partial(project_kernel, which, heads, width)
        return call(kernel, [shaped(rows, len(which) * quarter)], [PLAIN] * (head_count + 1))(*slots, out_weight)[0]

    slots[-1] = after(slots[-1], ready)
    cot = projected(rest, slots)
    made = call(functools.partial(turn_kernel, rest, heads), [piece] * 3 + [shaped(rows, 3 * quarter)], [PLAIN] * 6)(
        early_queries, attended, cot, *[states[s] for s in rest]
    )
    pieces, dout_rest = dict(zip(rest, made)), made[-1]
    got = swaps(pieces, "ctx", ctx_count)
    mine, dout_own = call(
        functools.partial(turn_own_kernel, heads, width),
        [piece, shaped(rows, quarter)],
        [PLAIN] * (head_count + 4),
        [pltpu.VMEM((rows, quarter), BF16)],
    )(after(early_queries, dout_rest), attended, states[0], *slots, out_weight)
    (value_part,) = call(functools.partial(value_grads_kernel, heads), [slot_sums], [PLAIN] * 4)(
        top, bottom, dout_own, dout_rest
    )
    got = dict(zip(SENT, after([{0: mine, **got}[s] for s in SENT], value_part)))
    total = add_up(got, rates, rows, heads, True)
    carry = from_groups(total, rates, rows, heads, "ctx", ctx_count, True)
    key_part, top, bottom = call(
        functools.partial(key_grads_kernel, heads),
        [slot_sums, shaped(GROUP * per * half, half), shaped(GROUP * per * half, rows)],
        [PLAIN] * 5,
    )(rates, query, after(value, total), dout_own, dout_rest)
    ready = spread_out(after(carry, key_part), got, rates, rows, heads, ctx_count, True)
    back = {0: ready[0], **swaps(ready, "ctx", ctx_count)}
    (grad_query,) = call(functools.partial(query_grads_kernel, heads), [whole_rows], [PLAIN] * (6 + GROUP))(
        rates, after(key_in, ready[0]), top, bottom, dout_own, dout_rest, *[states[s] for s in SENT]
    )
    early_slots, late_slots = [0, 3], [1, 2]
    sums = [late_keys, late_values, key_part, value_part]
    grads = []
    for which, pieces in ((early_slots, [back[0], after(back[early_slots[1]], grad_query)]), (late_slots, None)):
        if pieces is None:
            pieces = after([back[s] for s in which], *grads)
        held = pltpu.VMEM((rows, 2 * quarter), BF16)
        grads = call(
            functools.partial(finish_kernel, which, heads, len(grads)),
            [whole_rows] * 2,
            [PLAIN] * 6 + [STREAM] * len(grads),
            [held, held, pltpu.SemaphoreType.DMA((2, 2 * per))],
            out_specs=[STREAM] * 2,
            aliases={6 + n: n for n in range(len(grads))},
        )(*sums, *pieces, *grads)
    grad_key, grad_value = grads
    return grad_query, grad_key, grad_value


def solution(mesh):
    return jax.shard_map(
        functools.partial(body, mesh.shape["ctx"], mesh.shape["head"]),
        mesh=mesh,
        in_specs=(
            P("ctx", "head"),
            P("ctx", "head"),
            P("ctx", "head"),
            P("head", None),
            P(("ctx", "head"), None),
            P("head"),
        ),
        out_specs=(P("ctx", "head"), P("ctx", "head"), P("ctx", "head")),
        check_vma=False,
    )
```

```python
import functools

import jax
import jax.numpy as jnp
from jax import lax
from jax.experimental import pallas as pl
from jax.experimental.pallas import tpu as pltpu
from jax.sharding import PartitionSpec as P

EPSILON = 1e-06
GROUP = 4
SENT = (0, 1, 3, 2)
BF16 = jnp.bfloat16
F32 = jnp.float32

PLAIN = pl.BlockSpec(memory_space=pltpu.VMEM)
STREAM = pl.BlockSpec(memory_space=pltpu.HBM)


def call(kernel, outs, in_specs, scratch=(), limit=8, work=1, out_specs=None, aliases=None):
    made = pl.pallas_call(
        kernel,
        out_shape=outs,
        in_specs=in_specs,
        out_specs=out_specs or [PLAIN] * len(outs),
        scratch_shapes=list(scratch),
        input_output_aliases=aliases or {},
        compiler_params=pltpu.CompilerParams(vmem_limit_bytes=limit * 2**20),
        cost_estimate=pl.CostEstimate(flops=work, bytes_accessed=1, transcendentals=0),
    )

    def run(*operands):
        held = [
            pltpu.with_memory_space_constraint(x, pltpu.HBM) if spec is STREAM else x
            for x, spec in zip(operands, in_specs)
        ]
        return made(*held)

    return run


def dot(a, b, dims):
    return lax.dot_general(a, b, (dims, ((), ())), preferred_element_type=F32)


NN = ((1,), (0,))
NT = ((1,), (1,))
TN = ((0,), (0,))


def steps_from(rows, width, axis, start, turn):
    place = lax.broadcasted_iota(jnp.int32, (rows, width), axis)
    return (start + turn * place).astype(F32)


def query_decay(rate, rows, width):
    return jnp.exp(steps_from(rows, width, 0, 1, 1) * rate)


def key_decay(rate, rows, width):
    return jnp.exp(steps_from(rows, width, 0, rows - 1, -1) * rate)


def since_decay(rate, rows):
    return jnp.exp(steps_from(8, rows, 1, -1, -1) * rate)[0:1]


def head_rate(rates_ref, head):
    return rates_ref[band(head, 8), :][0:1, 0:1]


def band(place, size):
    return pl.ds(pl.multiple_of(place * size, size), size)


def slot_heads(slots, heads):
    per = -(-heads // GROUP)

    def visit(one):
        for n, slot in enumerate(slots):
            for j in range(per):
                head = (group_member() ^ slot) * per + j
                if heads % GROUP == 0:
                    one(n * per + j, head)
                else:
                    pl.when(head < heads)(functools.partial(one, n * per + j, head))

    return visit


def group_member():
    return lax.axis_index("ctx") % GROUP


def decayed_pairs(left, right, upto, since, half):
    keep = steps_from(half, half, 0, 0, 1) >= steps_from(half, half, 1, 0, 1)

    def tile(rows, columns):
        pair = dot(left[rows], right[columns], NT)
        return pair * upto[rows, :half] * since[:, columns]

    low, high = slice(0, half), slice(half, 2 * half)
    top = jnp.where(keep, tile(low, low), 0.0).astype(BF16)
    side = tile(high, low).astype(BF16)
    end = jnp.where(keep, tile(high, high), 0.0).astype(BF16)
    return top, jnp.concatenate([side, end], axis=1)


def mix(pairs, values, half):
    top, bottom = pairs
    return jnp.concatenate([dot(top, values[:half], NN), dot(bottom, values, NN)], axis=0)


def mix_back(pairs, values, half):
    top, bottom = pairs
    low = dot(top, values[:half], TN)
    both = dot(bottom, values[half:], TN)
    return jnp.concatenate([low + both[:half], both[half:]], axis=0)


def deal(quarter, held, outs):
    for slot in range(GROUP):
        outs[slot][...] = held[band(group_member() ^ slot, quarter), :]


def local_state_kernel(heads, quarter, exponent_hbm, q_hbm, k_hbm, v_hbm, grad_hbm, *rest):
    outs, rest = rest[:GROUP], rest[GROUP:]
    rates_ref, q_ref, k_ref, v_ref, late_ref, grad_ref, held, decay_ref, exponent_ref, sems, later = rest
    rows = k_ref.shape[0]
    width = k_ref.shape[1] // heads
    exponents = pltpu.make_async_copy(exponent_hbm, exponent_ref, later.at[2])
    exponents.start()
    loads = []
    chunks = sems.shape[1]
    for chunk in range(chunks):
        cols = slice(chunk * heads // chunks * width, (chunk + 1) * heads // chunks * width)
        loads.append(
            [
                pltpu.make_async_copy(source.at[:, cols], target.at[:, cols], sems.at[n, chunk])
                for n, (source, target) in enumerate(((k_hbm, k_ref), (v_hbm, v_ref)))
            ]
        )
        for load in loads[-1]:
            load.start()
    moves = [
        pltpu.make_async_copy(q_hbm, q_ref, later.at[0]),
        pltpu.make_async_copy(grad_hbm, grad_ref, later.at[1]),
    ]
    for move in moves:
        move.start()
    exponents.wait()
    for h in range(heads):
        spread = jnp.full((8, 128), exponent_ref[h].astype(F32))
        rates_ref[8 * h : 8 * h + 8, :] = jnp.log1p(-jnp.exp2(-spread))
        decay_ref[:, h * width : (h + 1) * width] = key_decay(head_rate(rates_ref, h), rows, width)
    for h in range(heads):
        if h % (heads // chunks) == 0:
            for load in loads[h * chunks // heads]:
                load.wait()
        cols = slice(h * width, (h + 1) * width)
        k = (k_ref[:, cols].astype(F32) * decay_ref[:, cols]).astype(BF16)
        late_ref[:, cols] = k
        held[cols, :] = dot(k, v_ref[:, cols], TN).astype(BF16)
    deal(quarter, held, outs)
    for move in moves:
        move.wait()


def owned_parts(member, heads, width):
    per = -(-heads // GROUP)
    for j in range(per):
        if member * per + j < heads:
            yield slice(j * width, (j + 1) * width), member * per + j


def total_kernel(order, rows, heads, rates_ref, *rest):
    pieces, out_ref = [rest[SENT.index(s)] for s in range(GROUP)], rest[GROUP]
    width = out_ref.shape[1]
    for me in range(GROUP):

        @pl.when(group_member() == me)
        def _():
            for part, head in owned_parts(me, heads, width):
                decay = jnp.exp(rows * head_rate(rates_ref, head))
                total = None
                for m in order:
                    state = pieces[m ^ me][part, :].astype(F32)
                    total = state if total is None else total * decay + state
                out_ref[part, :] = total.astype(BF16)


def spread_kernel(order, rows, heads, groups, reverse, rates_ref, carry_ref, *rest):
    pieces, outs = [rest[SENT.index(s)] for s in range(GROUP)], rest[GROUP:]
    width = outs[0].shape[1]
    group = lax.axis_index("ctx") // GROUP
    first = group == (groups - 1 if reverse else 0)
    for me in range(GROUP):

        @pl.when(group_member() == me)
        def _():
            for part, head in owned_parts(me, heads, width):
                decay = jnp.exp(rows * head_rate(rates_ref, head))
                state = jnp.where(first, 0.0, carry_ref[part, :].astype(F32))
                for n, m in enumerate(order):
                    outs[m ^ me][part, :] = state.astype(BF16)
                    if n + 1 < GROUP:
                        state = state * decay + pieces[m ^ me][part, :].astype(F32)


def within_kernel(heads, rates_ref, q_ref, k_ref, v_ref, out_ref, early_ref, late_ref, top_ref, bottom_ref):
    rows, width = q_ref.shape[0], q_ref.shape[1] // heads
    half = rows // 2
    for h in range(heads):
        cols = slice(h * width, (h + 1) * width)
        held = slice(h * half, (h + 1) * half)
        rate = head_rate(rates_ref, h)
        upto = query_decay(rate, rows, half)
        q, v = q_ref[:, cols], v_ref[:, cols]
        early_ref[:, cols] = (q.astype(F32) * upto).astype(BF16)
        late_ref[:, cols] = (v.astype(F32) * key_decay(rate, rows, width)).astype(BF16)
        weights = decayed_pairs(q, k_ref[:, cols], upto, since_decay(rate, rows), half)
        top_ref[held, :], bottom_ref[held, :] = weights
        out_ref[:, cols] = mix(weights, v, half)


def project_rows(slots, heads, width, pieces, weight_ref, cot_ref):
    count = len(pieces)
    rows = pieces[0].shape[0]
    per = -(-heads // GROUP)
    taken = per if heads % GROUP == 0 else 1
    tile = taken * width
    index = lax.axis_index("head")
    core, line = index % 2, index // 2

    def one(step, head):
        whole = jnp.concatenate([p[...] for p in pieces], axis=0)
        total = dot(weight_ref[band(head // taken, tile), :], whole, NT).astype(BF16).T
        for n in range(count):
            place = ((line + n // 2) % (count // 2)) * 2 + (core ^ (n % 2))
            cot_ref[band(place, rows), slice(step * tile, (step + 1) * tile)] = total[n * rows : (n + 1) * rows, :]

    for step in range(len(slots) * per // taken):
        head = (group_member() ^ slots[step * taken // per]) * per + step * taken % per
        if heads % GROUP == 0:
            one(step, head)
        else:
            pl.when(head < heads)(functools.partial(one, step, head))


def turn_heads(slots, heads, early_ref, attended_ref, cot_ref, states, outs, dout_ref):
    width = early_ref.shape[1] // heads
    per = -(-heads // GROUP)

    @slot_heads(slots, heads)
    def two(n, head):
        cols = slice(n * width, (n + 1) * width)
        part = slice(n % per * width, (n % per + 1) * width)
        q = early_ref[:, band(head, width)]
        attended = attended_ref[:, band(head, width)] + dot(q, states[n // per][part, :], NN)
        cot = cot_ref[:, cols].astype(F32)
        squares = jnp.mean(attended * attended, axis=-1, keepdims=True)
        shared = jnp.mean(cot * attended, axis=-1, keepdims=True)
        inverse = lax.rsqrt(squares + EPSILON)
        dout = ((cot - attended * (shared * inverse * inverse)) * inverse).astype(BF16)
        dout_ref[:, cols] = dout
        outs[n // per][part, :] = dot(q, dout, TN).astype(BF16)


def project_kernel(slots, heads, width, *refs):
    pieces, weight_ref, outs = refs[: -1 - len(slots)], refs[-1 - len(slots)], refs[-len(slots) :]
    for slot, out_ref in zip(slots, outs):
        project_rows([slot], heads, width, pieces, weight_ref, out_ref)


def turn_kernel(slots, heads, early_ref, attended_ref, cot_ref, *refs):
    states, outs, dout_ref = refs[: len(slots)], refs[len(slots) : -1], refs[-1]
    turn_heads(slots, heads, early_ref, attended_ref, cot_ref, states, outs, dout_ref)


def turn_own_kernel(heads, width, early_ref, attended_ref, state_ref, *refs):
    pieces, (weight_ref, out_ref, dout_ref, cot_ref) = refs[:-4], refs[-4:]
    project_rows([0], heads, width, pieces, weight_ref, cot_ref)
    turn_heads([0], heads, early_ref, attended_ref, cot_ref, [state_ref], [out_ref], dout_ref)


def slot_columns(refs, n, per, width):
    return refs[n // per][:, n % per * width : (n % per + 1) * width]


def value_grads_kernel(heads, top_ref, bottom_ref, *rest):
    douts, gv_ref = rest[:GROUP], rest[GROUP]
    half = top_ref.shape[1]
    per = -(-heads // GROUP)
    width = gv_ref.shape[1] // (GROUP * per)

    @slot_heads(SENT, heads)
    def one(n, head):
        weights = top_ref[band(head, half), :], bottom_ref[band(head, half), :]
        gv_ref[:, n * width : (n + 1) * width] = mix_back(weights, slot_columns(douts, n, per, width), half)


def key_grads_kernel(heads, rates_ref, q_ref, v_ref, *rest):
    douts, (gk_ref, top_ref, bottom_ref) = rest[:GROUP], rest[GROUP:]
    rows, width = q_ref.shape[0], q_ref.shape[1] // heads
    half = rows // 2
    per = -(-heads // GROUP)

    @slot_heads(SENT, heads)
    def one(n, head):
        held = slice(n * half, (n + 1) * half)
        rate = head_rate(rates_ref, head)
        upto = query_decay(rate, rows, half)
        dout = slot_columns(douts, n, per, width)
        dweights = decayed_pairs(dout, v_ref[:, band(head, width)], upto, since_decay(rate, rows), half)
        top_ref[held, :], bottom_ref[held, :] = dweights
        gk_ref[:, n * width : (n + 1) * width] = mix_back(dweights, q_ref[:, band(head, width)], half)


def query_grads_kernel(heads, rates_ref, k_ref, top_ref, bottom_ref, *rest):
    douts, states, gq_ref = rest[:GROUP], rest[GROUP : 2 * GROUP], rest[2 * GROUP]
    rows, width = k_ref.shape[0], k_ref.shape[1] // heads
    half = rows // 2
    per = -(-heads // GROUP)

    @slot_heads(SENT, heads)
    def one(n, head):
        held = slice(n * half, (n + 1) * half)
        dout = slot_columns(douts, n, per, width)
        late = (dout.astype(F32) * query_decay(head_rate(rates_ref, head), rows, width)).astype(BF16)
        state = states[n // per][n % per * width : (n % per + 1) * width, :]
        gq = mix((top_ref[held, :], bottom_ref[held, :]), k_ref[:, band(head, width)], half) + dot(late, state, NT)
        gq_ref[:, band(head, width)] = gq.astype(BF16)


def finish_kernel(slots, heads, taken_over, late_keys, late_values, gk_in, gv_in, *rest):
    backs, rest = rest[: len(slots)], rest[len(slots) + taken_over :]
    gk_hbm, gv_hbm, gk_ref, gv_ref, sems = rest
    per = -(-heads // GROUP)
    width = late_keys.shape[1] // heads

    def stores(n, head):
        cols = slice(n * width, (n + 1) * width)
        for side, (source, target) in enumerate(((gk_ref, gk_hbm), (gv_ref, gv_hbm))):
            yield pltpu.make_async_copy(source.at[:, cols], target.at[:, band(head, width)], sems.at[side, n])

    @slot_heads(slots, heads)
    def one(n, head):
        cols = slice(n * width, (n + 1) * width)
        at = (SENT.index(slots[n // per]) * per + n % per) * width
        back = backs[n // per][n % per * width : (n % per + 1) * width, :]
        gk = gk_in[:, at : at + width] + dot(late_values[:, band(head, width)], back, NT)
        gv = gv_in[:, at : at + width] + dot(late_keys[:, band(head, width)], back, NN)
        gk_ref[:, cols] = gk.astype(BF16)
        gv_ref[:, cols] = gv.astype(BF16)
        for store in stores(n, head):
            store.start()

    @slot_heads(slots, heads)
    def two(n, head):
        for store in stores(n, head):
            store.wait()


def swaps(pieces, axis, count):
    return {s: lax.ppermute(pieces[s], axis, [(i, i ^ s) for i in range(count)]) for s in range(1, GROUP)}


def add_up(got, rates, rows, heads, reverse):
    order = list(reversed(range(GROUP))) if reverse else list(range(GROUP))
    kernel = functools.partial(total_kernel, order, rows, heads)
    return call(kernel, [jax.ShapeDtypeStruct(got[0].shape, BF16)], [PLAIN] * (1 + GROUP), limit=4)(
        rates, *[got[s] for s in SENT]
    )[0]


def from_groups(total, rates, rows, heads, axis, count, reverse):
    groups = count // GROUP

    def shift(x, by):
        step = -by if reverse else by
        return lax.ppermute(x, axis, [(i, (i + step * GROUP) % count) for i in range(count)])

    carry = total
    if groups > 1:
        carry = shift(total, 1)
        span = 1
        while span < groups - 1:
            carry = widen(carry, shift(carry, span), rates, rows, heads, groups, span, reverse)
            span *= 2
    return carry


def spread_out(carry, got, rates, rows, heads, count, reverse):
    order = list(reversed(range(GROUP))) if reverse else list(range(GROUP))
    kernel = functools.partial(spread_kernel, order, rows, heads, count // GROUP, reverse)
    piece = jax.ShapeDtypeStruct(carry.shape, BF16)
    return call(kernel, [piece] * GROUP, [PLAIN] * (2 + GROUP), limit=4)(rates, carry, *[got[s] for s in SENT])


def widen_kernel(rows, heads, groups, span, reverse, rates_ref, near_ref, far_ref, out_ref):
    width = out_ref.shape[1]
    group = lax.axis_index("ctx") // GROUP
    reached = group + span + 1 <= groups - 1 if reverse else group >= span + 1
    for me in range(GROUP):

        @pl.when(group_member() == me)
        def _():
            for part, head in owned_parts(me, heads, width):
                decay = jnp.exp(GROUP * rows * span * head_rate(rates_ref, head))
                far = jnp.where(reached, far_ref[part, :].astype(F32), 0.0)
                out_ref[part, :] = (near_ref[part, :].astype(F32) + decay * far).astype(BF16)


def widen(near, far, rates, rows, heads, groups, span, reverse):
    kernel = functools.partial(widen_kernel, rows, heads, groups, span, reverse)
    return call(kernel, [jax.ShapeDtypeStruct(near.shape, BF16)], [PLAIN] * 3, limit=4)(rates, near, far)[0]


def gather_lines(x, axis, count):
    lines = count // 2
    return [lax.ppermute(x, axis, [(i, (i - 2 * s) % count) for i in range(count)]) for s in range(1, lines)]


def flipped(x, axis, count):
    return lax.ppermute(x, axis, [(i, i ^ 1) for i in range(count)])


def after(x, *others):
    return lax.optimization_barrier((x, others))[0]


def body(ctx_count, head_count, query, key_in, value, out_weight, grad_layer, decay_exp):
    rows, flat = query.shape
    heads = decay_exp.shape[0]
    width = flat // heads
    per = -(-heads // GROUP)
    quarter = per * width
    half = rows // 2
    rest = list(SENT[1:])

    def shaped(*shape, dtype=BF16):
        return jax.ShapeDtypeStruct(shape, dtype)

    piece = shaped(quarter, width)
    whole_rows = shaped(rows, flat)
    slot_sums = shaped(rows, GROUP * quarter, dtype=F32)

    moved = gather_lines(grad_layer, "head", head_count)
    made = call(
        functools.partial(local_state_kernel, heads, quarter),
        [piece] * GROUP
        + [shaped(8 * heads, 128, dtype=F32)]
        + [whole_rows] * 4
        + [shaped(*grad_layer.shape)],
        [STREAM] * 5,
        [
            pltpu.VMEM((GROUP * quarter, width), BF16),
            pltpu.VMEM((rows, flat), F32),
            pltpu.SMEM((heads,), jnp.int32),
            pltpu.SemaphoreType.DMA((2, max(n for n in (1, 2, 3, 4) if heads % n == 0))),
            pltpu.SemaphoreType.DMA((3,)),
        ],
        work=3 * 10**9,
    )(decay_exp, query, key_in, value, grad_layer)
    pieces = made[:GROUP]
    rates, query, key_in, value, late_keys, own = made[GROUP:]

    got = {0: pieces[0], **swaps(pieces, "ctx", ctx_count)}
    inner = call(
        functools.partial(within_kernel, heads),
        [shaped(rows, flat, dtype=F32), whole_rows, whole_rows, shaped(heads * half, half), shaped(heads * half, rows)],
        [PLAIN] * 4,
        work=3 * 10**9,
    )(rates, query, key_in, value)
    got = dict(zip(SENT, after([got[s] for s in SENT], *inner)))
    attended, early_queries, late_values, top, bottom = inner
    total = add_up(got, rates, rows, heads, False)
    carry = from_groups(total, rates, rows, heads, "ctx", ctx_count, False)
    slots = [own, flipped(after(own, total), "head", head_count)]
    for x in moved:
        x = after(x, carry)
        slots += [x, flipped(x, "head", head_count)]
    ready = spread_out(carry, got, rates, rows, heads, ctx_count, False)
    ready = dict(enumerate(ready))
    ready[SENT[-1]] = after(ready[SENT[-1]], slots[1])
    states = {0: ready[0], **swaps(ready, "ctx", ctx_count)}

    slots[-1] = after(slots[-1], ready[0])
    cots = call(
        functools.partial(project_kernel, rest, heads, width),
        [shaped(rows, quarter)] * len(rest),
        [PLAIN] * (head_count + 1),
    )(*slots, out_weight)
    pieces, douts = {}, {}
    for s, cot in zip(rest, cots):
        pieces[s], douts[s] = call(
            functools.partial(turn_kernel, [s], heads), [piece, shaped(rows, quarter)], [PLAIN] * 4
        )(early_queries, attended, cot, states[s])
    got = swaps(pieces, "ctx", ctx_count)
    mine, douts[0] = call(
        functools.partial(turn_own_kernel, heads, width),
        [piece, shaped(rows, quarter)],
        [PLAIN] * (head_count + 4),
        [pltpu.VMEM((rows, quarter), BF16)],
    )(after(early_queries, *[douts[s] for s in rest]), attended, states[0], *slots, out_weight)
    douts = [douts[s] for s in SENT]
    (value_part,) = call(functools.partial(value_grads_kernel, heads), [slot_sums], [PLAIN] * (2 + GROUP))(
        top, bottom, *douts
    )
    got = dict(zip(SENT, after([{0: mine, **got}[s] for s in SENT], value_part)))
    total = add_up(got, rates, rows, heads, True)
    carry = from_groups(total, rates, rows, heads, "ctx", ctx_count, True)
    key_part, top, bottom = call(
        functools.partial(key_grads_kernel, heads),
        [slot_sums, shaped(GROUP * per * half, half), shaped(GROUP * per * half, rows)],
        [PLAIN] * (3 + GROUP),
    )(rates, query, after(value, total), *douts)
    ready = spread_out(after(carry, key_part), got, rates, rows, heads, ctx_count, True)
    back = {0: ready[0], **swaps(ready, "ctx", ctx_count)}
    (grad_query,) = call(functools.partial(query_grads_kernel, heads), [whole_rows], [PLAIN] * (4 + 2 * GROUP))(
        rates, after(key_in, ready[0]), top, bottom, *douts, *[states[s] for s in SENT]
    )
    early_slots, late_slots = [0, 1], [3, 2]
    sums = [late_keys, late_values, key_part, value_part]
    grads = []
    for which, pieces in ((early_slots, [back[0], after(back[early_slots[1]], grad_query)]), (late_slots, None)):
        if pieces is None:
            pieces = after([back[s] for s in which], *grads)
        held = pltpu.VMEM((rows, 2 * quarter), BF16)
        grads = call(
            functools.partial(finish_kernel, which, heads, len(grads)),
            [whole_rows] * 2,
            [PLAIN] * 6 + [STREAM] * len(grads),
            [held, held, pltpu.SemaphoreType.DMA((2, 2 * per))],
            out_specs=[STREAM] * 2,
            aliases={6 + n: n for n in range(len(grads))},
        )(*sums, *pieces, *grads)
    grad_key, grad_value = grads
    return grad_query, grad_key, grad_value


def solution(mesh):
    return jax.shard_map(
        functools.partial(body, mesh.shape["ctx"], mesh.shape["head"]),
        mesh=mesh,
        in_specs=(
            P("ctx", "head"),
            P("ctx", "head"),
            P("ctx", "head"),
            P("head", None),
            P(("ctx", "head"), None),
            P("head"),
        ),
        out_specs=(P("ctx", "head"), P("ctx", "head"), P("ctx", "head")),
        check_vma=False,
    )
```

```python
import functools

import jax
import jax.numpy as jnp
from jax import lax
from jax.experimental import pallas as pl
from jax.experimental.pallas import tpu as pltpu
from jax.sharding import PartitionSpec as P

EPSILON = 1e-06
GROUP = 4
SENT = (0, 1, 3, 2)
BF16 = jnp.bfloat16
F32 = jnp.float32

PLAIN = pl.BlockSpec(memory_space=pltpu.VMEM)
STREAM = pl.BlockSpec(memory_space=pltpu.HBM)


def call(kernel, outs, in_specs, scratch=(), limit=8, work=1, out_specs=None, aliases=None):
    made = pl.pallas_call(
        kernel,
        out_shape=outs,
        in_specs=in_specs,
        out_specs=out_specs or [PLAIN] * len(outs),
        scratch_shapes=list(scratch),
        input_output_aliases=aliases or {},
        compiler_params=pltpu.CompilerParams(vmem_limit_bytes=limit * 2**20),
        cost_estimate=pl.CostEstimate(flops=work, bytes_accessed=1, transcendentals=0),
    )

    def run(*operands):
        held = [
            pltpu.with_memory_space_constraint(x, pltpu.HBM) if spec is STREAM else x
            for x, spec in zip(operands, in_specs)
        ]
        return made(*held)

    return run


def dot(a, b, dims):
    return lax.dot_general(a, b, (dims, ((), ())), preferred_element_type=F32)


NN = ((1,), (0,))
NT = ((1,), (1,))
TN = ((0,), (0,))


def steps_from(rows, width, axis, start, turn):
    place = lax.broadcasted_iota(jnp.int32, (rows, width), axis)
    return (start + turn * place).astype(F32)


def query_decay(rate, rows, width):
    return jnp.exp(steps_from(rows, width, 0, 1, 1) * rate)


def key_decay(rate, rows, width):
    return jnp.exp(steps_from(rows, width, 0, rows - 1, -1) * rate)


def since_decay(rate, rows):
    return jnp.exp(steps_from(8, rows, 1, -1, -1) * rate)[0:1]


def head_rate(rates_ref, head):
    return rates_ref[band(head, 8), :][0:1, 0:1]


def band(place, size):
    return pl.ds(pl.multiple_of(place * size, size), size)


def slot_heads(slots, heads):
    per = -(-heads // GROUP)

    def visit(one):
        for n, slot in enumerate(slots):
            for j in range(per):
                head = (group_member() ^ slot) * per + j
                if heads % GROUP == 0:
                    one(n * per + j, head)
                else:
                    pl.when(head < heads)(functools.partial(one, n * per + j, head))

    return visit


def group_member():
    return lax.axis_index("ctx") % GROUP


def decayed_pairs(left, right, upto, since, half):
    keep = steps_from(half, half, 0, 0, 1) >= steps_from(half, half, 1, 0, 1)

    def tile(rows, columns):
        pair = dot(left[rows], right[columns], NT)
        return pair * upto[rows, :half] * since[:, columns]

    low, high = slice(0, half), slice(half, 2 * half)
    top = jnp.where(keep, tile(low, low), 0.0).astype(BF16)
    side = tile(high, low).astype(BF16)
    end = jnp.where(keep, tile(high, high), 0.0).astype(BF16)
    return top, jnp.concatenate([side, end], axis=1)


def mix(pairs, values, half):
    top, bottom = pairs
    return jnp.concatenate([dot(top, values[:half], NN), dot(bottom, values, NN)], axis=0)


def mix_back(pairs, values, half):
    top, bottom = pairs
    low = dot(top, values[:half], TN)
    both = dot(bottom, values[half:], TN)
    return jnp.concatenate([low + both[:half], both[half:]], axis=0)


def deal(quarter, held, outs):
    for slot in range(GROUP):
        outs[slot][...] = held[band(group_member() ^ slot, quarter), :]


def local_state_kernel(heads, quarter, exponent_hbm, q_hbm, k_hbm, v_hbm, grad_hbm, *rest):
    outs, rest = rest[:GROUP], rest[GROUP:]
    rates_ref, q_ref, k_ref, v_ref, late_ref, grad_ref, held, decay_ref, exponent_ref, sems, later = rest
    rows = k_ref.shape[0]
    width = k_ref.shape[1] // heads
    exponents = pltpu.make_async_copy(exponent_hbm, exponent_ref, later.at[2])
    exponents.start()
    loads = []
    chunks = sems.shape[1]
    for chunk in range(chunks):
        cols = slice(chunk * heads // chunks * width, (chunk + 1) * heads // chunks * width)
        loads.append(
            [
                pltpu.make_async_copy(source.at[:, cols], target.at[:, cols], sems.at[n, chunk])
                for n, (source, target) in enumerate(((k_hbm, k_ref), (v_hbm, v_ref)))
            ]
        )
        for load in loads[-1]:
            load.start()
    moves = [
        pltpu.make_async_copy(q_hbm, q_ref, later.at[0]),
        pltpu.make_async_copy(grad_hbm, grad_ref, later.at[1]),
    ]
    for move in moves:
        move.start()
    exponents.wait()
    for h in range(heads):
        spread = jnp.full((8, 128), exponent_ref[h].astype(F32))
        rates_ref[8 * h : 8 * h + 8, :] = jnp.log1p(-jnp.exp2(-spread))
        decay_ref[:, h * width : (h + 1) * width] = key_decay(head_rate(rates_ref, h), rows, width)
    for h in range(heads):
        if h % (heads // chunks) == 0:
            for load in loads[h * chunks // heads]:
                load.wait()
        cols = slice(h * width, (h + 1) * width)
        k = (k_ref[:, cols].astype(F32) * decay_ref[:, cols]).astype(BF16)
        late_ref[:, cols] = k
        held[cols, :] = dot(k, v_ref[:, cols], TN).astype(BF16)
    deal(quarter, held, outs)
    for move in moves:
        move.wait()


def owned_parts(member, heads, width):
    per = -(-heads // GROUP)
    for j in range(per):
        if member * per + j < heads:
            yield slice(j * width, (j + 1) * width), member * per + j


def total_kernel(order, rows, heads, rates_ref, *rest):
    pieces, out_ref = [rest[SENT.index(s)] for s in range(GROUP)], rest[GROUP]
    width = out_ref.shape[1]
    for me in range(GROUP):

        @pl.when(group_member() == me)
        def _():
            for part, head in owned_parts(me, heads, width):
                decay = jnp.exp(rows * head_rate(rates_ref, head))
                total = None
                for m in order:
                    state = pieces[m ^ me][part, :].astype(F32)
                    total = state if total is None else total * decay + state
                out_ref[part, :] = total.astype(BF16)


def spread_kernel(order, rows, heads, groups, reverse, rates_ref, carry_ref, *rest):
    pieces, outs = [rest[SENT.index(s)] for s in range(GROUP)], rest[GROUP:]
    width = outs[0].shape[1]
    group = lax.axis_index("ctx") // GROUP
    first = group == (groups - 1 if reverse else 0)
    for me in range(GROUP):

        @pl.when(group_member() == me)
        def _():
            for part, head in owned_parts(me, heads, width):
                decay = jnp.exp(rows * head_rate(rates_ref, head))
                state = jnp.where(first, 0.0, carry_ref[part, :].astype(F32))
                for n, m in enumerate(order):
                    outs[m ^ me][part, :] = state.astype(BF16)
                    if n + 1 < GROUP:
                        state = state * decay + pieces[m ^ me][part, :].astype(F32)


def within_kernel(heads, rates_ref, q_ref, k_ref, v_ref, out_ref, early_ref, late_ref, top_ref, bottom_ref):
    rows, width = q_ref.shape[0], q_ref.shape[1] // heads
    half = rows // 2
    for h in range(heads):
        cols = slice(h * width, (h + 1) * width)
        held = slice(h * half, (h + 1) * half)
        rate = head_rate(rates_ref, h)
        upto = query_decay(rate, rows, half)
        q, v = q_ref[:, cols], v_ref[:, cols]
        early_ref[:, cols] = (q.astype(F32) * upto).astype(BF16)
        late_ref[:, cols] = (v.astype(F32) * key_decay(rate, rows, width)).astype(BF16)
        weights = decayed_pairs(q, k_ref[:, cols], upto, since_decay(rate, rows), half)
        top_ref[held, :], bottom_ref[held, :] = weights
        out_ref[:, cols] = mix(weights, v, half)


def project_rows(slots, heads, width, pieces, weight_ref, cot_ref):
    count = len(pieces)
    rows = pieces[0].shape[0]
    per = -(-heads // GROUP)
    taken = per if heads % GROUP == 0 else 1
    tile = taken * width
    index = lax.axis_index("head")
    core, line = index % 2, index // 2

    def one(step, head):
        whole = jnp.concatenate([p[...] for p in pieces], axis=0)
        total = dot(weight_ref[band(head // taken, tile), :], whole, NT).astype(BF16).T
        for n in range(count):
            place = ((line + n // 2) % (count // 2)) * 2 + (core ^ (n % 2))
            cot_ref[band(place, rows), slice(step * tile, (step + 1) * tile)] = total[n * rows : (n + 1) * rows, :]

    for step in range(len(slots) * per // taken):
        head = (group_member() ^ slots[step * taken // per]) * per + step * taken % per
        if heads % GROUP == 0:
            one(step, head)
        else:
            pl.when(head < heads)(functools.partial(one, step, head))


def turn_heads(slots, heads, early_ref, attended_ref, cot_ref, states, outs, dout_ref):
    width = early_ref.shape[1] // heads
    per = -(-heads // GROUP)

    @slot_heads(slots, heads)
    def two(n, head):
        cols = slice(n * width, (n + 1) * width)
        part = slice(n % per * width, (n % per + 1) * width)
        q = early_ref[:, band(head, width)]
        attended = attended_ref[:, band(head, width)] + dot(q, states[n // per][part, :], NN)
        cot = cot_ref[:, cols].astype(F32)
        squares = jnp.mean(attended * attended, axis=-1, keepdims=True)
        shared = jnp.mean(cot * attended, axis=-1, keepdims=True)
        inverse = lax.rsqrt(squares + EPSILON)
        dout = ((cot - attended * (shared * inverse * inverse)) * inverse).astype(BF16)
        dout_ref[:, cols] = dout
        outs[n // per][part, :] = dot(q, dout, TN).astype(BF16)


def project_kernel(slots, heads, width, *refs):
    pieces, weight_ref, outs = refs[: -1 - len(slots)], refs[-1 - len(slots)], refs[-len(slots) :]
    for slot, out_ref in zip(slots, outs):
        project_rows([slot], heads, width, pieces, weight_ref, out_ref)


def turn_kernel(slots, heads, early_ref, attended_ref, cot_ref, *refs):
    states, outs, dout_ref = refs[: len(slots)], refs[len(slots) : -1], refs[-1]
    turn_heads(slots, heads, early_ref, attended_ref, cot_ref, states, outs, dout_ref)


def turn_own_kernel(heads, width, early_ref, attended_ref, state_ref, *refs):
    pieces, (weight_ref, out_ref, dout_ref, cot_ref) = refs[:-4], refs[-4:]
    project_rows([0], heads, width, pieces, weight_ref, cot_ref)
    turn_heads([0], heads, early_ref, attended_ref, cot_ref, [state_ref], [out_ref], dout_ref)


def slot_columns(refs, n, per, width):
    return refs[n // per][:, n % per * width : (n % per + 1) * width]


def value_grads_kernel(heads, top_ref, bottom_ref, *rest):
    douts, gv_ref = rest[:GROUP], rest[GROUP]
    half = top_ref.shape[1]
    per = -(-heads // GROUP)
    width = gv_ref.shape[1] // (GROUP * per)

    @slot_heads(SENT, heads)
    def one(n, head):
        weights = top_ref[band(head, half), :], bottom_ref[band(head, half), :]
        gv_ref[:, n * width : (n + 1) * width] = mix_back(weights, slot_columns(douts, n, per, width), half)


def key_grads_kernel(heads, rates_ref, q_ref, v_ref, *rest):
    douts, (gk_ref, top_ref, bottom_ref) = rest[:GROUP], rest[GROUP:]
    rows, width = q_ref.shape[0], q_ref.shape[1] // heads
    half = rows // 2
    per = -(-heads // GROUP)

    @slot_heads(SENT, heads)
    def one(n, head):
        held = slice(n * half, (n + 1) * half)
        rate = head_rate(rates_ref, head)
        upto = query_decay(rate, rows, half)
        dout = slot_columns(douts, n, per, width)
        dweights = decayed_pairs(dout, v_ref[:, band(head, width)], upto, since_decay(rate, rows), half)
        top_ref[held, :], bottom_ref[held, :] = dweights
        gk_ref[:, n * width : (n + 1) * width] = mix_back(dweights, q_ref[:, band(head, width)], half)


def query_grads_kernel(heads, rates_ref, k_ref, top_ref, bottom_ref, *rest):
    douts, states, gq_ref = rest[:GROUP], rest[GROUP : 2 * GROUP], rest[2 * GROUP]
    rows, width = k_ref.shape[0], k_ref.shape[1] // heads
    half = rows // 2
    per = -(-heads // GROUP)

    @slot_heads(SENT, heads)
    def one(n, head):
        held = slice(n * half, (n + 1) * half)
        dout = slot_columns(douts, n, per, width)
        late = (dout.astype(F32) * query_decay(head_rate(rates_ref, head), rows, width)).astype(BF16)
        state = states[n // per][n % per * width : (n % per + 1) * width, :]
        gq = mix((top_ref[held, :], bottom_ref[held, :]), k_ref[:, band(head, width)], half) + dot(late, state, NT)
        gq_ref[:, band(head, width)] = gq.astype(BF16)


def finish_kernel(slots, heads, taken_over, late_keys, late_values, gk_in, gv_in, *rest):
    backs, rest = rest[: len(slots)], rest[len(slots) + taken_over :]
    gk_hbm, gv_hbm, gk_ref, gv_ref, sems = rest
    per = -(-heads // GROUP)
    width = late_keys.shape[1] // heads

    def stores(n, head):
        cols = slice(n * width, (n + 1) * width)
        for side, (source, target) in enumerate(((gk_ref, gk_hbm), (gv_ref, gv_hbm))):
            yield pltpu.make_async_copy(source.at[:, cols], target.at[:, band(head, width)], sems.at[side, n])

    @slot_heads(slots, heads)
    def one(n, head):
        cols = slice(n * width, (n + 1) * width)
        at = (SENT.index(slots[n // per]) * per + n % per) * width
        back = backs[n // per][n % per * width : (n % per + 1) * width, :]
        gk = gk_in[:, at : at + width] + dot(late_values[:, band(head, width)], back, NT)
        gv = gv_in[:, at : at + width] + dot(late_keys[:, band(head, width)], back, NN)
        gk_ref[:, cols] = gk.astype(BF16)
        gv_ref[:, cols] = gv.astype(BF16)
        for store in stores(n, head):
            store.start()

    @slot_heads(slots, heads)
    def two(n, head):
        for store in stores(n, head):
            store.wait()


def swaps(pieces, axis, count):
    return {s: lax.ppermute(pieces[s], axis, [(i, i ^ s) for i in range(count)]) for s in range(1, GROUP)}


def add_up(got, rates, rows, heads, reverse):
    order = list(reversed(range(GROUP))) if reverse else list(range(GROUP))
    kernel = functools.partial(total_kernel, order, rows, heads)
    return call(kernel, [jax.ShapeDtypeStruct(got[0].shape, BF16)], [PLAIN] * (1 + GROUP), limit=4)(
        rates, *[got[s] for s in SENT]
    )[0]


def from_groups(total, rates, rows, heads, axis, count, reverse):
    groups = count // GROUP

    def shift(x, by):
        step = -by if reverse else by
        return lax.ppermute(x, axis, [(i, (i + step * GROUP) % count) for i in range(count)])

    carry = total
    if groups > 1:
        carry = shift(total, 1)
        span = 1
        while span < groups - 1:
            carry = widen(carry, shift(carry, span), rates, rows, heads, groups, span, reverse)
            span *= 2
    return carry


def spread_out(carry, got, rates, rows, heads, count, reverse):
    order = list(reversed(range(GROUP))) if reverse else list(range(GROUP))
    kernel = functools.partial(spread_kernel, order, rows, heads, count // GROUP, reverse)
    piece = jax.ShapeDtypeStruct(carry.shape, BF16)
    return call(kernel, [piece] * GROUP, [PLAIN] * (2 + GROUP), limit=4)(rates, carry, *[got[s] for s in SENT])


def widen_kernel(rows, heads, groups, span, reverse, rates_ref, near_ref, far_ref, out_ref):
    width = out_ref.shape[1]
    group = lax.axis_index("ctx") // GROUP
    reached = group + span + 1 <= groups - 1 if reverse else group >= span + 1
    for me in range(GROUP):

        @pl.when(group_member() == me)
        def _():
            for part, head in owned_parts(me, heads, width):
                decay = jnp.exp(GROUP * rows * span * head_rate(rates_ref, head))
                far = jnp.where(reached, far_ref[part, :].astype(F32), 0.0)
                out_ref[part, :] = (near_ref[part, :].astype(F32) + decay * far).astype(BF16)


def widen(near, far, rates, rows, heads, groups, span, reverse):
    kernel = functools.partial(widen_kernel, rows, heads, groups, span, reverse)
    return call(kernel, [jax.ShapeDtypeStruct(near.shape, BF16)], [PLAIN] * 3, limit=4)(rates, near, far)[0]


def gather_lines(x, axis, count):
    lines = count // 2
    return [lax.ppermute(x, axis, [(i, (i - 2 * s) % count) for i in range(count)]) for s in range(1, lines)]


def flipped(x, axis, count):
    return lax.ppermute(x, axis, [(i, i ^ 1) for i in range(count)])


def after(x, *others):
    return lax.optimization_barrier((x, others))[0]


def body(ctx_count, head_count, query, key_in, value, out_weight, grad_layer, decay_exp):
    rows, flat = query.shape
    heads = decay_exp.shape[0]
    width = flat // heads
    per = -(-heads // GROUP)
    quarter = per * width
    half = rows // 2
    rest = list(SENT[1:])

    def shaped(*shape, dtype=BF16):
        return jax.ShapeDtypeStruct(shape, dtype)

    piece = shaped(quarter, width)
    whole_rows = shaped(rows, flat)
    slot_sums = shaped(rows, GROUP * quarter, dtype=F32)

    moved = gather_lines(grad_layer, "head", head_count)
    made = call(
        functools.partial(local_state_kernel, heads, quarter),
        [piece] * GROUP
        + [shaped(8 * heads, 128, dtype=F32)]
        + [whole_rows] * 4
        + [shaped(*grad_layer.shape)],
        [STREAM] * 5,
        [
            pltpu.VMEM((GROUP * quarter, width), BF16),
            pltpu.VMEM((rows, flat), F32),
            pltpu.SMEM((heads,), jnp.int32),
            pltpu.SemaphoreType.DMA((2, max(n for n in (1, 2, 3, 4) if heads % n == 0))),
            pltpu.SemaphoreType.DMA((3,)),
        ],
        work=3 * 10**9,
    )(decay_exp, query, key_in, value, grad_layer)
    pieces = made[:GROUP]
    rates, query, key_in, value, late_keys, own = made[GROUP:]

    got = {0: pieces[0], **swaps(pieces, "ctx", ctx_count)}
    inner = call(
        functools.partial(within_kernel, heads),
        [shaped(rows, flat, dtype=F32), whole_rows, whole_rows, shaped(heads * half, half), shaped(heads * half, rows)],
        [PLAIN] * 4,
        work=3 * 10**9,
    )(rates, query, key_in, value)
    got = dict(zip(SENT, after([got[s] for s in SENT], *inner)))
    attended, early_queries, late_values, top, bottom = inner
    total = add_up(got, rates, rows, heads, False)
    carry = from_groups(total, rates, rows, heads, "ctx", ctx_count, False)
    slots = [own, flipped(after(own, total), "head", head_count)]
    for x in moved:
        x = after(x, carry)
        slots += [x, flipped(x, "head", head_count)]
    ready = spread_out(carry, got, rates, rows, heads, ctx_count, False)
    ready = dict(enumerate(ready))
    ready[SENT[-1]] = after(ready[SENT[-1]], slots[1])
    states = {0: ready[0], **swaps(ready, "ctx", ctx_count)}

    slots[-1] = after(slots[-1], ready[0])
    cots = call(
        functools.partial(project_kernel, rest, heads, width),
        [shaped(rows, quarter)] * len(rest),
        [PLAIN] * (head_count + 1),
    )(*slots, out_weight)
    pieces, douts = {}, {}
    for s, cot in zip(rest, cots):
        pieces[s], douts[s] = call(
            functools.partial(turn_kernel, [s], heads), [piece, shaped(rows, quarter)], [PLAIN] * 4
        )(early_queries, attended, cot, states[s])
    got = swaps(pieces, "ctx", ctx_count)
    mine, douts[0] = call(
        functools.partial(turn_own_kernel, heads, width),
        [piece, shaped(rows, quarter)],
        [PLAIN] * (head_count + 4),
        [pltpu.VMEM((rows, quarter), BF16)],
    )(after(early_queries, *[douts[s] for s in rest]), attended, states[0], *slots, out_weight)
    douts = [douts[s] for s in SENT]
    (value_part,) = call(functools.partial(value_grads_kernel, heads), [slot_sums], [PLAIN] * (2 + GROUP))(
        top, bottom, *douts
    )
    got = dict(zip(SENT, after([{0: mine, **got}[s] for s in SENT], value_part)))
    total = add_up(got, rates, rows, heads, True)
    carry = from_groups(total, rates, rows, heads, "ctx", ctx_count, True)
    key_part, top, bottom = call(
        functools.partial(key_grads_kernel, heads),
        [slot_sums, shaped(GROUP * per * half, half), shaped(GROUP * per * half, rows)],
        [PLAIN] * (3 + GROUP),
    )(rates, query, after(value, total), *douts)
    ready = spread_out(after(carry, key_part), got, rates, rows, heads, ctx_count, True)
    back = {0: ready[0], **swaps(ready, "ctx", ctx_count)}
    (grad_query,) = call(functools.partial(query_grads_kernel, heads), [whole_rows], [PLAIN] * (4 + 2 * GROUP))(
        rates, after(key_in, ready[0]), top, bottom, *douts, *[states[s] for s in SENT]
    )
    stages = [0, 1], [3], [2]
    sums = [late_keys, late_values, key_part, value_part]
    grads = []
    for which in stages:
        pieces = after([back[s] for s in which], *(grads or [grad_query]))
        held = pltpu.VMEM((rows, len(which) * quarter), BF16)
        grads = call(
            functools.partial(finish_kernel, which, heads, len(grads)),
            [whole_rows] * 2,
            [PLAIN] * (4 + len(which)) + [STREAM] * len(grads),
            [held, held, pltpu.SemaphoreType.DMA((2, len(which) * per))],
            out_specs=[STREAM] * 2,
            aliases={4 + len(which) + n: n for n in range(len(grads))},
        )(*sums, *pieces, *grads)
    grad_key, grad_value = grads
    return grad_query, grad_key, grad_value


def solution(mesh):
    return jax.shard_map(
        functools.partial(body, mesh.shape["ctx"], mesh.shape["head"]),
        mesh=mesh,
        in_specs=(
            P("ctx", "head"),
            P("ctx", "head"),
            P("ctx", "head"),
            P("head", None),
            P(("ctx", "head"), None),
            P("head"),
        ),
        out_specs=(P("ctx", "head"), P("ctx", "head"), P("ctx", "head")),
        check_vma=False,
    )
```

```python
import functools

import jax
import jax.numpy as jnp
from jax import lax
from jax.experimental import pallas as pl
from jax.experimental.pallas import tpu as pltpu
from jax.sharding import PartitionSpec as P

EPSILON = 1e-06
GROUP = 4
SENT = (0, 1, 3, 2)
BF16 = jnp.bfloat16
F32 = jnp.float32

PLAIN = pl.BlockSpec(memory_space=pltpu.VMEM)
STREAM = pl.BlockSpec(memory_space=pltpu.HBM)


def call(kernel, outs, in_specs, scratch=(), limit=8, work=1, out_specs=None, aliases=None):
    made = pl.pallas_call(
        kernel,
        out_shape=outs,
        in_specs=in_specs,
        out_specs=out_specs or [PLAIN] * len(outs),
        scratch_shapes=list(scratch),
        input_output_aliases=aliases or {},
        compiler_params=pltpu.CompilerParams(vmem_limit_bytes=limit * 2**20),
        cost_estimate=pl.CostEstimate(flops=work, bytes_accessed=1, transcendentals=0),
    )

    def run(*operands):
        held = [
            pltpu.with_memory_space_constraint(x, pltpu.HBM) if spec is STREAM else x
            for x, spec in zip(operands, in_specs)
        ]
        return made(*held)

    return run


def dot(a, b, dims):
    return lax.dot_general(a, b, (dims, ((), ())), preferred_element_type=F32)


NN = ((1,), (0,))
NT = ((1,), (1,))
TN = ((0,), (0,))


def steps_from(rows, width, axis, start, turn):
    place = lax.broadcasted_iota(jnp.int32, (rows, width), axis)
    return (start + turn * place).astype(F32)


def query_decay(rate, rows, width):
    return jnp.exp(steps_from(rows, width, 0, 1, 1) * rate)


def key_decay(rate, rows, width):
    return jnp.exp(steps_from(rows, width, 0, rows - 1, -1) * rate)


def since_decay(rate, rows):
    return jnp.exp(steps_from(8, rows, 1, -1, -1) * rate)[0:1]


def head_rate(rates_ref, head):
    return rates_ref[band(head, 8), :][0:1, 0:1]


def band(place, size):
    return pl.ds(pl.multiple_of(place * size, size), size)


def slot_heads(slots, heads):
    per = -(-heads // GROUP)

    def visit(one):
        for n, slot in enumerate(slots):
            for j in range(per):
                head = (group_member() ^ slot) * per + j
                if heads % GROUP == 0:
                    one(n * per + j, head)
                else:
                    pl.when(head < heads)(functools.partial(one, n * per + j, head))

    return visit


def group_member():
    return lax.axis_index("ctx") % GROUP


def decayed_pairs(left, right, upto, since, half):
    keep = steps_from(half, half, 0, 0, 1) >= steps_from(half, half, 1, 0, 1)

    def tile(rows, columns):
        pair = dot(left[rows], right[columns], NT)
        return pair * upto[rows, :half] * since[:, columns]

    low, high = slice(0, half), slice(half, 2 * half)
    top = jnp.where(keep, tile(low, low), 0.0).astype(BF16)
    side = tile(high, low).astype(BF16)
    end = jnp.where(keep, tile(high, high), 0.0).astype(BF16)
    return top, jnp.concatenate([side, end], axis=1)


def mix(pairs, values, half):
    top, bottom = pairs
    return jnp.concatenate([dot(top, values[:half], NN), dot(bottom, values, NN)], axis=0)


def mix_back(pairs, values, half):
    top, bottom = pairs
    low = dot(top, values[:half], TN)
    both = dot(bottom, values[half:], TN)
    return jnp.concatenate([low + both[:half], both[half:]], axis=0)


def deal(quarter, held, outs):
    for slot in range(GROUP):
        outs[slot][...] = held[band(group_member() ^ slot, quarter), :]


def local_state_kernel(heads, quarter, exponent_hbm, q_hbm, k_hbm, v_hbm, grad_hbm, *rest):
    outs, rest = rest[:GROUP], rest[GROUP:]
    rates_ref, q_ref, k_ref, v_ref, late_ref, grad_ref, held, decay_ref, exponent_ref, sems, later = rest
    rows = k_ref.shape[0]
    width = k_ref.shape[1] // heads
    exponents = pltpu.make_async_copy(exponent_hbm, exponent_ref, later.at[2])
    exponents.start()
    loads = []
    chunks = sems.shape[1]
    for chunk in range(chunks):
        cols = slice(chunk * heads // chunks * width, (chunk + 1) * heads // chunks * width)
        loads.append(
            [
                pltpu.make_async_copy(source.at[:, cols], target.at[:, cols], sems.at[n, chunk])
                for n, (source, target) in enumerate(((k_hbm, k_ref), (v_hbm, v_ref)))
            ]
        )
        for load in loads[-1]:
            load.start()
    moves = [
        pltpu.make_async_copy(q_hbm, q_ref, later.at[0]),
        pltpu.make_async_copy(grad_hbm, grad_ref, later.at[1]),
    ]
    for move in moves:
        move.start()
    exponents.wait()
    for h in range(heads):
        spread = jnp.full((8, 128), exponent_ref[h].astype(F32))
        rates_ref[8 * h : 8 * h + 8, :] = jnp.log1p(-jnp.exp2(-spread))
        decay_ref[:, h * width : (h + 1) * width] = key_decay(head_rate(rates_ref, h), rows, width)
    for h in range(heads):
        if h % (heads // chunks) == 0:
            for load in loads[h * chunks // heads]:
                load.wait()
        cols = slice(h * width, (h + 1) * width)
        k = (k_ref[:, cols].astype(F32) * decay_ref[:, cols]).astype(BF16)
        late_ref[:, cols] = k
        held[cols, :] = dot(k, v_ref[:, cols], TN).astype(BF16)
    deal(quarter, held, outs)
    for move in moves:
        move.wait()


def owned_parts(member, heads, width):
    per = -(-heads // GROUP)
    for j in range(per):
        if member * per + j < heads:
            yield slice(j * width, (j + 1) * width), member * per + j


def total_kernel(order, rows, heads, rates_ref, *rest):
    pieces, out_ref = [rest[SENT.index(s)] for s in range(GROUP)], rest[GROUP]
    width = out_ref.shape[1]
    for me in range(GROUP):

        @pl.when(group_member() == me)
        def _():
            for part, head in owned_parts(me, heads, width):
                decay = jnp.exp(rows * head_rate(rates_ref, head))
                total = None
                for m in order:
                    state = pieces[m ^ me][part, :].astype(F32)
                    total = state if total is None else total * decay + state
                out_ref[part, :] = total.astype(BF16)


def spread_kernel(order, rows, heads, groups, reverse, rates_ref, carry_ref, *rest):
    pieces, outs = [rest[SENT.index(s)] for s in range(GROUP)], rest[GROUP:]
    width = outs[0].shape[1]
    group = lax.axis_index("ctx") // GROUP
    first = group == (groups - 1 if reverse else 0)
    for me in range(GROUP):

        @pl.when(group_member() == me)
        def _():
            for part, head in owned_parts(me, heads, width):
                decay = jnp.exp(rows * head_rate(rates_ref, head))
                state = jnp.where(first, 0.0, carry_ref[part, :].astype(F32))
                for n, m in enumerate(order):
                    outs[m ^ me][part, :] = state.astype(BF16)
                    if n + 1 < GROUP:
                        state = state * decay + pieces[m ^ me][part, :].astype(F32)


def within_kernel(heads, rates_ref, q_ref, k_ref, v_ref, out_ref, early_ref, turned_ref, late_ref, top_ref, bottom_ref):
    rows, width = q_ref.shape[0], q_ref.shape[1] // heads
    half = rows // 2
    for h in range(heads):
        cols = slice(h * width, (h + 1) * width)
        held = slice(h * half, (h + 1) * half)
        rate = head_rate(rates_ref, h)
        upto = query_decay(rate, rows, half)
        q, v = q_ref[:, cols], v_ref[:, cols]
        early = (q.astype(F32) * upto).astype(BF16)
        early_ref[:, cols] = early
        turned_ref[cols, :] = early.T
        late_ref[:, cols] = (v.astype(F32) * key_decay(rate, rows, width)).astype(BF16)
        weights = decayed_pairs(q, k_ref[:, cols], upto, since_decay(rate, rows), half)
        top_ref[held, :], bottom_ref[held, :] = weights
        out_ref[:, cols] = mix(weights, v, half)


def project_rows(slots, heads, width, pieces, weight_ref, cot_ref):
    count = len(pieces)
    rows = pieces[0].shape[0]
    per = -(-heads // GROUP)
    taken = per if heads % GROUP == 0 else 1
    tile = taken * width
    index = lax.axis_index("head")
    core, line = index % 2, index // 2

    def one(step, head):
        whole = jnp.concatenate([p[...] for p in pieces], axis=0)
        total = dot(weight_ref[band(head // taken, tile), :], whole, NT).astype(BF16).T
        for n in range(count):
            place = ((line + n // 2) % (count // 2)) * 2 + (core ^ (n % 2))
            cot_ref[band(place, rows), slice(step * tile, (step + 1) * tile)] = total[n * rows : (n + 1) * rows, :]

    for step in range(len(slots) * per // taken):
        head = (group_member() ^ slots[step * taken // per]) * per + step * taken % per
        if heads % GROUP == 0:
            one(step, head)
        else:
            pl.when(head < heads)(functools.partial(one, step, head))


def turn_heads(slots, heads, early_ref, turned_ref, attended_ref, cot_ref, states, outs, dout_ref):
    width = early_ref.shape[1] // heads
    per = -(-heads // GROUP)

    @slot_heads(slots, heads)
    def two(n, head):
        cols = slice(n * width, (n + 1) * width)
        part = slice(n % per * width, (n % per + 1) * width)
        q = early_ref[:, band(head, width)]
        attended = attended_ref[:, band(head, width)] + dot(q, states[n // per][part, :], NN)
        cot = cot_ref[:, cols].astype(F32)
        squares = jnp.mean(attended * attended, axis=-1, keepdims=True)
        shared = jnp.mean(cot * attended, axis=-1, keepdims=True)
        inverse = lax.rsqrt(squares + EPSILON)
        dout = ((cot - attended * (shared * inverse * inverse)) * inverse).astype(BF16)
        dout_ref[:, cols] = dout
        outs[n // per][part, :] = dot(turned_ref[band(head, width), :], dout, NN).astype(BF16)


def project_kernel(slots, heads, width, *refs):
    pieces, weight_ref, outs = refs[: -1 - len(slots)], refs[-1 - len(slots)], refs[-len(slots) :]
    for slot, out_ref in zip(slots, outs):
        project_rows([slot], heads, width, pieces, weight_ref, out_ref)


def turn_kernel(slots, heads, early_ref, turned_ref, attended_ref, cot_ref, *refs):
    states, outs, dout_ref = refs[: len(slots)], refs[len(slots) : -1], refs[-1]
    turn_heads(slots, heads, early_ref, turned_ref, attended_ref, cot_ref, states, outs, dout_ref)


def turn_own_kernel(heads, width, early_ref, turned_ref, attended_ref, state_ref, *refs):
    pieces, (weight_ref, out_ref, dout_ref, cot_ref) = refs[:-4], refs[-4:]
    project_rows([0], heads, width, pieces, weight_ref, cot_ref)
    turn_heads([0], heads, early_ref, turned_ref, attended_ref, cot_ref, [state_ref], [out_ref], dout_ref)


def slot_columns(refs, n, per, width):
    return refs[n // per][:, n % per * width : (n % per + 1) * width]


def value_grads_kernel(heads, top_ref, bottom_ref, *rest):
    douts, gv_ref = rest[:GROUP], rest[GROUP]
    half = top_ref.shape[1]
    per = -(-heads // GROUP)
    width = gv_ref.shape[1] // (GROUP * per)

    @slot_heads(SENT, heads)
    def one(n, head):
        weights = top_ref[band(head, half), :], bottom_ref[band(head, half), :]
        gv_ref[:, n * width : (n + 1) * width] = mix_back(weights, slot_columns(douts, n, per, width), half)


def key_grads_kernel(heads, rates_ref, q_ref, v_ref, *rest):
    douts, (gk_ref, top_ref, bottom_ref) = rest[:GROUP], rest[GROUP:]
    rows, width = q_ref.shape[0], q_ref.shape[1] // heads
    half = rows // 2
    per = -(-heads // GROUP)

    @slot_heads(SENT, heads)
    def one(n, head):
        held = slice(n * half, (n + 1) * half)
        rate = head_rate(rates_ref, head)
        upto = query_decay(rate, rows, half)
        dout = slot_columns(douts, n, per, width)
        dweights = decayed_pairs(dout, v_ref[:, band(head, width)], upto, since_decay(rate, rows), half)
        top_ref[held, :], bottom_ref[held, :] = dweights
        gk_ref[:, n * width : (n + 1) * width] = mix_back(dweights, q_ref[:, band(head, width)], half)


def query_grads_kernel(heads, rates_ref, k_ref, top_ref, bottom_ref, *rest):
    douts, states, gq_ref = rest[:GROUP], rest[GROUP : 2 * GROUP], rest[2 * GROUP]
    rows, width = k_ref.shape[0], k_ref.shape[1] // heads
    half = rows // 2
    per = -(-heads // GROUP)

    @slot_heads(SENT, heads)
    def one(n, head):
        held = slice(n * half, (n + 1) * half)
        dout = slot_columns(douts, n, per, width)
        late = (dout.astype(F32) * query_decay(head_rate(rates_ref, head), rows, width)).astype(BF16)
        state = states[n // per][n % per * width : (n % per + 1) * width, :]
        gq = mix((top_ref[held, :], bottom_ref[held, :]), k_ref[:, band(head, width)], half) + dot(late, state, NT)
        gq_ref[:, band(head, width)] = gq.astype(BF16)


def finish_kernel(slots, heads, taken_over, late_keys, late_values, gk_in, gv_in, *rest):
    backs, rest = rest[: len(slots)], rest[len(slots) + taken_over :]
    gk_hbm, gv_hbm, gk_ref, gv_ref, sems = rest
    per = -(-heads // GROUP)
    width = late_keys.shape[1] // heads

    def stores(n, head):
        cols = slice(n * width, (n + 1) * width)
        for side, (source, target) in enumerate(((gk_ref, gk_hbm), (gv_ref, gv_hbm))):
            yield pltpu.make_async_copy(source.at[:, cols], target.at[:, band(head, width)], sems.at[side, n])

    @slot_heads(slots, heads)
    def one(n, head):
        cols = slice(n * width, (n + 1) * width)
        at = (SENT.index(slots[n // per]) * per + n % per) * width
        back = backs[n // per][n % per * width : (n % per + 1) * width, :]
        key_store, value_store = stores(n, head)
        gk = gk_in[:, at : at + width] + dot(late_values[:, band(head, width)], back, NT)
        gk_ref[:, cols] = gk.astype(BF16)
        key_store.start()
        gv = gv_in[:, at : at + width] + dot(late_keys[:, band(head, width)], back, NN)
        gv_ref[:, cols] = gv.astype(BF16)
        value_store.start()

    @slot_heads(slots, heads)
    def two(n, head):
        for store in stores(n, head):
            store.wait()


def swaps(pieces, axis, count):
    return {s: lax.ppermute(pieces[s], axis, [(i, i ^ s) for i in range(count)]) for s in range(1, GROUP)}


def add_up(got, rates, rows, heads, reverse):
    order = list(reversed(range(GROUP))) if reverse else list(range(GROUP))
    kernel = functools.partial(total_kernel, order, rows, heads)
    return call(kernel, [jax.ShapeDtypeStruct(got[0].shape, BF16)], [PLAIN] * (1 + GROUP), limit=4)(
        rates, *[got[s] for s in SENT]
    )[0]


def from_groups(total, rates, rows, heads, axis, count, reverse):
    groups = count // GROUP

    def shift(x, by):
        step = -by if reverse else by
        return lax.ppermute(x, axis, [(i, (i + step * GROUP) % count) for i in range(count)])

    carry = total
    if groups > 1:
        carry = shift(total, 1)
        span = 1
        while span < groups - 1:
            carry = widen(carry, shift(carry, span), rates, rows, heads, groups, span, reverse)
            span *= 2
    return carry


def spread_out(carry, got, rates, rows, heads, count, reverse):
    order = list(reversed(range(GROUP))) if reverse else list(range(GROUP))
    kernel = functools.partial(spread_kernel, order, rows, heads, count // GROUP, reverse)
    piece = jax.ShapeDtypeStruct(carry.shape, BF16)
    return call(kernel, [piece] * GROUP, [PLAIN] * (2 + GROUP), limit=4)(rates, carry, *[got[s] for s in SENT])


def widen_kernel(rows, heads, groups, span, reverse, rates_ref, near_ref, far_ref, out_ref):
    width = out_ref.shape[1]
    group = lax.axis_index("ctx") // GROUP
    reached = group + span + 1 <= groups - 1 if reverse else group >= span + 1
    for me in range(GROUP):

        @pl.when(group_member() == me)
        def _():
            for part, head in owned_parts(me, heads, width):
                decay = jnp.exp(GROUP * rows * span * head_rate(rates_ref, head))
                far = jnp.where(reached, far_ref[part, :].astype(F32), 0.0)
                out_ref[part, :] = (near_ref[part, :].astype(F32) + decay * far).astype(BF16)


def widen(near, far, rates, rows, heads, groups, span, reverse):
    kernel = functools.partial(widen_kernel, rows, heads, groups, span, reverse)
    return call(kernel, [jax.ShapeDtypeStruct(near.shape, BF16)], [PLAIN] * 3, limit=4)(rates, near, far)[0]


def gather_lines(x, axis, count):
    lines = count // 2
    return [lax.ppermute(x, axis, [(i, (i - 2 * s) % count) for i in range(count)]) for s in range(1, lines)]


def flipped(x, axis, count):
    return lax.ppermute(x, axis, [(i, i ^ 1) for i in range(count)])


def after(x, *others):
    return lax.optimization_barrier((x, others))[0]


def body(ctx_count, head_count, query, key_in, value, out_weight, grad_layer, decay_exp):
    rows, flat = query.shape
    heads = decay_exp.shape[0]
    width = flat // heads
    per = -(-heads // GROUP)
    quarter = per * width
    half = rows // 2
    rest = list(SENT[1:])

    def shaped(*shape, dtype=BF16):
        return jax.ShapeDtypeStruct(shape, dtype)

    piece = shaped(quarter, width)
    whole_rows = shaped(rows, flat)
    slot_sums = shaped(rows, GROUP * quarter, dtype=F32)

    moved = gather_lines(grad_layer, "head", head_count)
    made = call(
        functools.partial(local_state_kernel, heads, quarter),
        [piece] * GROUP
        + [shaped(8 * heads, 128, dtype=F32)]
        + [whole_rows] * 4
        + [shaped(*grad_layer.shape)],
        [STREAM] * 5,
        [
            pltpu.VMEM((GROUP * quarter, width), BF16),
            pltpu.VMEM((rows, flat), F32),
            pltpu.SMEM((heads,), jnp.int32),
            pltpu.SemaphoreType.DMA((2, max(n for n in (1, 2, 3, 4) if heads % n == 0))),
            pltpu.SemaphoreType.DMA((3,)),
        ],
        work=3 * 10**9,
    )(decay_exp, query, key_in, value, grad_layer)
    pieces = made[:GROUP]
    rates, query, key_in, value, late_keys, own = made[GROUP:]

    got = {0: pieces[0], **swaps(pieces, "ctx", ctx_count)}
    inner = call(
        functools.partial(within_kernel, heads),
        [shaped(rows, flat, dtype=F32), whole_rows, shaped(flat, rows), whole_rows]
        + [shaped(heads * half, half), shaped(heads * half, rows)],
        [PLAIN] * 4,
        work=3 * 10**9,
    )(rates, query, key_in, value)
    got = dict(zip(SENT, after([got[s] for s in SENT], *inner)))
    attended, early_queries, turned_queries, late_values, top, bottom = inner
    total = add_up(got, rates, rows, heads, False)
    carry = from_groups(total, rates, rows, heads, "ctx", ctx_count, False)
    slots = [own, flipped(after(own, total), "head", head_count)]
    for x in moved:
        x = after(x, carry)
        slots += [x, flipped(x, "head", head_count)]
    ready = spread_out(carry, got, rates, rows, heads, ctx_count, False)
    ready = dict(enumerate(ready))
    ready[SENT[-1]] = after(ready[SENT[-1]], slots[1])
    states = {0: ready[0], **swaps(ready, "ctx", ctx_count)}

    slots[-1] = after(slots[-1], ready[0])
    cots = call(
        functools.partial(project_kernel, rest, heads, width),
        [shaped(rows, quarter)] * len(rest),
        [PLAIN] * (head_count + 1),
    )(*slots, out_weight)
    pieces, douts = {}, {}
    for s, cot in zip(rest, cots):
        pieces[s], douts[s] = call(
            functools.partial(turn_kernel, [s], heads), [piece, shaped(rows, quarter)], [PLAIN] * 5
        )(early_queries, turned_queries, attended, cot, states[s])
    got = swaps(pieces, "ctx", ctx_count)
    mine, douts[0] = call(
        functools.partial(turn_own_kernel, heads, width),
        [piece, shaped(rows, quarter)],
        [PLAIN] * (head_count + 5),
        [pltpu.VMEM((rows, quarter), BF16)],
    )(after(early_queries, *[douts[s] for s in rest]), turned_queries, attended, states[0], *slots, out_weight)
    douts = [douts[s] for s in SENT]
    (value_part,) = call(functools.partial(value_grads_kernel, heads), [slot_sums], [PLAIN] * (2 + GROUP))(
        top, bottom, *douts
    )
    got = dict(zip(SENT, after([{0: mine, **got}[s] for s in SENT], value_part)))
    total = add_up(got, rates, rows, heads, True)
    carry = from_groups(total, rates, rows, heads, "ctx", ctx_count, True)
    key_part, top, bottom = call(
        functools.partial(key_grads_kernel, heads),
        [slot_sums, shaped(GROUP * per * half, half), shaped(GROUP * per * half, rows)],
        [PLAIN] * (3 + GROUP),
    )(rates, query, after(value, total), *douts)
    ready = spread_out(after(carry, key_part), got, rates, rows, heads, ctx_count, True)
    back = {0: ready[0], **swaps(ready, "ctx", ctx_count)}
    (grad_query,) = call(functools.partial(query_grads_kernel, heads), [whole_rows], [PLAIN] * (4 + 2 * GROUP))(
        rates, after(key_in, ready[0]), top, bottom, *douts, *[states[s] for s in SENT]
    )
    stages = [0, 1], [3], [2]
    sums = [late_keys, late_values, key_part, value_part]
    grads = []
    for which in stages:
        pieces = after([back[s] for s in which], *(grads or [grad_query]))
        held = pltpu.VMEM((rows, len(which) * quarter), BF16)
        grads = call(
            functools.partial(finish_kernel, which, heads, len(grads)),
            [whole_rows] * 2,
            [PLAIN] * (4 + len(which)) + [STREAM] * len(grads),
            [held, held, pltpu.SemaphoreType.DMA((2, len(which) * per))],
            out_specs=[STREAM] * 2,
            aliases={4 + len(which) + n: n for n in range(len(grads))},
        )(*sums, *pieces, *grads)
    grad_key, grad_value = grads
    return grad_query, grad_key, grad_value


def solution(mesh):
    return jax.shard_map(
        functools.partial(body, mesh.shape["ctx"], mesh.shape["head"]),
        mesh=mesh,
        in_specs=(
            P("ctx", "head"),
            P("ctx", "head"),
            P("ctx", "head"),
            P("head", None),
            P(("ctx", "head"), None),
            P("head"),
        ),
        out_specs=(P("ctx", "head"), P("ctx", "head"), P("ctx", "head")),
        check_vma=False,
    )
```

```python
import functools

import jax
import jax.numpy as jnp
from jax import lax
from jax.experimental import pallas as pl
from jax.experimental.pallas import tpu as pltpu
from jax.sharding import PartitionSpec as P

EPSILON = 1e-06
GROUP = 4
SENT = (0, 1, 3, 2)
BF16 = jnp.bfloat16
F32 = jnp.float32

PLAIN = pl.BlockSpec(memory_space=pltpu.VMEM)
STREAM = pl.BlockSpec(memory_space=pltpu.HBM)


def call(kernel, outs, in_specs, scratch=(), limit=8, work=1, out_specs=None, aliases=None):
    made = pl.pallas_call(
        kernel,
        out_shape=outs,
        in_specs=in_specs,
        out_specs=out_specs or [PLAIN] * len(outs),
        scratch_shapes=list(scratch),
        input_output_aliases=aliases or {},
        compiler_params=pltpu.CompilerParams(vmem_limit_bytes=limit * 2**20),
        cost_estimate=pl.CostEstimate(flops=work, bytes_accessed=1, transcendentals=0),
    )

    def run(*operands):
        held = [
            pltpu.with_memory_space_constraint(x, pltpu.HBM) if spec is STREAM else x
            for x, spec in zip(operands, in_specs)
        ]
        return made(*held)

    return run


def dot(a, b, dims):
    return lax.dot_general(a, b, (dims, ((), ())), preferred_element_type=F32)


NN = ((1,), (0,))
NT = ((1,), (1,))
TN = ((0,), (0,))


def steps_from(rows, width, axis, start, turn):
    place = lax.broadcasted_iota(jnp.int32, (rows, width), axis)
    return (start + turn * place).astype(F32)


def query_decay(rate, rows, width):
    return jnp.exp(steps_from(rows, width, 0, 1, 1) * rate)


def key_decay(rate, rows, width):
    return jnp.exp(steps_from(rows, width, 0, rows - 1, -1) * rate)


def since_decay(rate, rows):
    return jnp.exp(steps_from(8, rows, 1, -1, -1) * rate)[0:1]


def head_rate(rates_ref, head):
    return rates_ref[band(head, 8), :][0:1, 0:1]


def band(place, size):
    return pl.ds(pl.multiple_of(place * size, size), size)


def slot_heads(slots, heads):
    per = -(-heads // GROUP)

    def visit(one):
        for n, slot in enumerate(slots):
            for j in range(per):
                head = (group_member() ^ slot) * per + j
                if heads % GROUP == 0:
                    one(n * per + j, head)
                else:
                    pl.when(head < heads)(functools.partial(one, n * per + j, head))

    return visit


def group_member():
    return lax.axis_index("ctx") % GROUP


def decayed_pairs(left, right, upto, since, half):
    keep = steps_from(half, half, 0, 0, 1) >= steps_from(half, half, 1, 0, 1)

    def tile(rows, columns):
        pair = dot(left[rows], right[columns], NT)
        return pair * upto[rows, :half] * since[:, columns]

    low, high = slice(0, half), slice(half, 2 * half)
    top = jnp.where(keep, tile(low, low), 0.0).astype(BF16)
    side = tile(high, low).astype(BF16)
    end = jnp.where(keep, tile(high, high), 0.0).astype(BF16)
    return top, jnp.concatenate([side, end], axis=1)


def mix(pairs, values, half):
    top, bottom = pairs
    return jnp.concatenate([dot(top, values[:half], NN), dot(bottom, values, NN)], axis=0)


def mix_back(pairs, values, half):
    top, bottom = pairs
    low = dot(top, values[:half], TN)
    both = dot(bottom, values[half:], TN)
    return jnp.concatenate([low + both[:half], both[half:]], axis=0)


def deal(quarter, held, outs):
    for slot in range(GROUP):
        outs[slot][...] = held[band(group_member() ^ slot, quarter), :]


def local_state_kernel(heads, quarter, exponent_hbm, q_hbm, k_hbm, v_hbm, grad_hbm, *rest):
    outs, rest = rest[:GROUP], rest[GROUP:]
    rates_ref, q_ref, k_ref, v_ref, late_ref, grad_ref, held, decay_ref, exponent_ref, sems, later = rest
    rows = k_ref.shape[0]
    width = k_ref.shape[1] // heads
    exponents = pltpu.make_async_copy(exponent_hbm, exponent_ref, later.at[2])
    exponents.start()
    loads = []
    chunks = sems.shape[1]
    for chunk in range(chunks):
        cols = slice(chunk * heads // chunks * width, (chunk + 1) * heads // chunks * width)
        loads.append(
            [
                pltpu.make_async_copy(source.at[:, cols], target.at[:, cols], sems.at[n, chunk])
                for n, (source, target) in enumerate(((k_hbm, k_ref), (v_hbm, v_ref)))
            ]
        )
        for load in loads[-1]:
            load.start()
    moves = [
        pltpu.make_async_copy(q_hbm, q_ref, later.at[0]),
        pltpu.make_async_copy(grad_hbm, grad_ref, later.at[1]),
    ]
    for move in moves:
        move.start()
    exponents.wait()
    for h in range(heads):
        spread = jnp.full((8, 128), exponent_ref[h].astype(F32))
        rates_ref[8 * h : 8 * h + 8, :] = jnp.log1p(-jnp.exp2(-spread))
        decay_ref[:, h * width : (h + 1) * width] = key_decay(head_rate(rates_ref, h), rows, width)
    for h in range(heads):
        if h % (heads // chunks) == 0:
            for load in loads[h * chunks // heads]:
                load.wait()
        cols = slice(h * width, (h + 1) * width)
        k = (k_ref[:, cols].astype(F32) * decay_ref[:, cols]).astype(BF16)
        late_ref[:, cols] = k
        held[cols, :] = dot(k, v_ref[:, cols], TN).astype(BF16)
    deal(quarter, held, outs)
    for move in moves:
        move.wait()


def owned_parts(member, heads, width):
    per = -(-heads // GROUP)
    for j in range(per):
        if member * per + j < heads:
            yield slice(j * width, (j + 1) * width), member * per + j


def total_kernel(order, rows, heads, rates_ref, *rest):
    pieces, out_ref = [rest[SENT.index(s)] for s in range(GROUP)], rest[GROUP]
    width = out_ref.shape[1]
    for me in range(GROUP):

        @pl.when(group_member() == me)
        def _():
            for part, head in owned_parts(me, heads, width):
                decay = jnp.exp(rows * head_rate(rates_ref, head))
                total = None
                for m in order:
                    state = pieces[m ^ me][part, :].astype(F32)
                    total = state if total is None else total * decay + state
                out_ref[part, :] = total.astype(BF16)


def spread_kernel(order, rows, heads, groups, reverse, rates_ref, carry_ref, *rest):
    pieces, outs = [rest[SENT.index(s)] for s in range(GROUP)], rest[GROUP:]
    width = outs[0].shape[1]
    group = lax.axis_index("ctx") // GROUP
    first = group == (groups - 1 if reverse else 0)
    for me in range(GROUP):

        @pl.when(group_member() == me)
        def _():
            for part, head in owned_parts(me, heads, width):
                decay = jnp.exp(rows * head_rate(rates_ref, head))
                state = jnp.where(first, 0.0, carry_ref[part, :].astype(F32))
                for n, m in enumerate(order):
                    outs[m ^ me][part, :] = state.astype(BF16)
                    if n + 1 < GROUP:
                        state = state * decay + pieces[m ^ me][part, :].astype(F32)


def within_kernel(heads, rates_ref, q_ref, k_ref, v_ref, out_ref, early_ref, turned_ref, late_ref, top_ref, bottom_ref):
    rows, width = q_ref.shape[0], q_ref.shape[1] // heads
    half = rows // 2
    for h in range(heads):
        cols = slice(h * width, (h + 1) * width)
        held = slice(h * half, (h + 1) * half)
        rate = head_rate(rates_ref, h)
        upto = query_decay(rate, rows, half)
        q, v = q_ref[:, cols], v_ref[:, cols]
        early = (q.astype(F32) * upto).astype(BF16)
        early_ref[:, cols] = early
        turned_ref[cols, :] = early.T
        late_ref[:, cols] = (v.astype(F32) * key_decay(rate, rows, width)).astype(BF16)
        weights = decayed_pairs(q, k_ref[:, cols], upto, since_decay(rate, rows), half)
        top_ref[held, :], bottom_ref[held, :] = weights
        out_ref[:, cols] = mix(weights, v, half)


def project_rows(slots, heads, width, pieces, weight_ref, cot_ref):
    count = len(pieces)
    rows = pieces[0].shape[0]
    per = -(-heads // GROUP)
    taken = per if heads % GROUP == 0 else 1
    tile = taken * width
    index = lax.axis_index("head")
    core, line = index % 2, index // 2

    def one(step, head):
        whole = jnp.concatenate([p[...] for p in pieces], axis=0)
        total = dot(weight_ref[band(head // taken, tile), :], whole, NT).astype(BF16).T
        for n in range(count):
            place = ((line + n // 2) % (count // 2)) * 2 + (core ^ (n % 2))
            cot_ref[band(place, rows), slice(step * tile, (step + 1) * tile)] = total[n * rows : (n + 1) * rows, :]

    for step in range(len(slots) * per // taken):
        head = (group_member() ^ slots[step * taken // per]) * per + step * taken % per
        if heads % GROUP == 0:
            one(step, head)
        else:
            pl.when(head < heads)(functools.partial(one, step, head))


def turn_heads(slots, heads, early_ref, turned_ref, attended_ref, cot_ref, states, outs, dout_ref):
    width = early_ref.shape[1] // heads
    per = -(-heads // GROUP)

    @slot_heads(slots, heads)
    def two(n, head):
        cols = slice(n * width, (n + 1) * width)
        part = slice(n % per * width, (n % per + 1) * width)
        q = early_ref[:, band(head, width)]
        attended = attended_ref[:, band(head, width)] + dot(q, states[n // per][part, :], NN)
        cot = cot_ref[:, cols].astype(F32)
        squares = jnp.mean(attended * attended, axis=-1, keepdims=True)
        shared = jnp.mean(cot * attended, axis=-1, keepdims=True)
        inverse = lax.rsqrt(squares + EPSILON)
        dout = ((cot - attended * (shared * inverse * inverse)) * inverse).astype(BF16)
        dout_ref[:, cols] = dout
        outs[n // per][part, :] = dot(turned_ref[band(head, width), :], dout, NN).astype(BF16)


def project_kernel(slots, heads, width, *refs):
    pieces, weight_ref, outs = refs[: -1 - len(slots)], refs[-1 - len(slots)], refs[-len(slots) :]
    for slot, out_ref in zip(slots, outs):
        project_rows([slot], heads, width, pieces, weight_ref, out_ref)


def turn_kernel(slots, heads, early_ref, turned_ref, attended_ref, cot_ref, *refs):
    states, outs, dout_ref = refs[: len(slots)], refs[len(slots) : -1], refs[-1]
    turn_heads(slots, heads, early_ref, turned_ref, attended_ref, cot_ref, states, outs, dout_ref)


def turn_own_kernel(heads, width, early_ref, turned_ref, attended_ref, state_ref, *refs):
    pieces, (weight_ref, out_ref, dout_ref, cot_ref) = refs[:-4], refs[-4:]
    project_rows([0], heads, width, pieces, weight_ref, cot_ref)
    turn_heads([0], heads, early_ref, turned_ref, attended_ref, cot_ref, [state_ref], [out_ref], dout_ref)


def slot_columns(refs, n, per, width):
    return refs[n // per][:, n % per * width : (n % per + 1) * width]


def value_grads_kernel(heads, top_ref, bottom_ref, *rest):
    douts, gv_ref = rest[:GROUP], rest[GROUP]
    half = top_ref.shape[1]
    per = -(-heads // GROUP)
    width = gv_ref.shape[1] // (GROUP * per)

    @slot_heads(SENT, heads)
    def one(n, head):
        weights = top_ref[band(head, half), :], bottom_ref[band(head, half), :]
        gv_ref[:, n * width : (n + 1) * width] = mix_back(weights, slot_columns(douts, n, per, width), half)


def key_grads_kernel(heads, rates_ref, q_ref, v_ref, *rest):
    douts, (gk_ref, top_ref, bottom_ref) = rest[:GROUP], rest[GROUP:]
    rows, width = q_ref.shape[0], q_ref.shape[1] // heads
    half = rows // 2
    per = -(-heads // GROUP)

    @slot_heads(SENT, heads)
    def one(n, head):
        held = slice(n * half, (n + 1) * half)
        rate = head_rate(rates_ref, head)
        upto = query_decay(rate, rows, half)
        dout = slot_columns(douts, n, per, width)
        dweights = decayed_pairs(dout, v_ref[:, band(head, width)], upto, since_decay(rate, rows), half)
        top_ref[held, :], bottom_ref[held, :] = dweights
        gk_ref[:, n * width : (n + 1) * width] = mix_back(dweights, q_ref[:, band(head, width)], half)


def query_grads_kernel(heads, rates_ref, k_ref, top_ref, bottom_ref, *rest):
    douts, states, gq_ref = rest[:GROUP], rest[GROUP : 2 * GROUP], rest[2 * GROUP]
    rows, width = k_ref.shape[0], k_ref.shape[1] // heads
    half = rows // 2
    per = -(-heads // GROUP)

    @slot_heads(SENT, heads)
    def one(n, head):
        held = slice(n * half, (n + 1) * half)
        dout = slot_columns(douts, n, per, width)
        late = (dout.astype(F32) * query_decay(head_rate(rates_ref, head), rows, width)).astype(BF16)
        state = states[n // per][n % per * width : (n % per + 1) * width, :]
        gq = mix((top_ref[held, :], bottom_ref[held, :]), k_ref[:, band(head, width)], half) + dot(late, state, NT)
        gq_ref[:, band(head, width)] = gq.astype(BF16)


def finish_kernel(slots, heads, taken_over, late_keys, late_values, gk_in, gv_in, *rest):
    backs, rest = rest[: len(slots)], rest[len(slots) + taken_over :]
    gk_hbm, gv_hbm, gk_ref, gv_ref, sems = rest
    per = -(-heads // GROUP)
    width = late_keys.shape[1] // heads

    def stores(n, head):
        cols = slice(n * width, (n + 1) * width)
        for side, (source, target) in enumerate(((gk_ref, gk_hbm), (gv_ref, gv_hbm))):
            yield pltpu.make_async_copy(source.at[:, cols], target.at[:, band(head, width)], sems.at[side, n])

    @slot_heads(slots, heads)
    def one(n, head):
        cols = slice(n * width, (n + 1) * width)
        at = (SENT.index(slots[n // per]) * per + n % per) * width
        back = backs[n // per][n % per * width : (n % per + 1) * width, :]
        key_store, value_store = stores(n, head)
        gk = gk_in[:, at : at + width] + dot(late_values[:, band(head, width)], back, NT)
        gk_ref[:, cols] = gk.astype(BF16)
        key_store.start()
        gv = gv_in[:, at : at + width] + dot(late_keys[:, band(head, width)], back, NN)
        gv_ref[:, cols] = gv.astype(BF16)
        value_store.start()

    @slot_heads(slots, heads)
    def two(n, head):
        for store in stores(n, head):
            store.wait()


def swaps(pieces, axis, count):
    return {s: lax.ppermute(pieces[s], axis, [(i, i ^ s) for i in range(count)]) for s in range(1, GROUP)}


def add_up(got, rates, rows, heads, reverse):
    order = list(reversed(range(GROUP))) if reverse else list(range(GROUP))
    kernel = functools.partial(total_kernel, order, rows, heads)
    return call(kernel, [jax.ShapeDtypeStruct(got[0].shape, BF16)], [PLAIN] * (1 + GROUP), limit=4)(
        rates, *[got[s] for s in SENT]
    )[0]


def from_groups(total, rates, rows, heads, axis, count, reverse):
    groups = count // GROUP

    def shift(x, by):
        step = -by if reverse else by
        return lax.ppermute(x, axis, [(i, (i + step * GROUP) % count) for i in range(count)])

    carry = total
    if groups > 1:
        carry = shift(total, 1)
        span = 1
        while span < groups - 1:
            carry = widen(carry, shift(carry, span), rates, rows, heads, groups, span, reverse)
            span *= 2
    return carry


def spread_out(carry, got, rates, rows, heads, count, reverse):
    order = list(reversed(range(GROUP))) if reverse else list(range(GROUP))
    kernel = functools.partial(spread_kernel, order, rows, heads, count // GROUP, reverse)
    piece = jax.ShapeDtypeStruct(carry.shape, BF16)
    return call(kernel, [piece] * GROUP, [PLAIN] * (2 + GROUP), limit=4)(rates, carry, *[got[s] for s in SENT])


def widen_kernel(rows, heads, groups, span, reverse, rates_ref, near_ref, far_ref, out_ref):
    width = out_ref.shape[1]
    group = lax.axis_index("ctx") // GROUP
    reached = group + span + 1 <= groups - 1 if reverse else group >= span + 1
    for me in range(GROUP):

        @pl.when(group_member() == me)
        def _():
            for part, head in owned_parts(me, heads, width):
                decay = jnp.exp(GROUP * rows * span * head_rate(rates_ref, head))
                far = jnp.where(reached, far_ref[part, :].astype(F32), 0.0)
                out_ref[part, :] = (near_ref[part, :].astype(F32) + decay * far).astype(BF16)


def widen(near, far, rates, rows, heads, groups, span, reverse):
    kernel = functools.partial(widen_kernel, rows, heads, groups, span, reverse)
    return call(kernel, [jax.ShapeDtypeStruct(near.shape, BF16)], [PLAIN] * 3, limit=4)(rates, near, far)[0]


def gather_lines(x, axis, count):
    lines = count // 2
    return [lax.ppermute(x, axis, [(i, (i - 2 * s) % count) for i in range(count)]) for s in range(1, lines)]


def flipped(x, axis, count):
    return lax.ppermute(x, axis, [(i, i ^ 1) for i in range(count)])


def after(x, *others):
    return lax.optimization_barrier((x, others))[0]


def body(ctx_count, head_count, query, key_in, value, out_weight, grad_layer, decay_exp):
    rows, flat = query.shape
    heads = decay_exp.shape[0]
    width = flat // heads
    per = -(-heads // GROUP)
    quarter = per * width
    half = rows // 2
    rest = list(SENT[1:])

    def shaped(*shape, dtype=BF16):
        return jax.ShapeDtypeStruct(shape, dtype)

    piece = shaped(quarter, width)
    whole_rows = shaped(rows, flat)
    slot_sums = shaped(rows, GROUP * quarter, dtype=F32)

    moved = gather_lines(grad_layer, "head", head_count)
    made = call(
        functools.partial(local_state_kernel, heads, quarter),
        [piece] * GROUP
        + [shaped(8 * heads, 128, dtype=F32)]
        + [whole_rows] * 4
        + [shaped(*grad_layer.shape)],
        [STREAM] * 5,
        [
            pltpu.VMEM((GROUP * quarter, width), BF16),
            pltpu.VMEM((rows, flat), F32),
            pltpu.SMEM((heads,), jnp.int32),
            pltpu.SemaphoreType.DMA((2, max(n for n in (1, 2, 3, 4) if heads % n == 0))),
            pltpu.SemaphoreType.DMA((3,)),
        ],
        work=3 * 10**9,
    )(decay_exp, query, key_in, value, grad_layer)
    pieces = made[:GROUP]
    rates, query, key_in, value, late_keys, own = made[GROUP:]

    got = {0: pieces[0], **swaps(pieces, "ctx", ctx_count)}
    inner = call(
        functools.partial(within_kernel, heads),
        [shaped(rows, flat, dtype=F32), whole_rows, shaped(flat, rows), whole_rows]
        + [shaped(heads * half, half), shaped(heads * half, rows)],
        [PLAIN] * 4,
        work=3 * 10**9,
    )(rates, query, key_in, value)
    got = dict(zip(SENT, after([got[s] for s in SENT], *inner)))
    attended, early_queries, turned_queries, late_values, top, bottom = inner
    total = add_up(got, rates, rows, heads, False)
    carry = from_groups(total, rates, rows, heads, "ctx", ctx_count, False)
    slots = [own, flipped(after(own, total), "head", head_count)]
    for x in moved:
        x = after(x, carry)
        slots += [x, flipped(x, "head", head_count)]
    ready = spread_out(carry, got, rates, rows, heads, ctx_count, False)
    ready = dict(enumerate(ready))
    ready[1], ready[2] = after((ready[1], ready[2]), slots[1])
    states = {0: ready[0], **swaps(ready, "ctx", ctx_count)}

    slots[-1] = after(slots[-1], ready[0])
    cots = call(
        functools.partial(project_kernel, rest, heads, width),
        [shaped(rows, quarter)] * len(rest),
        [PLAIN] * (head_count + 1),
    )(*slots, out_weight)
    pieces, douts = {}, {}
    for s, cot in zip(rest, cots):
        pieces[s], douts[s] = call(
            functools.partial(turn_kernel, [s], heads), [piece, shaped(rows, quarter)], [PLAIN] * 5
        )(early_queries, turned_queries, attended, cot, states[s])
    got = swaps(pieces, "ctx", ctx_count)
    mine, douts[0] = call(
        functools.partial(turn_own_kernel, heads, width),
        [piece, shaped(rows, quarter)],
        [PLAIN] * (head_count + 5),
        [pltpu.VMEM((rows, quarter), BF16)],
    )(after(early_queries, *[douts[s] for s in rest]), turned_queries, attended, states[0], *slots, out_weight)
    douts = [douts[s] for s in SENT]
    (value_part,) = call(functools.partial(value_grads_kernel, heads), [slot_sums], [PLAIN] * (2 + GROUP))(
        top, bottom, *douts
    )
    got = dict(zip(SENT, after([{0: mine, **got}[s] for s in SENT], value_part)))
    total = add_up(got, rates, rows, heads, True)
    carry = from_groups(total, rates, rows, heads, "ctx", ctx_count, True)
    key_part, top, bottom = call(
        functools.partial(key_grads_kernel, heads),
        [slot_sums, shaped(GROUP * per * half, half), shaped(GROUP * per * half, rows)],
        [PLAIN] * (3 + GROUP),
    )(rates, query, after(value, total), *douts)
    ready = spread_out(after(carry, key_part), got, rates, rows, heads, ctx_count, True)
    back = {0: ready[0], **swaps(ready, "ctx", ctx_count)}
    (grad_query,) = call(functools.partial(query_grads_kernel, heads), [whole_rows], [PLAIN] * (4 + 2 * GROUP))(
        rates, after(key_in, ready[0]), top, bottom, *douts, *[states[s] for s in SENT]
    )
    stages = [0], [1, 3], [2]
    sums = [late_keys, late_values, key_part, value_part]
    grads = []
    for which in stages:
        pieces = after([back[s] for s in which], *(grads or [grad_query]))
        held = pltpu.VMEM((rows, len(which) * quarter), BF16)
        grads = call(
            functools.partial(finish_kernel, which, heads, len(grads)),
            [whole_rows] * 2,
            [PLAIN] * (4 + len(which)) + [STREAM] * len(grads),
            [held, held, pltpu.SemaphoreType.DMA((2, len(which) * per))],
            out_specs=[STREAM] * 2,
            aliases={4 + len(which) + n: n for n in range(len(grads))},
        )(*sums, *pieces, *grads)
    grad_key, grad_value = grads
    return grad_query, grad_key, grad_value


def solution(mesh):
    return jax.shard_map(
        functools.partial(body, mesh.shape["ctx"], mesh.shape["head"]),
        mesh=mesh,
        in_specs=(
            P("ctx", "head"),
            P("ctx", "head"),
            P("ctx", "head"),
            P("head", None),
            P(("ctx", "head"), None),
            P("head"),
        ),
        out_specs=(P("ctx", "head"), P("ctx", "head"), P("ctx", "head")),
        check_vma=False,
    )
```
